32 devices in a mesh: section: 2 (over core), seq: 4 (over z), tensor: 4 (over y, x).
Axes of the slice: x: 2, y: 2, z: 4, core: 2. Of those that a mesh axis runs over, the one named last changes fastest.
Arguments:
- inputs: bfloat16 [3, 1024, 2048], P(None, 'seq'), may hold values from -6 to 6
- cotangent: bfloat16 [3, 1024, 2048], P(None, 'seq'), may hold values from -6 to 6
- query_proj: bfloat16 [2, 2048, 1024], P('section', 'seq', 'tensor'), may hold values from -0.125 to 0.125
- key_proj: bfloat16 [2, 2048, 1024], P('section', 'seq', 'tensor'), may hold values from -0.125 to 0.125
- value_proj: bfloat16 [2, 2048, 2048], P('section', 'seq', 'tensor'), may hold values from -0.125 to 0.125
- outgate_proj: bfloat16 [2, 2048, 2048], P('section', 'seq', 'tensor'), may hold values from -0.125 to 0.125
- output_proj: bfloat16 [2, 2048, 2048], P('section', 'seq', 'tensor'), may hold values from -0.125 to 0.125
- decay_down: bfloat16 [2, 2048, 16], P('section', 'seq'), may hold values from -0.125 to 0.125
- decay_up: bfloat16 [2, 256, 64], P('section', 'seq', 'tensor'), may hold values from -4 to 4
- decay_bias: bfloat16 [2, 256, 4], P('section', 'seq', 'tensor'), may hold values from -1 to 14
- head_gain: bfloat16 [2, 512], P('section', 'seq'), may hold values from 0.099609375 to 1.8984375
- mixer_gain: bfloat16 [2, 2048], P('section', 'seq'), may hold values from 0.099609375 to 1.8984375
- feed_gain: bfloat16 [2, 2048], P('section', 'seq'), may hold values from 0.099609375 to 1.8984375
- feed_gate: bfloat16 [2, 2048, 5632], P('section', 'seq', 'tensor'), may hold values from -0.125 to 0.125
- feed_up: bfloat16 [2, 2048, 5632], P('section', 'seq', 'tensor'), may hold values from -0.125 to 0.125
- feed_down: bfloat16 [2, 2048, 5632], P('section', 'seq', 'tensor'), may hold values from -0.078125 to 0.078125
Outputs:
- layer_outputs: bfloat16 [2, 3, 1024, 2048], P('section', None, 'seq')
- input_grads: float32 [2, 3, 1024, 2048], P('section', None, 'seq')
- query_proj_grad: float32 [2, 2048, 1024], P('section', 'seq', 'tensor')
- key_proj_grad: float32 [2, 2048, 1024], P('section', 'seq', 'tensor')
- value_proj_grad: float32 [2, 2048, 2048], P('section', 'seq', 'tensor')
- outgate_proj_grad: float32 [2, 2048, 2048], P('section', 'seq', 'tensor')
- output_proj_grad: float32 [2, 2048, 2048], P('section', 'seq', 'tensor')
- decay_down_grad: float32 [2, 2048, 16], P('section', 'seq')
- decay_up_grad: float32 [2, 256, 64], P('section', 'seq', 'tensor')
- decay_bias_grad: float32 [2, 256, 4], P('section', 'seq', 'tensor')
- head_gain_grad: float32 [2, 512], P('section', 'seq')
- mixer_gain_grad: float32 [2, 2048], P('section', 'seq')
- feed_gain_grad: float32 [2, 2048], P('section', 'seq')
- feed_gate_grad: float32 [2, 2048, 5632], P('section', 'seq', 'tensor')
- feed_up_grad: float32 [2, 2048, 5632], P('section', 'seq', 'tensor')
- feed_down_grad: float32 [2, 2048, 5632], P('section', 'seq', 'tensor')
The draws below stay inside these ranges and needn't reach their ends.
All inputs are finite; a program needn't handle non-finite values.
Results may differ from the reference program's by a relative error of at most 0.035.
Values may be sent and summed in bfloat16 or wider, within the bound.
A program may use at most 320 MiB of HBM per device.

```python
import jax
import jax.numpy as jnp
from jax import lax

D = 2048
HEADS = 4
KH = 256
VH = 512
FF = 5632
RANK = 16
SPAN = 64
MB = 3
LAYERS = 2
LEN = 1024
KD = 1024
VD = 2048


def draw_decay_bias(key, part):
    key = jax.random.fold_in(key, 7)
    values = jax.random.uniform(key, (LAYERS, KH, HEADS), jnp.float32, -1.0, 14.0)
    return values.astype(jnp.bfloat16)


def shard_levels(rng, extent, shards, low, top_value):
    def one(position, parts):
        steps = jax.random.uniform(jax.random.fold_in(jax.random.fold_in(rng, 6), position), (parts,), jnp.float32, low / len(shards), top_value / len(shards))
        return jnp.repeat(jnp.exp(steps), extent[position] // parts).reshape((-1,) + (1,) * (len(extent) - position - 1))

    loudness = one(*shards[0])
    for cut in shards[1:]:
        loudness = loudness * one(*cut)
    return loudness


def normal_values(key, dims, width, bound, cuts=(), held_as=jnp.bfloat16):
    level = shard_levels(key, dims, cuts, -0.22, 0.18) if cuts else 1.0
    array = jax.random.normal(key, dims, jnp.float32) * width * level
    return jnp.minimum(jnp.maximum(array, -bound), bound).astype(held_as)


def setup_inputs(seed: int = 0) -> dict:
    key_list = jax.random.split(jax.random.key(seed), 17)
    return {
        "inputs": normal_values(key_list[0], (MB, LEN, D), 1.0, 6.0, ((1, 4),)),
        "cotangent": normal_values(key_list[1], (MB, LEN, D), 1.0, 6.0, ((1, 4),)),
        "query_proj": normal_values(key_list[2], (LAYERS, D, KD), D ** -0.5, 0.125, ((0, 2), (1, 4), (2, 4))),
        "key_proj": normal_values(key_list[3], (LAYERS, D, KD), D ** -0.5, 0.125, ((0, 2), (1, 4), (2, 4))),
        "value_proj": normal_values(key_list[4], (LAYERS, D, VD), D ** -0.5, 0.125, ((0, 2), (1, 4), (2, 4))),
        "outgate_proj": normal_values(key_list[5], (LAYERS, D, VD), D ** -0.5, 0.125, ((0, 2), (1, 4), (2, 4))),
        "output_proj": normal_values(key_list[6], (LAYERS, D, VD), VD ** -0.5, 0.125, ((0, 2), (1, 4), (2, 4))),
        "decay_down": normal_values(key_list[7], (LAYERS, D, RANK), D ** -0.5, 0.125, ((0, 2), (1, 4))),
        "decay_up": normal_values(key_list[8], (LAYERS, KH, HEADS * RANK), 1.0, 4.0, ((0, 2), (1, 4), (2, 4))),
        "decay_bias": draw_decay_bias(jax.random.fold_in(key_list[16], 71), 0),
        "head_gain": jnp.clip(1.0 + 0.18 * jax.random.normal(key_list[10], (LAYERS, VH), jnp.float32), 0.099609375, 1.8984375).astype(jnp.bfloat16),
        "mixer_gain": jnp.clip(1.0 + 0.18 * jax.random.normal(key_list[11], (LAYERS, D), jnp.float32), 0.099609375, 1.8984375).astype(jnp.bfloat16),
        "feed_gain": jnp.clip(1.0 + 0.18 * jax.random.normal(key_list[12], (LAYERS, D), jnp.float32), 0.099609375, 1.8984375).astype(jnp.bfloat16),
        "feed_gate": normal_values(key_list[13], (LAYERS, D, FF), D ** -0.5, 0.125, ((0, 2), (1, 4), (2, 4))),
        "feed_up": normal_values(key_list[14], (LAYERS, D, FF), D ** -0.5, 0.125, ((0, 2), (1, 4), (2, 4))),
        "feed_down": normal_values(key_list[15], (LAYERS, D, FF), FF ** -0.5, 0.078125, ((0, 2), (1, 4), (2, 4))),
    }


HIGH = lax.Precision.HIGHEST
MODEL_EPS = 1e-06
HEAD_EPS = 1e-05
GATE_SCALE = 16.0

@jax.custom_vjp
def low(v):
    return lax.optimization_barrier(v.astype(jnp.bfloat16)).astype(jnp.float32)

@jax.custom_vjp
def low_back(v):
    return v

def low_keep(v):
    return (low(v), None)

def low_pass(kept, grad):
    return (grad,)

def back_keep(v):
    return (v, None)

def back_low(kept, grad):
    return (low(grad),)
low.defvjp(low_keep, low_pass)
low_back.defvjp(back_keep, back_low)

def high_dot(left, right):
    return jnp.dot(left, right, precision=HIGH)

def norm_gain(field, gain, eps):
    return gain * field * lax.rsqrt(lax.optimization_barrier(jnp.mean(field * field, axis=-1, keepdims=True)) + eps)

def head_output(inner, out_gate, gain):
    return norm_gain(inner, gain, HEAD_EPS) * jax.nn.silu(out_gate)

def span_scan(queries, keys, values, decay, state):
    length = queries.shape[0]
    count = length // SPAN
    key_dim = queries.shape[1]
    causal = (jnp.arange(SPAN)[:, None] >= jnp.arange(SPAN)[None, :]).astype(queries.dtype)

    def one_block(carry, pieces):
        query_b, key_b, value_b, decay_b = pieces
        cumul = jnp.cumsum(decay_b, axis=0)
        middle_ref = cumul[SPAN // 2]
        scores = jnp.dot(query_b * jnp.exp(cumul - middle_ref), (key_b * jnp.exp(middle_ref - cumul)).T, precision=HIGH) * causal
        local = jnp.dot(scores, value_b, precision=HIGH)
        carried = jnp.dot(query_b * jnp.exp(cumul), carry, precision=HIGH)
        last = cumul[-1]
        moved = jnp.dot((key_b * jnp.exp(last[None, :] - cumul)).T, value_b, precision=HIGH)
        return (jnp.exp(last)[:, None] * carry + moved, local + carried)
    pieces = (queries.reshape(count, SPAN, key_dim), keys.reshape(count, SPAN, key_dim), values.reshape(count, SPAN, values.shape[1]), decay.reshape(count, SPAN, key_dim))
    state_end, outputs = lax.scan(jax.checkpoint(one_block), state, pieces)
    return (outputs.reshape(length, values.shape[1]), state_end)

def layer(hidden, weights):
    query_w, key_w, value_w, outgate_w, output_w, down_w, up_w, bias_w, head_w, mixer_w, feed_w, gate_w, upper_w, lower_w = weights
    length = hidden.shape[0]
    normed = low(norm_gain(hidden, mixer_w, MODEL_EPS))
    queries = low_back(low(high_dot(normed, query_w)))
    keys = low_back(low(high_dot(normed, key_w)))
    values = low_back(low(high_dot(normed, value_w)))
    out_gate = low_back(high_dot(normed, outgate_w))
    rank_part = high_dot(normed, down_w)
    logits = jnp.einsum('lr,chr->lhc', rank_part, up_w.reshape(KH, HEADS, RANK), precision=HIGH) + bias_w.T[None]
    decay = jax.nn.log_sigmoid(logits) / GATE_SCALE
    query_heads = (queries * KH ** (-0.5)).reshape(length, HEADS, KH).transpose(1, 0, 2)
    key_heads = keys.reshape(length, HEADS, KH).transpose(1, 0, 2)
    value_heads = values.reshape(length, HEADS, VH).transpose(1, 0, 2)
    decay_heads = decay.transpose(1, 0, 2)
    start = jnp.zeros((HEADS, KH, VH), jnp.float32)
    inner, finals = jax.vmap(span_scan)(query_heads, key_heads, value_heads, decay_heads, start)
    inner = inner.transpose(1, 0, 2)
    gated = low(head_output(inner, out_gate.reshape(length, HEADS, VH), head_w).reshape(length, HEADS * VH))
    mixed = low_back(high_dot(gated, output_w.T))
    middle = hidden + mixed
    feed_in = low(norm_gain(middle, feed_w, MODEL_EPS))
    gate_v = low_back(high_dot(feed_in, gate_w))
    upper_v = low_back(high_dot(feed_in, upper_w))
    hidden_ff = low(jax.nn.silu(gate_v) * upper_v)
    return middle + low_back(high_dot(hidden_ff, lower_w.T))

def reference(inputs, cotangent, query_proj, key_proj, value_proj, outgate_proj, output_proj, decay_down, decay_up, decay_bias, head_gain, mixer_gain, feed_gain, feed_gate, feed_up, feed_down):
    weights = tuple((w.astype(jnp.float32) for w in (query_proj, key_proj, value_proj, outgate_proj, output_proj, decay_down, decay_up, decay_bias, head_gain, mixer_gain, feed_gain, feed_gate, feed_up, feed_down)))

    def model(batch_in, probe, params):
        first = layer(batch_in, tuple((p[0] for p in params)))
        middle_in = low_back(low(first)) + probe
        second = layer(middle_in, tuple((p[1] for p in params)))
        return (second, low(first))

    def per_batch(totals, pair):
        batch_in, batch_cot = pair
        start = batch_in.astype(jnp.float32)
        second, pull, first = jax.vjp(model, start, jnp.zeros_like(start), weights, has_aux=True)
        grad_in, grad_mid, grad_w = pull(batch_cot.astype(jnp.float32))
        totals = jax.tree.map(lambda a, b: a + b, totals, grad_w)
        return (totals, (first.astype(jnp.bfloat16), second.astype(jnp.bfloat16), grad_in, grad_mid))
    zeros = jax.tree.map(jnp.zeros_like, weights)
    totals, outs = lax.scan(per_batch, zeros, (inputs, cotangent))
    firsts, seconds, grads_in, grads_mid = outs
    layer_outputs = jnp.stack([firsts, seconds])
    input_grads = jnp.stack([grads_in, grads_mid])
    return (layer_outputs, input_grads, totals[0], totals[1], totals[2], totals[3], totals[4], totals[5], totals[6], totals[7], totals[8], totals[9], totals[10], totals[11], totals[12], totals[13])
```

```python
from functools import partial

import jax
import jax.numpy as jnp
from jax import lax
from jax.experimental import pallas as pl
from jax.experimental.pallas import tpu as pltpu
from jax.sharding import Mesh
from jax.sharding import PartitionSpec as P

SPAN = 64
FINE = 8

HIGH = lax.Precision.HIGHEST
MODEL_EPS = 1e-06
HEAD_EPS = 1e-05
GATE_SCALE = 16.0

f32 = jnp.float32
bf16 = jnp.bfloat16
GROUP = ("section", "q")


def dot_plain(left, right):
    return jnp.dot(left, right, preferred_element_type=f32)


def dot_left(left, right):
    return lax.dot_general(left, right, (((0,), (0,)), ((), ())), preferred_element_type=f32)


def dot_right(left, right):
    return lax.dot_general(left, right, (((1,), (1,)), ((), ())), preferred_element_type=f32)


def normed_rows(u, gain):
    return gain * u * lax.rsqrt(jnp.mean(u * u, axis=-1, keepdims=True) + MODEL_EPS)


def norm_back(d, u, gain):
    s = lax.rsqrt(jnp.mean(u * u, axis=-1, keepdims=True) + MODEL_EPS)
    w = gain * d
    d_u = s * w - u * (s * s * s) * jnp.mean(w * u, axis=-1, keepdims=True)
    return d_u, jnp.sum(d * u * s, axis=0, keepdims=True)


class Peers:
    def __init__(self, peers):
        self.peers = peers
        self.me = lax.axis_index("tensor")

    def at(self, d):
        return lax.rem(self.me + d, self.peers)

    def enter(self, relay_to):
        barrier = pltpu.get_barrier_semaphore()
        for d in range(1, self.peers):
            pl.semaphore_signal(barrier, inc=1, device_id={"tensor": self.at(d)})
        if relay_to is None:
            pl.semaphore_wait(barrier, self.peers - 1)
            return
        stage = lax.axis_index("stage")

        @pl.when(stage == relay_to)
        def _():
            pl.semaphore_signal(barrier, inc=1, device_id={"stage": 1 - relay_to})
            pl.semaphore_wait(barrier, self.peers - 1)

        @pl.when(stage != relay_to)
        def _():
            pl.semaphore_wait(barrier, self.peers)


def reduce_rows(peers, part, send, land, sems, total, fine=None, fine_sems=None):
    copies = []
    for d in range(1, peers.peers):
        peer = peers.at(d)
        send[d - 1] = part[peer].astype(bf16)
        copy = pltpu.make_async_remote_copy(
            src_ref=send.at[d - 1],
            dst_ref=land.at[d - 1],
            send_sem=sems.at[0, d - 1],
            recv_sem=sems.at[1, d - 1],
            device_id={"tensor": peer},
        )
        copy.start()
        copies.append(copy)
    if fine is not None:
        for d in range(1, peers.peers):

            @pl.when(peers.at(d) == 0)
            def _():
                fine_copy(part, fine, fine_sems, d).start()

    acc = part[peers.me].astype(f32)
    for d in range(1, peers.peers):
        copies[d - 1].wait()
        acc = acc + land[d - 1].astype(f32)
    total[...] = acc
    if fine is not None:
        for d in range(1, peers.peers):

            @pl.when(peers.at(d) == 0)
            def _():
                fine_copy(part, fine, fine_sems, d).wait_send()

        @pl.when(peers.me == 0)
        def _():
            top = part[0, 0:FINE, :]
            for d in range(1, peers.peers):
                fine_copy(part, fine, fine_sems, d).wait_recv()
                top = top + fine[d - 1]
            total[0:FINE, :] = top


def fine_copy(part, fine, fine_sems, d):
    return pltpu.make_async_remote_copy(
        src_ref=part.at[0, pl.ds(0, FINE), :],
        dst_ref=fine.at[d - 1],
        send_sem=fine_sems.at[0, d - 1],
        recv_sem=fine_sems.at[1, d - 1],
        device_id={"tensor": 0},
    )


def share_rows(peers, full, sems):
    copies = []
    for d in range(1, peers.peers):
        copy = pltpu.make_async_remote_copy(
            src_ref=full.at[peers.me],
            dst_ref=full.at[peers.me],
            send_sem=sems.at[0, d - 1],
            recv_sem=sems.at[1, d - 1],
            device_id={"tensor": peers.at(d)},
        )
        copy.start()
        copies.append(copy)
    for copy in copies:
        copy.wait()


def relay_rows(src, land, sems, relay_to):
    return pltpu.make_async_remote_copy(
        src_ref=src,
        dst_ref=land,
        send_sem=sems.at[0],
        recv_sem=sems.at[1],
        device_id={"stage": relay_to},
    )


def first_kernel(peers_n, norm, h, gain, full, share_sems):
    peers = Peers(peers_n)
    peers.enter(None)
    if norm:
        full[peers.me] = normed_rows(h[...].astype(f32), gain[...]).astype(bf16)
    else:
        full[peers.me] = h[...]
    share_rows(peers, full, share_sems)


def forward_mid_kernel(
    peers_n, part, h, gain, middle, full, send, land, fine, total, sems, fine_sems, share_sems
):
    peers = Peers(peers_n)
    peers.enter(None)
    reduce_rows(peers, part, send, land, sems, total, fine, fine_sems)
    value = h[...].astype(f32) + total[...]
    middle[...] = value
    full[peers.me] = normed_rows(value, gain[...]).astype(bf16)
    share_rows(peers, full, share_sems)


def forward_end_kernel(
    peers_n,
    part,
    middle,
    gain,
    own,
    y,
    h,
    full,
    send,
    land,
    fine,
    total,
    relayed,
    sems,
    fine_sems,
    share_sems,
    relay_sems,
):
    peers = Peers(peers_n)
    stage = lax.axis_index("stage")
    peers.enter(1)
    reduce_rows(peers, part, send, land, sems, total, fine, fine_sems)
    y[...] = (middle[...] + total[...]).astype(bf16)
    relay = relay_rows(y, relayed, relay_sems, 1)

    @pl.when(stage == 0)
    def _():
        relay.start()
        h[...] = own[...]

    @pl.when(stage == 1)
    def _():
        relay.wait_recv()
        h[...] = relayed[...]

    full[peers.me] = normed_rows(h[...].astype(f32), gain[...]).astype(bf16)
    share_rows(peers, full, share_sems)

    @pl.when(stage == 0)
    def _():
        relay.wait_send()


def forward_last_kernel(
    peers_n, part, middle, y, send, land, fine, total, sems, fine_sems
):
    peers = Peers(peers_n)
    peers.enter(None)
    reduce_rows(peers, part, send, land, sems, total, fine, fine_sems)
    y[...] = (middle[...] + total[...]).astype(bf16)


def backward_mid_kernel(
    peers_n, part, gy, middle, gain, d_middle, gain_part, full, send, land, total, sems, share_sems
):
    peers = Peers(peers_n)
    peers.enter(None)
    reduce_rows(peers, part, send, land, sems, total)
    d_u, g = norm_back(total[...], middle[...], gain[...])
    value = gy[...].astype(f32) + d_u
    d_middle[...] = value
    gain_part[...] = g
    full[peers.me] = value.astype(bf16)
    share_rows(peers, full, share_sems)


def backward_end_kernel(
    peers_n,
    part,
    d_middle,
    h,
    gain,
    own,
    grad,
    gain_part,
    gy,
    full,
    send,
    land,
    total,
    relayed,
    sems,
    share_sems,
    relay_sems,
):
    peers = Peers(peers_n)
    stage = lax.axis_index("stage")
    peers.enter(0)
    reduce_rows(peers, part, send, land, sems, total)
    d_u, g = norm_back(total[...], h[...].astype(f32), gain[...])
    value = d_middle[...] + d_u
    grad[...] = value.astype(bf16)
    gain_part[...] = g
    relay = relay_rows(grad, relayed, relay_sems, 0)

    @pl.when(stage == 1)
    def _():
        relay.start()
        gy[...] = own[...]

    @pl.when(stage == 0)
    def _():
        relay.wait_recv()
        gy[...] = relayed[...]

    full[peers.me] = gy[...]
    share_rows(peers, full, share_sems)

    @pl.when(stage == 1)
    def _():
        relay.wait_send()


def backward_last_kernel(
    peers_n, part, d_middle, h, gain, grad, gain_part, send, land, total, sems
):
    peers = Peers(peers_n)
    peers.enter(None)
    reduce_rows(peers, part, send, land, sems, total)
    d_u, g = norm_back(total[...], h[...].astype(f32), gain[...])
    grad[...] = (d_middle[...] + d_u).astype(bf16)
    gain_part[...] = g


def in_vmem(count):
    return [pl.BlockSpec(memory_space=pltpu.VMEM)] * count


def kernel_call(body, outs, scratch, ident, *args):
    single = not isinstance(outs, list)
    return pl.pallas_call(
        body,
        out_shape=outs,
        in_specs=in_vmem(len(args)),
        out_specs=in_vmem(1)[0] if single else in_vmem(len(outs)),
        scratch_shapes=scratch,
        compiler_params=pltpu.CompilerParams(
            collective_id=ident, has_side_effects=True, vmem_limit_bytes=40 * 1024 * 1024
        ),
    )(*args)


def shape(dims, kind):
    return jax.ShapeDtypeStruct(dims, kind)


class Rows:
    def __init__(self, rows, width, peers):
        self.rows, self.width, self.peers = rows, width, peers
        self.slice_b = shape((rows, width), bf16)
        self.slice_f = shape((rows, width), f32)
        self.gain_f = shape((1, width), f32)
        self.full = shape((peers, rows, width), bf16)
        self.pair = pltpu.SemaphoreType.DMA((2, peers - 1))
        self.reduce = [
            pltpu.VMEM((peers - 1, rows, width), bf16),
            pltpu.VMEM((peers - 1, rows, width), bf16),
        ]
        self.fine = [pltpu.VMEM((peers - 1, FINE, width), f32)]
        self.total = [pltpu.VMEM((rows, width), f32)]
        self.relayed = [pltpu.VMEM((rows, width), bf16)]
        self.relay = pltpu.SemaphoreType.DMA((2,))

    def parts(self, part):
        return part.reshape(self.peers, self.rows, self.width)

    def flat(self, full):
        return full.reshape(self.peers * self.rows, self.width)

    def first(self, h, gain, norm, ident):
        body = partial(first_kernel, self.peers, norm)
        return self.flat(kernel_call(body, self.full, [self.pair], ident, h, gain))

    def forward_mid(self, part, h, gain):
        middle, full = kernel_call(
            partial(forward_mid_kernel, self.peers),
            [self.slice_f, self.full],
            self.reduce + self.fine + self.total + [self.pair] * 3,
            3,
            self.parts(part),
            h,
            gain,
        )
        return middle, self.flat(full)

    def forward_end(self, part, middle, gain, own):
        y, h, full = kernel_call(
            partial(forward_end_kernel, self.peers),
            [self.slice_b, self.slice_b, self.full],
            self.reduce + self.fine + self.total + self.relayed + [self.pair] * 3 + [self.relay],
            4,
            self.parts(part),
            middle,
            gain,
            own,
        )
        return y, h, self.flat(full)

    def forward_last(self, part, middle):
        return kernel_call(
            partial(forward_last_kernel, self.peers),
            self.slice_b,
            self.reduce + self.fine + self.total + [self.pair] * 2,
            5,
            self.parts(part),
            middle,
        )

    def backward_mid(self, part, gy, middle, gain):
        d_middle, gain_part, full = kernel_call(
            partial(backward_mid_kernel, self.peers),
            [self.slice_f, self.gain_f, self.full],
            self.reduce + self.total + [self.pair] * 2,
            6,
            self.parts(part),
            gy,
            middle,
            gain,
        )
        return d_middle, gain_part, self.flat(full)

    def backward_end(self, part, d_middle, h, gain, own):
        grad, gain_part, gy, full = kernel_call(
            partial(backward_end_kernel, self.peers),
            [self.slice_b, self.gain_f, self.slice_b, self.full],
            self.reduce + self.total + self.relayed + [self.pair] * 2 + [self.relay],
            7,
            self.parts(part),
            d_middle,
            h,
            gain,
            own,
        )
        return grad, gain_part, gy, self.flat(full)

    def backward_last(self, part, d_middle, h, gain):
        return kernel_call(
            partial(backward_last_kernel, self.peers),
            [self.slice_b, self.gain_f],
            self.reduce + self.total + [self.pair],
            8,
            self.parts(part),
            d_middle,
            h,
            gain,
        )


PAD = 16


class Chain:
    def __init__(self, ranges, half):
        self.ranges, self.half = ranges, half
        self.me = lax.axis_index("section") * half + lax.axis_index("q")

    def place(self, d):
        other = lax.rem(self.me + d, self.ranges)
        return {"section": other // self.half, "q": lax.rem(other, self.half)}

    def enter(self):
        barrier = pltpu.get_barrier_semaphore()
        for d in range(1, self.ranges):
            pl.semaphore_signal(barrier, inc=1, device_id=self.place(d))
        pl.semaphore_wait(barrier, self.ranges - 1)

    def copy(self, land, sems, d):
        return pltpu.make_async_remote_copy(
            src_ref=land.at[self.me],
            dst_ref=land.at[self.me],
            send_sem=sems.at[0, d - 1],
            recv_sem=sems.at[1, d - 1],
            device_id=self.place(d),
        )

    def start(self, land, sems, state, through):
        high = state.shape[0]
        land[self.me, 0:high, :] = state.astype(bf16)
        land[self.me, high : high + PAD, :] = jnp.broadcast_to(
            through, (PAD, through.shape[1])
        ).astype(bf16)
        for d in range(1, self.ranges):
            self.copy(land, sems, d).start()

    def finish(self, land, sems, high, later):
        for d in range(1, self.ranges):
            self.copy(land, sems, d).wait()

        def step(n, state):
            place = self.ranges - 1 - n if later else n
            taken = (place > self.me) if later else (place < self.me)
            through = land[place, high : high + PAD, :].astype(f32)[0:1, :]
            joined = through * state + land[place, 0:high, :].astype(f32)
            return jnp.where(taken, joined, state)

        zero = jnp.zeros((high, land.shape[2]), f32)
        state = zero
        for n in range(self.ranges):
            state = step(n, state)
        return state


def triangle(size):
    row = lax.broadcasted_iota(jnp.int32, (size, size), 0)
    col = lax.broadcasted_iota(jnp.int32, (size, size), 1)
    return row, col


def scores_of(q, k, c):
    row, col = triangle(SPAN)
    middle = c[SPAN // 2 : SPAN // 2 + 1, :]
    up, down = jnp.exp(c - middle), jnp.exp(middle - c)
    a, b = (q * up).astype(bf16), (k * down).astype(bf16)
    own = jnp.sum(q * k, axis=1, keepdims=True)
    scores = jnp.where(row == col, own, jnp.where(row > col, dot_right(a, b), 0.0))
    return scores, a, b, up, down


def mixer_forward_kernel(
    ranges, half, q_ref, k_ref, v_ref, og_ref, g_ref, hg_ref, inner_ref, gated_ref, c_ref, s_ref,
    moved, out, land, sems,
):
    chain = Chain(ranges, half)
    chain.enter()
    length, key_dim = q_ref.shape
    value_dim = v_ref.shape[1]
    spans = length // SPAN
    scale = key_dim ** (-0.5)
    row, col = triangle(SPAN)
    lower = (row >= col).astype(f32)
    state = jnp.zeros((value_dim, key_dim), f32)
    reach = jnp.zeros((1, key_dim), f32)
    for i in range(spans):
        rows = slice(i * SPAN, (i + 1) * SPAN)
        c = jnp.dot(lower, g_ref[rows, :], precision=HIGH, preferred_element_type=f32)
        c_ref[rows, :] = c
        last = c[SPAN - 1 : SPAN, :]
        fading = (k_ref[rows, :].astype(f32) * jnp.exp(last - c)).astype(bf16)
        step = dot_left(v_ref[rows, :], fading)
        moved[i] = step
        state = jnp.exp(last) * state + step
        reach = reach + last
    chain.start(land, sems, state, jnp.exp(reach))
    for i in range(spans):
        rows = slice(i * SPAN, (i + 1) * SPAN)
        q = q_ref[rows, :].astype(f32) * scale
        k = k_ref[rows, :].astype(f32)
        scores = scores_of(q, k, c_ref[rows, :])[0]
        out[rows, :] = dot_plain(scores.astype(bf16), v_ref[rows, :])
    state = chain.finish(land, sems, value_dim, False)
    for i in range(spans):
        rows = slice(i * SPAN, (i + 1) * SPAN)
        c = c_ref[rows, :]
        held = state.astype(bf16)
        s_ref[i] = held
        q = (q_ref[rows, :].astype(f32) * scale * jnp.exp(c)).astype(bf16)
        inner = out[rows, :] + dot_right(q, held)
        inner_ref[rows, :] = inner
        r = lax.rsqrt(jnp.mean(inner * inner, axis=-1, keepdims=True) + HEAD_EPS)
        og = og_ref[rows, :]
        gated = hg_ref[...] * inner * r * (og / (1.0 + jnp.exp(-og)))
        gated_ref[rows, :] = gated.astype(bf16)
        state = jnp.exp(c[SPAN - 1 : SPAN, :]) * state + moved[i]
    s_ref[spans] = state.astype(bf16)


def mixer_backward_kernel(
    ranges, half, dgated_ref, inner_ref, og_ref, hg_ref, q_ref, k_ref, v_ref, c_ref, s_ref,
    dq_ref, dk_ref, dv_ref, dog_ref, dg_ref, hgp_ref, pulled, o_ref, dqs, dks, dvs, land, sems,
):
    chain = Chain(ranges, half)
    chain.enter()
    length, key_dim = q_ref.shape
    value_dim = v_ref.shape[1]
    spans = length // SPAN
    scale = key_dim ** (-0.5)
    row, col = triangle(SPAN)
    upper = (row <= col).astype(f32)
    state = jnp.zeros((value_dim, key_dim), f32)
    reach = jnp.zeros((1, key_dim), f32)
    hg = hg_ref[...]
    head_part = jnp.zeros((1, value_dim), f32)
    for i in reversed(range(spans)):
        rows = slice(i * SPAN, (i + 1) * SPAN)
        inner, og, dgated = inner_ref[rows, :], og_ref[rows, :], dgated_ref[rows, :]
        r = lax.rsqrt(jnp.mean(inner * inner, axis=-1, keepdims=True) + HEAD_EPS)
        sg = 1.0 / (1.0 + jnp.exp(-og))
        d_norm = dgated * (og * sg)
        unit = inner * r
        head_part = head_part + jnp.sum(d_norm * unit, axis=0, keepdims=True)
        w = d_norm * hg
        d_inner = r * w - inner * (r * r * r) * jnp.mean(w * inner, axis=-1, keepdims=True)
        dog = dgated * unit * hg * (sg * (1.0 + og * (1.0 - sg)))
        dog_ref[rows, :] = dog.astype(bf16)
        o = d_inner.astype(bf16)
        o_ref[rows, :] = o
        c = c_ref[rows, :]
        q = (q_ref[rows, :].astype(f32) * scale * jnp.exp(c)).astype(bf16)
        step = dot_left(o, q)
        pulled[i] = step
        last = c[SPAN - 1 : SPAN, :]
        state = jnp.exp(last) * state + step
        reach = reach + last
    hgp_ref[...] = head_part
    chain.start(land, sems, state, jnp.exp(reach))
    for i in range(spans):
        rows = slice(i * SPAN, (i + 1) * SPAN)
        q = q_ref[rows, :].astype(f32) * scale
        k = k_ref[rows, :].astype(f32)
        scores, a, b, up, down = scores_of(q, k, c_ref[rows, :])
        o, v = o_ref[rows, :], v_ref[rows, :]
        d_scores = jnp.where(row >= col, dot_right(o, v), 0.0).astype(bf16)
        dvs[rows, :] = dot_left(scores.astype(bf16), o)
        dqs[rows, :] = up * dot_plain(d_scores, b) + jnp.exp(c_ref[rows, :]) * dot_plain(o, s_ref[i])
        dks[rows, :] = down * dot_left(d_scores, a)
    state = chain.finish(land, sems, value_dim, True)
    for i in reversed(range(spans)):
        rows = slice(i * SPAN, (i + 1) * SPAN)
        c = c_ref[rows, :]
        last = c[SPAN - 1 : SPAN, :]
        fade = jnp.exp(last - c)
        held = state.astype(bf16)
        k = k_ref[rows, :].astype(f32)
        dk = dks[rows, :] + fade * dot_plain(v_ref[rows, :], held)
        dv = dvs[rows, :] + dot_right((k * fade).astype(bf16), held)
        dq = dqs[rows, :]
        dq_ref[rows, :] = (dq * scale).astype(bf16)
        dk_ref[rows, :] = dk.astype(bf16)
        dv_ref[rows, :] = dv.astype(bf16)
        ended = jnp.sum(state * s_ref[i + 1].astype(f32), axis=0, keepdims=True)
        terms = q_ref[rows, :].astype(f32) * scale * dq - k * dk
        dg_ref[rows, :] = jnp.dot(upper, terms, precision=HIGH, preferred_element_type=f32) + ended
        state = jnp.exp(last) * state + pulled[i]


def mixer_forward(ranges, half, q, k, v, og, g, hg):
    length, key_dim = q.shape
    value_dim = v.shape[1]
    spans = length // SPAN
    return kernel_call(
        partial(mixer_forward_kernel, ranges, half),
        [
            shape((length, value_dim), f32),
            shape((length, value_dim), bf16),
            shape((length, key_dim), f32),
            shape((spans + 1, value_dim, key_dim), bf16),
        ],
        [
            pltpu.VMEM((spans, value_dim, key_dim), f32),
            pltpu.VMEM((length, value_dim), f32),
            pltpu.VMEM((ranges, value_dim + PAD, key_dim), bf16),
            pltpu.SemaphoreType.DMA((2, ranges - 1)),
        ],
        9,
        q, k, v, og, g, hg,
    )


def mixer_backward(ranges, half, dgated, inner, og, hg, q, k, v, c, s):
    length, key_dim = q.shape
    value_dim = v.shape[1]
    spans = length // SPAN
    return kernel_call(
        partial(mixer_backward_kernel, ranges, half),
        [
            shape((length, key_dim), bf16),
            shape((length, key_dim), bf16),
            shape((length, value_dim), bf16),
            shape((length, value_dim), bf16),
            shape((length, key_dim), f32),
            shape((1, value_dim), f32),
        ],
        [
            pltpu.VMEM((spans, value_dim, key_dim), f32),
            pltpu.VMEM((length, value_dim), bf16),
            pltpu.VMEM((length, key_dim), f32),
            pltpu.VMEM((length, key_dim), f32),
            pltpu.VMEM((length, value_dim), f32),
            pltpu.VMEM((ranges, value_dim + PAD, key_dim), bf16),
            pltpu.SemaphoreType.DMA((2, ranges - 1)),
        ],
        10,
        dgated, inner, og, hg, q, k, v, c, s,
    )


def swapped(array):
    return lax.ppermute(array, ("section", "stage"), [(0, 0), (1, 2), (2, 1), (3, 3)])


def work_weights(weights):
    return [lax.all_gather(swapped(w), GROUP, axis=0, tiled=True) for w in weights]


def shards(
    inputs,
    cotangent,
    query_proj,
    key_proj,
    value_proj,
    outgate_proj,
    output_proj,
    decay_down,
    decay_up,
    decay_bias,
    head_gain,
    mixer_gain,
    feed_gain,
    feed_gate,
    feed_up,
    feed_down,
):
    micro, length, width = inputs.shape
    peers = lax.axis_size("tensor")
    half = lax.axis_size("q")
    ranges = 2 * half
    stage = lax.axis_index("stage")
    me = lax.axis_index("tensor")
    rows = length // peers
    calls = Rows(rows, width, peers)

    def own_rows(array):
        return swapped(lax.dynamic_slice_in_dim(array, me * rows, rows, 1))

    own_in = own_rows(inputs)
    small = [decay_up[0], decay_bias[0], head_gain[0], mixer_gain[0], feed_gain[0], decay_down[0]]
    sizes = [a.size for a in small]
    packed = lax.all_gather(
        swapped(jnp.concatenate([a.reshape(-1) for a in small])), GROUP, axis=0
    )
    cuts = [sum(sizes[:n]) for n in range(len(sizes) + 1)]
    pieces = [packed[:, cuts[n] : cuts[n + 1]] for n in range(len(sizes))]
    up_w = pieces[0].reshape(-1, decay_up.shape[2]).astype(f32)
    bias_w = pieces[1].reshape(1, -1).astype(f32)
    head_w = pieces[2].reshape(1, -1).astype(f32)
    mixer_w = pieces[3].reshape(1, -1).astype(f32)
    feed_w = pieces[4].reshape(1, -1).astype(f32)
    down_w = pieces[5].reshape(-1, decay_down.shape[2])
    query_w, key_w, value_w, outgate_w, output_w, gate_w, upper_w, lower_w = work_weights(
        [
            query_proj[0],
            key_proj[0],
            value_proj[0],
            outgate_proj[0],
            output_proj[0],
            feed_gate[0],
            feed_up[0],
            feed_down[0],
        ]
    )
    own_cot = own_rows(cotangent)

    kept, ys = [], []
    h = jnp.where(stage == 0, own_in[0], jnp.zeros_like(own_in[0]))
    normed = calls.first(h, mixer_w, True, 1)
    for step in range(micro + 1):
        q = dot_plain(normed, query_w).astype(bf16)
        k = dot_plain(normed, key_w).astype(bf16)
        v = dot_plain(normed, value_w).astype(bf16)
        out_gate = dot_plain(normed, outgate_w)
        rank_part = dot_plain(normed, down_w)
        logits = jnp.dot(rank_part, up_w.T, precision=HIGH) + bias_w
        decay = jax.nn.log_sigmoid(logits) / GATE_SCALE
        inner, gated, cumul, states = mixer_forward(
            ranges, half, q, k, v, out_gate, decay, head_w
        )
        middle, feed_in = calls.forward_mid(dot_right(gated, output_w), h, feed_w)
        gate_v = dot_plain(feed_in, gate_w)
        upper_v = dot_plain(feed_in, upper_w)
        hidden_ff = (jax.nn.silu(gate_v) * upper_v).astype(bf16)
        kept.append(
            dict(
                h=h, normed=normed, q=q, k=k, v=v, out_gate=out_gate, rank_part=rank_part,
                logits=logits, inner=inner, gated=gated, cumul=cumul, states=states,
                middle=middle, feed_in=feed_in, gate_v=gate_v, upper_v=upper_v,
                hidden_ff=hidden_ff,
            )
        )
        part = dot_right(hidden_ff, lower_w)
        if step < micro:
            y, h, normed = calls.forward_end(
                part, middle, mixer_w, own_in[min(step + 1, micro - 1)]
            )
        else:
            y = calls.forward_last(part, middle)
        ys.append(y)

    grads, saved = [], []
    gy = jnp.where(stage == 1, own_cot[micro - 1], jnp.zeros_like(own_cot[0]))
    d_feed = calls.first(gy, mixer_w, False, 2)
    for step in range(micro + 1):
        now = kept[micro - step]
        d_hidden = dot_plain(d_feed, lower_w)
        sig = jax.nn.sigmoid(now["gate_v"])
        d_gate = (
            d_hidden * now["upper_v"] * (sig * (1.0 + now["gate_v"] * (1.0 - sig)))
        ).astype(bf16)
        d_upper = (d_hidden * (now["gate_v"] * sig)).astype(bf16)
        part = dot_right(d_gate, gate_w) + dot_right(d_upper, upper_w)
        d_middle, feed_part, d_mixed = calls.backward_mid(part, gy, now["middle"], feed_w)
        d_gated = dot_plain(d_mixed, output_w)
        d_q, d_k, d_v, d_outgate, d_decay, head_part = mixer_backward(
            ranges, half, d_gated, now["inner"], now["out_gate"], head_w,
            now["q"], now["k"], now["v"], now["cumul"], now["states"],
        )
        d_logits = d_decay * jax.nn.sigmoid(-now["logits"]) / GATE_SCALE
        d_rank = jnp.dot(d_logits, up_w, precision=HIGH)
        part = (
            dot_right(d_q, query_w)
            + dot_right(d_k, key_w)
            + dot_right(d_v, value_w)
            + dot_right(d_outgate, outgate_w)
            + dot_right(d_rank.astype(bf16), down_w)
        )
        saved.append(
            dict(
                d_feed=d_feed, d_gate=d_gate, d_upper=d_upper, d_mixed=d_mixed, d_q=d_q, d_k=d_k,
                d_v=d_v, d_outgate=d_outgate, d_logits=d_logits, d_rank=d_rank,
            )
        )
        if step < micro:
            later = micro - 2 - step
            own = own_cot[later] if later >= 0 else jnp.zeros_like(own_cot[0])
            grad, mixer_part, gy, d_feed = calls.backward_end(part, d_middle, now["h"], mixer_w, own)
        else:
            grad, mixer_part = calls.backward_last(part, d_middle, now["h"], mixer_w)
        grads.append(grad)
        saved[-1].update(head=head_part, mixer=mixer_part, feed=feed_part)

    def rows_of(name):
        if name in kept[0]:
            return jnp.concatenate([item[name] for item in kept])
        return jnp.concatenate([item[name] for item in reversed(saved)])

    def home(whole):
        return swapped(
            lax.psum_scatter(whole.astype(bf16), GROUP, scatter_dimension=0, tiled=True)
        )[None].astype(f32)

    normed, feed_in, d_feed = rows_of("normed"), rows_of("feed_in"), rows_of("d_feed")
    gate_grad = home(dot_left(feed_in, rows_of("d_gate")))
    upper_grad = home(dot_left(feed_in, rows_of("d_upper")))
    lower_grad = home(dot_left(d_feed, rows_of("hidden_ff")))
    output_grad = home(dot_left(rows_of("d_mixed"), rows_of("gated")))
    query_grad = home(dot_left(normed, rows_of("d_q")))
    key_grad = home(dot_left(normed, rows_of("d_k")))
    value_grad = home(dot_left(normed, rows_of("d_v")))
    outgate_grad = home(dot_left(normed, rows_of("d_outgate")))

    d_logits = rows_of("d_logits")
    small_grads = [
        jnp.dot(d_logits.T, rows_of("rank_part"), precision=HIGH),
        jnp.sum(d_logits, axis=0),
        sum(item["head"] for item in saved),
        sum(item["mixer"] for item in saved),
        sum(item["feed"] for item in saved),
        dot_left(normed, rows_of("d_rank").astype(bf16)),
    ]
    small_sum = swapped(
        lax.psum_scatter(
            jnp.concatenate([g.reshape(ranges, -1) for g in small_grads], axis=1),
            GROUP,
            scatter_dimension=0,
            tiled=True,
        )
    )[0]
    shared = lax.psum(small_sum[cuts[2] :], "tensor")

    def piece(n, like):
        source = small_sum if n < 2 else shared
        begin = cuts[n] if n < 2 else cuts[n] - cuts[2]
        return source[begin : begin + sizes[n]].reshape(like.shape)

    def placed(early, late):
        mine = swapped(jnp.where(stage == 0, jnp.stack(early), jnp.stack(late)))
        return lax.all_gather(mine, "tensor", axis=1, tiled=True)[None]

    layer_outputs = placed(ys[:micro], ys[1:])
    input_grads = placed(grads[:0:-1], grads[micro - 1 :: -1]).astype(f32)
    return (
        layer_outputs,
        input_grads,
        query_grad,
        key_grad,
        value_grad,
        outgate_grad,
        output_grad,
        piece(5, decay_down),
        piece(0, decay_up),
        piece(1, decay_bias),
        piece(2, head_gain),
        piece(3, mixer_gain),
        piece(4, feed_gain),
        gate_grad,
        upper_grad,
        lower_grad,
    )


def solution(mesh):
    sections, ranges, peers = (mesh.shape[a] for a in ("section", "seq", "tensor"))
    staged = Mesh(
        mesh.devices.reshape(sections, 2, ranges // 2, peers), ("section", "stage", "q", "tensor")
    )
    seq = ("stage", "q")
    whole = P("section", seq, "tensor")
    row = P("section", seq)
    rows = P("section", None, seq, None)
    tokens = P(None, seq, None)
    narrow = P("section", seq, None)
    return jax.shard_map(
        shards,
        mesh=staged,
        in_specs=(tokens, tokens)
        + (whole,) * 5
        + (narrow, whole, whole, row, row, row)
        + (whole,) * 3,
        out_specs=(rows, rows) + (whole,) * 5 + (narrow, whole, whole, row, row, row) + (whole,) * 3,
        check_vma=False,
    )
```

```python
from functools import partial

import jax
import jax.numpy as jnp
from jax import lax
from jax.experimental import pallas as pl
from jax.experimental.pallas import tpu as pltpu
from jax.sharding import Mesh
from jax.sharding import PartitionSpec as P

SPAN = 64
LANES = 128
STRIP = 64
CHUNKS = 2
DIRECT, SUMMED, PASSED = 0, 1, 2
WINDOW = 2

HIGH = lax.Precision.HIGHEST
MODEL_EPS = 1e-06
HEAD_EPS = 1e-05
GATE_SCALE = 16.0

f32 = jnp.float32
bf16 = jnp.bfloat16
GROUP = ("section", "q")


def dot_plain(left, right):
    return jnp.dot(left, right, preferred_element_type=f32)


def dot_left(left, right):
    return lax.dot_general(left, right, (((0,), (0,)), ((), ())), preferred_element_type=f32)


def dot_right(left, right):
    return lax.dot_general(left, right, (((1,), (1,)), ((), ())), preferred_element_type=f32)


def head_output(inner, out_gate, gain):
    r = lax.rsqrt(jnp.mean(inner * inner, axis=-1, keepdims=True) + HEAD_EPS)
    return gain * inner * r * jax.nn.silu(out_gate)


def normed_rows(u, gain):
    return gain * u * lax.rsqrt(jnp.mean(u * u, axis=-1, keepdims=True) + MODEL_EPS)


def norm_back(d, u, gain):
    s = lax.rsqrt(jnp.mean(u * u, axis=-1, keepdims=True) + MODEL_EPS)
    w = gain * d
    d_u = s * w - u * (s * s * s) * jnp.mean(w * u, axis=-1, keepdims=True)
    return d_u, jnp.sum(d * u * s, axis=0, keepdims=True)


def greet(signals, waits, extra=None):
    if extra is not None:
        signals, waits = {**extra.signals, **signals}, {**extra.waits, **waits}
    barrier = pltpu.get_barrier_semaphore()
    for condition, device in signals.values():
        if condition is None:
            pl.semaphore_signal(barrier, inc=1, device_id=device)
        else:

            @pl.when(condition)
            def _():
                pl.semaphore_signal(barrier, inc=1, device_id=device)

    due = sum(1 for condition in waits.values() if condition is None)
    for condition in waits.values():
        if condition is not None:
            due = due + condition.astype(jnp.int32)
    pl.semaphore_wait(barrier, due)


class Peers:
    def __init__(self, peers):
        assert peers == 4, peers
        self.peers = peers
        self.me = lax.axis_index("tensor")
        low, high = lax.rem(self.me, 2), self.me // 2
        self.beside = (high * 2 + 1 - low, (1 - high) * 2 + low)
        self.opposite = 3 - self.me

    def at(self, d):
        return lax.rem(self.me + d, self.peers)

    def enter(self, relay_to=None, extra=None):
        signals = {("tensor", d): (None, {"tensor": self.at(d)}) for d in range(1, self.peers)}
        waits = dict.fromkeys(signals)
        if relay_to is not None:
            stage = lax.axis_index("stage")
            signals["stage"] = (stage == relay_to, {"stage": 1 - relay_to})
            waits["stage"] = stage != relay_to
        greet(signals, waits, extra)


class Sum:
    def __init__(self, peers, part, send, land, sems, fine=None, fine_sems=None):
        self.peers, self.part, self.send, self.land, self.sems = peers, part, send, land, sems
        self.fine, self.fine_sems = fine, fine_sems
        self.pieces = part.shape[2] // LANES
        self.step = part.shape[1] // CHUNKS

    def rows(self, c):
        return slice(c * self.step, (c + 1) * self.step)

    def copy(self, kind, c):
        target = self.peers.beside[1 - c if kind == SUMMED else c]
        return pltpu.make_async_remote_copy(
            src_ref=self.send.at[kind, c],
            dst_ref=self.land.at[kind, c],
            send_sem=self.sems.at[0, kind, c],
            recv_sem=self.sems.at[1, kind, c],
            device_id={"tensor": target},
        )

    def fine_copy(self, d):
        return pltpu.make_async_remote_copy(
            src_ref=self.fine.at[0],
            dst_ref=self.fine.at[d],
            send_sem=self.fine_sems.at[0, d - 1],
            recv_sem=self.fine_sems.at[1, d - 1],
            device_id={"tensor": 0},
        )

    def lanes(self, n):
        return slice(n * LANES, (n + 1) * LANES)

    def start(self):
        peers = self.peers
        for c in range(CHUNKS):
            self.send[PASSED, c] = self.part[peers.opposite, self.rows(c), :].astype(bf16)
            self.copy(PASSED, c).start()
        for c in range(CHUNKS):
            self.send[DIRECT, c] = self.part[peers.beside[c], self.rows(c), :].astype(bf16)
            self.copy(DIRECT, c).start()
        if self.fine is not None:
            for n in range(self.pieces):
                self.fine[0, n : n + 1, :] = self.part[0, 0:1, self.lanes(n)]
            for d in range(1, peers.peers):

                @pl.when(peers.at(d) == 0)
                def _():
                    self.fine_copy(d).start()

        for c in range(CHUNKS):
            self.copy(PASSED, c).wait_recv()
            own = self.part[peers.beside[1 - c], self.rows(c), :].astype(f32)
            self.send[SUMMED, c] = (own + self.land[PASSED, c].astype(f32)).astype(bf16)
            self.copy(SUMMED, c).start()

    def finish(self, c, total):
        self.copy(DIRECT, c).wait_recv()
        acc = self.part[self.peers.me, self.rows(c), :].astype(f32)
        acc = acc + self.land[DIRECT, c].astype(f32)
        self.copy(SUMMED, c).wait_recv()
        total[self.rows(c), :] = acc + self.land[SUMMED, c].astype(f32)
        if c == 0 and self.fine is not None:

            @pl.when(self.peers.me == 0)
            def _():
                top = self.fine[0]
                for d in range(1, self.peers.peers):
                    self.fine_copy(d).wait_recv()
                    top = top + self.fine[d]
                for n in range(self.pieces):
                    total[0:1, self.lanes(n)] = top[n : n + 1, :]

        return total[self.rows(c), :]

    def drain(self):
        for c in range(CHUNKS):
            for kind in (PASSED, DIRECT, SUMMED):
                self.copy(kind, c).wait_send()
        if self.fine is not None:
            for d in range(1, self.peers.peers):

                @pl.when(self.peers.at(d) == 0)
                def _():
                    self.fine_copy(d).wait_send()


class Share:
    def __init__(self, peers, full, sems):
        self.peers, self.full, self.sems = peers, full, sems
        self.step = full.shape[1] // CHUNKS

    def copy(self, kind, c):
        peers = self.peers
        if kind == PASSED:
            source, target = peers.beside[c], peers.beside[1 - c]
        else:
            source, target = peers.me, peers.beside[kind]
        block = self.full.at[source, pl.ds(c * self.step, self.step)]
        return pltpu.make_async_remote_copy(
            src_ref=block,
            dst_ref=block,
            send_sem=self.sems.at[0, kind, c],
            recv_sem=self.sems.at[1, kind, c],
            device_id={"tensor": target},
        )

    def start(self, c, value):
        self.full[self.peers.me, c * self.step : (c + 1) * self.step, :] = value
        for kind in range(2):
            self.copy(kind, c).start()

    def finish(self):
        for c in range(CHUNKS):
            self.copy(c, c).wait_recv()
            self.copy(PASSED, c).start()
        for c in range(CHUNKS):
            self.copy(1 - c, c).wait_recv()
            self.copy(PASSED, c).wait_recv()
            for kind in range(3):
                self.copy(kind, c).wait_send()


def relay_rows(src, land, sems, c, relay_to):
    step = src.shape[0] // CHUNKS
    rows = pl.ds(c * step, step)
    return pltpu.make_async_remote_copy(
        src_ref=src.at[rows],
        dst_ref=land.at[rows],
        send_sem=sems.at[0, c],
        recv_sem=sems.at[1, c],
        device_id={"stage": relay_to},
    )


def first_kernel(peers_n, h, gain, full, share_sems, extra=None):
    peers = Peers(peers_n)
    peers.enter(extra=extra)
    if extra is not None:
        extra.start()
    share = Share(peers, full, share_sems)
    for c in range(CHUNKS):
        rows = slice(c * share.step, (c + 1) * share.step)
        share.start(c, normed_rows(h[rows, :].astype(f32), gain[...]).astype(bf16))
    share.finish()
    if extra is not None:
        extra.finish()


def forward_mid_kernel(
    peers_n, part, h, gain, middle, full, send, land, fine, total, sems, fine_sems, share_sems, extra=None):
    peers = Peers(peers_n)
    peers.enter(extra=extra)
    if extra is not None:
        extra.start()
    reduced = Sum(peers, part, send, land, sems, fine, fine_sems)
    share = Share(peers, full, share_sems)
    reduced.start()
    for c in range(CHUNKS):
        rows = reduced.rows(c)
        value = h[rows, :].astype(f32) + reduced.finish(c, total)
        middle[rows, :] = value
        share.start(c, normed_rows(value, gain[...]).astype(bf16))
    share.finish()
    reduced.drain()
    if extra is not None:
        extra.finish()


def forward_end_kernel(
    peers_n,
    part,
    middle,
    gain,
    own,
    y,
    h,
    full,
    send,
    land,
    fine,
    total,
    relayed,
    sems,
    fine_sems,
    share_sems,
    relay_sems,
):
    peers = Peers(peers_n)
    stage = lax.axis_index("stage")
    peers.enter(1)
    reduced = Sum(peers, part, send, land, sems, fine, fine_sems)
    share = Share(peers, full, share_sems)
    reduced.start()
    for c in range(CHUNKS):
        rows = reduced.rows(c)
        relay = relay_rows(y, relayed, relay_sems, c, 1)

        @pl.when(stage == 0)
        def _():
            y[rows, :] = (middle[rows, :] + reduced.finish(c, total)).astype(bf16)
            relay.start()
            h[rows, :] = own[rows, :]

        @pl.when(stage == 1)
        def _():
            y[rows, :] = (middle[rows, :] + reduced.finish(c, total)).astype(bf16)
            relay.wait_recv()
            h[rows, :] = relayed[rows, :]

        share.start(c, normed_rows(h[rows, :].astype(f32), gain[...]).astype(bf16))

    share.finish()

    @pl.when(stage == 0)
    def _():
        for c in range(CHUNKS):
            relay_rows(y, relayed, relay_sems, c, 1).wait_send()
    reduced.drain()


def forward_last_kernel(
    peers_n, part, middle, gy, y, full, send, land, fine, total, sems, fine_sems, share_sems
):
    peers = Peers(peers_n)
    peers.enter()
    reduced = Sum(peers, part, send, land, sems, fine, fine_sems)
    share = Share(peers, full, share_sems)
    reduced.start()
    for c in range(CHUNKS):
        share.start(c, gy[reduced.rows(c), :])
    for c in range(CHUNKS):
        rows = reduced.rows(c)
        y[rows, :] = (middle[rows, :] + reduced.finish(c, total)).astype(bf16)
    share.finish()
    reduced.drain()


def backward_mid_kernel(
    peers_n, part, gy, middle, gain, d_middle, gain_part, full, send, land, total, sems, share_sems, extra=None):
    peers = Peers(peers_n)
    peers.enter(extra=extra)
    if extra is not None:
        extra.start()
    reduced = Sum(peers, part, send, land, sems)
    share = Share(peers, full, share_sems)
    reduced.start()
    gains = jnp.zeros(gain_part.shape, f32)
    for c in range(CHUNKS):
        rows = reduced.rows(c)
        d_u, g = norm_back(reduced.finish(c, total), middle[rows, :], gain[...])
        value = gy[rows, :].astype(f32) + d_u
        d_middle[rows, :] = value
        gains = gains + g
        share.start(c, value.astype(bf16))
    gain_part[...] = gains
    share.finish()
    reduced.drain()
    if extra is not None:
        extra.finish()


def backward_end_kernel(
    peers_n,
    part,
    d_middle,
    h,
    gain,
    own,
    grad,
    gain_part,
    gy,
    full,
    send,
    land,
    total,
    relayed,
    sems,
    share_sems,
    relay_sems,
    extra=None,
):
    peers = Peers(peers_n)
    stage = lax.axis_index("stage")
    peers.enter(0, extra)
    reduced = Sum(peers, part, send, land, sems)
    share = Share(peers, full, share_sems)
    reduced.start()
    if extra is not None:
        extra.start()
    gain_part[...] = jnp.zeros(gain_part.shape, f32)

    def finish(c):
        rows = reduced.rows(c)
        d_u, g = norm_back(reduced.finish(c, total), h[rows, :].astype(f32), gain[...])
        grad[rows, :] = (d_middle[rows, :] + d_u).astype(bf16)
        gain_part[...] += g

    for c in range(CHUNKS):
        rows = reduced.rows(c)
        relay = relay_rows(grad, relayed, relay_sems, c, 0)

        @pl.when(stage == 1)
        def _():
            finish(c)
            relay.start()
            gy[rows, :] = own[rows, :]

        @pl.when(stage == 0)
        def _():
            finish(c)
            relay.wait_recv()
            gy[rows, :] = relayed[rows, :]

        share.start(c, gy[rows, :])

    share.finish()

    @pl.when(stage == 1)
    def _():
        for c in range(CHUNKS):
            relay_rows(grad, relayed, relay_sems, c, 0).wait_send()
    reduced.drain()
    if extra is not None:
        extra.finish()


def backward_last_kernel(
    peers_n, part, d_middle, h, gain, grad, gain_part, send, land, total, sems, extra=None):
    peers = Peers(peers_n)
    peers.enter(extra=extra)
    if extra is not None:
        extra.start()
    reduced = Sum(peers, part, send, land, sems)
    reduced.start()
    gains = jnp.zeros(gain_part.shape, f32)
    for c in range(CHUNKS):
        rows = reduced.rows(c)
        d_u, g = norm_back(reduced.finish(c, total), h[rows, :].astype(f32), gain[...])
        grad[rows, :] = (d_middle[rows, :] + d_u).astype(bf16)
        gains = gains + g
    gain_part[...] = gains
    reduced.drain()
    if extra is not None:
        extra.finish()


def in_vmem(count):
    return [pl.BlockSpec(memory_space=pltpu.VMEM)] * count


def kernel_call(body, outs, scratch, ident, *args, extra=None):
    outs = outs if isinstance(outs, list) else [outs]
    in_specs, out_specs = in_vmem(len(args)), in_vmem(len(outs))
    if extra is not None:
        kind, more_args, more_outs, more_scratch = extra
        sizes = [len(args), len(more_args), len(outs), len(more_outs), len(scratch)]
        own_body = body

        def body(*refs):
            cuts = [sum(sizes[:n]) for n in range(len(sizes) + 1)]
            parts = [refs[cuts[n] : cuts[n + 1]] for n in range(len(sizes))] + [refs[cuts[-1] :]]
            own_body(
                *parts[0], *parts[2], *parts[4], extra=kind(*parts[1], *parts[3], *parts[5])
            )

        anywhere = pl.BlockSpec(memory_space=pl.ANY)
        args, outs = args + tuple(more_args), outs + more_outs
        scratch = scratch + more_scratch
        in_specs = in_specs + [anywhere] * len(more_args)
        out_specs = out_specs + [anywhere] * len(more_outs)
    results = pl.pallas_call(
        body,
        out_shape=outs,
        in_specs=in_specs,
        out_specs=out_specs,
        scratch_shapes=scratch,
        compiler_params=pltpu.CompilerParams(
            collective_id=ident, has_side_effects=True, vmem_limit_bytes=40 * 1024 * 1024
        ),
    )(*args)
    return results[0] if len(results) == 1 else list(results)


def shape(dims, kind):
    return jax.ShapeDtypeStruct(dims, kind)


class Rows:
    def __init__(self, rows, width, peers):
        self.rows, self.width, self.peers = rows, width, peers
        self.slice_b = shape((rows, width), bf16)
        self.slice_f = shape((rows, width), f32)
        self.gain_f = shape((1, width), f32)
        self.full = shape((peers, rows, width), bf16)
        self.pair = pltpu.SemaphoreType.DMA((2, peers - 1))
        self.many = pltpu.SemaphoreType.DMA((2, 3, CHUNKS))
        self.reduce = [
            pltpu.VMEM((3, CHUNKS, rows // CHUNKS, width), bf16),
            pltpu.VMEM((3, CHUNKS, rows // CHUNKS, width), bf16),
        ]
        self.fine = [pltpu.VMEM((peers, width // LANES, LANES), f32)]
        self.total = [pltpu.VMEM((rows, width), f32)]
        self.relayed = [pltpu.VMEM((rows, width), bf16)]
        self.relay = pltpu.SemaphoreType.DMA((2, CHUNKS))

    def parts(self, part):
        return part.reshape(self.peers, self.rows, self.width)

    def flat(self, full):
        return full.reshape(self.peers * self.rows, self.width)

    def first(self, h, gain, extra):
        body = partial(first_kernel, self.peers)
        full, *more = kernel_call(body, self.full, [self.many], 1, h, gain, extra=extra)
        return self.flat(full), *more

    def forward_mid(self, part, h, gain, ident=3, extra=None):
        middle, full, *more = kernel_call(
            partial(forward_mid_kernel, self.peers),
            [self.slice_f, self.full],
            self.reduce + self.fine + self.total + [self.many, self.pair, self.many],
            ident,
            self.parts(part),
            h,
            gain,
            extra=extra,
        )
        return middle, self.flat(full), *more

    def forward_end(self, part, middle, gain, own):
        y, h, full = kernel_call(
            partial(forward_end_kernel, self.peers),
            [self.slice_b, self.slice_b, self.full],
            self.reduce
            + self.fine
            + self.total
            + self.relayed
            + [self.many, self.pair, self.many, self.relay],
            4,
            self.parts(part),
            middle,
            gain,
            own,
        )
        return y, h, self.flat(full)

    def forward_last(self, part, middle, gy):
        y, full = kernel_call(
            partial(forward_last_kernel, self.peers),
            [self.slice_b, self.full],
            self.reduce + self.fine + self.total + [self.many, self.pair, self.many],
            5,
            self.parts(part),
            middle,
            gy,
        )
        return y, self.flat(full)

    def backward_mid(self, part, gy, middle, gain, ident=6, extra=None):
        d_middle, gain_part, full, *more = kernel_call(
            partial(backward_mid_kernel, self.peers),
            [self.slice_f, self.gain_f, self.full],
            self.reduce + self.total + [self.many] * 2,
            ident,
            self.parts(part),
            gy,
            middle,
            gain,
            extra=extra,
        )
        return d_middle, gain_part, self.flat(full), *more

    def backward_end(self, part, d_middle, h, gain, own, ident=7, extra=None):
        grad, gain_part, gy, full, *more = kernel_call(
            partial(backward_end_kernel, self.peers),
            [self.slice_b, self.gain_f, self.slice_b, self.full],
            self.reduce + self.total + self.relayed + [self.many] * 2 + [self.relay],
            ident,
            self.parts(part),
            d_middle,
            h,
            gain,
            own,
            extra=extra,
        )
        return grad, gain_part, gy, self.flat(full), *more

    def backward_last(self, part, d_middle, h, gain, extra=None):
        return kernel_call(
            partial(backward_last_kernel, self.peers),
            [self.slice_b, self.gain_f],
            self.reduce + self.total + [self.many],
            8,
            self.parts(part),
            d_middle,
            h,
            gain,
            extra=extra,
        )


PAD = 16


class Chain:
    def __init__(self, ranges, half):
        self.ranges, self.half = ranges, half
        self.s, self.q = lax.axis_index("section"), lax.axis_index("q")
        self.me = self.s * half + self.q

    def after(self, d):
        return lax.rem(self.q + d, self.half)

    def before(self, d):
        return self.s * self.half + lax.rem(self.q + self.half - d, self.half)

    def enter(self, extra=None):
        signals = {("q", d): (None, {"q": self.after(d)}) for d in range(1, self.half)}
        signals["core"] = (None, {"section": 1 - self.s})
        greet(signals, dict.fromkeys(signals), extra)

    def along(self, land, sems, d):
        return pltpu.make_async_remote_copy(
            src_ref=land.at[self.me],
            dst_ref=land.at[self.me],
            send_sem=sems.at[0, d],
            recv_sem=sems.at[1, d],
            device_id={"q": self.after(d)},
        )

    def across(self, land, sems, d):
        return pltpu.make_async_remote_copy(
            src_ref=land.at[self.before(d)],
            dst_ref=land.at[self.before(d)],
            send_sem=sems.at[2, d],
            recv_sem=sems.at[3, d],
            device_id={"section": 1 - self.s},
        )

    def start(self, land, sems, state, through):
        high = state.shape[0]
        land[self.me, 0:high, :] = state.astype(bf16)
        land[self.me, high : high + PAD, :] = jnp.broadcast_to(
            through, (PAD, through.shape[1])
        ).astype(bf16)
        for d in range(1, self.half):
            self.along(land, sems, d).start()
        self.across(land, sems, 0).start()

    def forward(self, land, sems):
        for d in range(1, self.half):
            self.along(land, sems, d).wait_recv()
            self.across(land, sems, d).start()

    def finish(self, land, sems, high, later):
        for d in range(1, self.half):
            self.along(land, sems, d).wait_send()
        for d in range(self.half):
            self.across(land, sems, d).wait()

        def step(n, state):
            place = self.ranges - 1 - n if later else n
            taken = (place > self.me) if later else (place < self.me)
            through = land[place, high : high + PAD, :].astype(f32)[0:1, :]
            joined = through * state + land[place, 0:high, :].astype(f32)
            return jnp.where(taken, joined, state)

        zero = jnp.zeros((high, land.shape[2]), f32)
        state = zero
        for n in range(self.ranges):
            state = step(n, state)
        return state


def triangle(size):
    row = lax.broadcasted_iota(jnp.int32, (size, size), 0)
    col = lax.broadcasted_iota(jnp.int32, (size, size), 1)
    return row, col


def scores_of(q, k, c, fine):
    row, col = triangle(SPAN)
    middle = c[SPAN // 2 : SPAN // 2 + 1, :]
    up, down = jnp.exp(c - middle), jnp.exp(middle - c)
    a, b = q * up, k * down
    own = jnp.sum(q * k, axis=1, keepdims=True)
    if fine:
        scores = lax.dot_general(
            a, b, (((1,), (1,)), ((), ())), precision=HIGH, preferred_element_type=f32
        )
    a, b = a.astype(bf16), b.astype(bf16)
    if not fine:
        scores = dot_right(a, b)
    return jnp.where(row > col, scores, 0.0).astype(bf16), own, a, b, up, down


class Cuts:
    def __init__(self, key_dim, value_dim, rank):
        self.key, self.value = key_dim, value_dim
        self.q = slice(0, key_dim)
        self.k = slice(key_dim, 2 * key_dim)
        self.v = slice(2 * key_dim, 2 * key_dim + value_dim)
        self.og = slice(2 * key_dim + value_dim, 2 * key_dim + 2 * value_dim)
        self.begin = 2 * key_dim + 2 * value_dim
        self.width = self.begin + LANES * (-(-rank // LANES))
        self.rank = slice(self.begin, self.width)


def rounded(array):
    return array.astype(bf16).astype(f32)


def log_sigmoid(u):
    return jnp.minimum(u, 0.0) - jnp.log1p(jnp.exp(-jnp.abs(u)))


def mixer_forward_kernel(
    ranges, half, cuts, cat, up, bias, inner_ref, c_ref, l_ref, s_ref,
    moved, out, land, sems, extra=None,
):
    chain = Chain(ranges, half)
    chain.enter(extra)
    length = cat.shape[0]
    spans = length // SPAN
    scale = cuts.key ** (-0.5)
    row, col = triangle(SPAN)
    lower = (row >= col).astype(f32)
    state = jnp.zeros((cuts.value, cuts.key), f32)
    reach = jnp.zeros((1, cuts.key), f32)
    for i in range(spans):
        rows = slice(i * SPAN, (i + 1) * SPAN)
        logits = (
            jnp.dot(cat[rows, cuts.rank], up[...], precision=HIGH, preferred_element_type=f32)
            + bias[...]
        )
        l_ref[rows, :] = logits
        decay = log_sigmoid(logits) * (1.0 / GATE_SCALE)
        c = jnp.dot(lower, decay, precision=HIGH, preferred_element_type=f32)
        c_ref[rows, :] = c
        last = c[SPAN - 1 : SPAN, :]
        fading = (rounded(cat[rows, cuts.k]) * jnp.exp(last - c)).astype(bf16)
        step = dot_left(cat[rows, cuts.v].astype(bf16), fading)
        moved[i] = step
        state = jnp.exp(last) * state + step
        reach = reach + last
    chain.start(land, sems, state, jnp.exp(reach))
    if extra is not None:
        extra.start()
    for i in range(spans):
        rows = slice(i * SPAN, (i + 1) * SPAN)
        q = rounded(cat[rows, cuts.q]) * scale
        k = rounded(cat[rows, cuts.k])
        scores, own, *_ = scores_of(q, k, c_ref[rows, :], True)
        v = cat[rows, cuts.v].astype(bf16)
        out[rows, :] = dot_plain(scores, v) + own * v.astype(f32)
    chain.forward(land, sems)
    state = chain.finish(land, sems, cuts.value, False)
    for i in range(spans):
        rows = slice(i * SPAN, (i + 1) * SPAN)
        c = c_ref[rows, :]
        held = state.astype(bf16)
        s_ref[i] = held
        q = (rounded(cat[rows, cuts.q]) * scale * jnp.exp(c)).astype(bf16)
        inner_ref[rows, :] = out[rows, :] + dot_right(q, held)
        state = jnp.exp(c[SPAN - 1 : SPAN, :]) * state + moved[i]
    s_ref[spans] = state.astype(bf16)
    if extra is not None:
        extra.finish()


def mixer_backward_kernel(
    ranges, half, cuts, dgated_ref, inner_ref, cat, up, hg_ref, c_ref, l_ref, s_ref,
    dcat, hgp_ref, dup_ref, dbias_ref, pulled, o_ref, dqs, dks, dvs, land, sems, extra=None,
):
    chain = Chain(ranges, half)
    chain.enter(extra)
    length = cat.shape[0]
    spans = length // SPAN
    scale = cuts.key ** (-0.5)
    row, col = triangle(SPAN)
    upper = (row <= col).astype(f32)
    state = jnp.zeros((cuts.value, cuts.key), f32)
    reach = jnp.zeros((1, cuts.key), f32)
    hg = hg_ref[...]
    head_part = jnp.zeros((1, cuts.value), f32)
    for i in reversed(range(spans)):
        rows = slice(i * SPAN, (i + 1) * SPAN)
        inner, og, dgated = inner_ref[rows, :], cat[rows, cuts.og], dgated_ref[rows, :]
        r = lax.rsqrt(jnp.mean(inner * inner, axis=-1, keepdims=True) + HEAD_EPS)
        sg = 1.0 / (1.0 + jnp.exp(-og))
        d_norm = dgated * (og * sg)
        unit = inner * r
        head_part = head_part + jnp.sum(d_norm * unit, axis=0, keepdims=True)
        w = d_norm * hg
        d_inner = r * w - inner * (r * r * r) * jnp.mean(w * inner, axis=-1, keepdims=True)
        dog = dgated * unit * hg * (sg * (1.0 + og * (1.0 - sg)))
        dcat[rows, cuts.og] = dog.astype(bf16)
        o_ref[rows, :] = d_inner
        o = d_inner.astype(bf16)
        c = c_ref[rows, :]
        q = (rounded(cat[rows, cuts.q]) * scale * jnp.exp(c)).astype(bf16)
        step = dot_left(o, q)
        pulled[i] = step
        last = c[SPAN - 1 : SPAN, :]
        state = jnp.exp(last) * state + step
        reach = reach + last
    hgp_ref[...] = head_part
    chain.start(land, sems, state, jnp.exp(reach))
    if extra is not None:
        extra.start()
    for i in range(spans):
        rows = slice(i * SPAN, (i + 1) * SPAN)
        q = rounded(cat[rows, cuts.q]) * scale
        k = rounded(cat[rows, cuts.k])
        scores, own, a, b, gain_up, gain_down = scores_of(q, k, c_ref[rows, :], False)
        d_inner, v = o_ref[rows, :], cat[rows, cuts.v].astype(bf16)
        o = d_inner.astype(bf16)
        d_own = jnp.sum(d_inner * v.astype(f32), axis=1, keepdims=True)
        d_scores = jnp.where(row > col, dot_right(o, v), 0.0).astype(bf16)
        dvs[rows, :] = dot_left(scores, o) + own * d_inner
        dqs[rows, :] = (
            d_own * k
            + gain_up * dot_plain(d_scores, b)
            + jnp.exp(c_ref[rows, :]) * dot_plain(o, s_ref[i])
        )
        dks[rows, :] = d_own * q + gain_down * dot_left(d_scores, a)
    chain.forward(land, sems)
    state = chain.finish(land, sems, cuts.value, True)
    d_up = jnp.zeros(dup_ref.shape, f32)
    d_bias = jnp.zeros(dbias_ref.shape, f32)
    for i in reversed(range(spans)):
        rows = slice(i * SPAN, (i + 1) * SPAN)
        c = c_ref[rows, :]
        last = c[SPAN - 1 : SPAN, :]
        fade = jnp.exp(last - c)
        held = state.astype(bf16)
        k = rounded(cat[rows, cuts.k])
        dk = dks[rows, :] + fade * dot_plain(cat[rows, cuts.v].astype(bf16), held)
        dv = dvs[rows, :] + dot_right((k * fade).astype(bf16), held)
        dq = dqs[rows, :]
        dcat[rows, cuts.q] = (dq * scale).astype(bf16)
        dcat[rows, cuts.k] = dk.astype(bf16)
        dcat[rows, cuts.v] = dv.astype(bf16)
        ended = jnp.sum(state * s_ref[i + 1].astype(f32), axis=0, keepdims=True)
        terms = rounded(cat[rows, cuts.q]) * scale * dq - k * dk
        d_decay = jnp.dot(upper, terms, precision=HIGH, preferred_element_type=f32) + ended
        d_logits = d_decay * (1.0 / (1.0 + jnp.exp(l_ref[rows, :]))) * (1.0 / GATE_SCALE)
        d_bias = d_bias + jnp.sum(d_logits, axis=0, keepdims=True)
        d_up = d_up + lax.dot_general(
            cat[rows, cuts.rank], d_logits, (((0,), (0,)), ((), ())),
            precision=HIGH, preferred_element_type=f32,
        )
        d_rank = lax.dot_general(
            d_logits, up[...], (((1,), (1,)), ((), ())),
            precision=HIGH, preferred_element_type=f32,
        )
        dcat[rows, cuts.rank] = d_rank.astype(bf16)
        state = jnp.exp(last) * state + pulled[i]
    dup_ref[...] = d_up
    dbias_ref[...] = d_bias
    if extra is not None:
        extra.finish()


def mixer_forward(ranges, half, cuts, cat, up, bias, ident=9, extra=None):
    length = cat.shape[0]
    spans = length // SPAN
    return kernel_call(
        partial(mixer_forward_kernel, ranges, half, cuts),
        [
            shape((length, cuts.value), f32),
            shape((length, cuts.key), f32),
            shape((length, cuts.key), f32),
            shape((spans + 1, cuts.value, cuts.key), bf16),
        ],
        [
            pltpu.VMEM((spans, cuts.value, cuts.key), f32),
            pltpu.VMEM((length, cuts.value), f32),
            pltpu.VMEM((ranges, cuts.value + PAD, cuts.key), bf16),
            pltpu.SemaphoreType.DMA((4, half)),
        ],
        ident,
        cat, up, bias,
        extra=extra,
    )


def mixer_backward(
    ranges, half, cuts, dgated, inner, cat, up, hg, c, logits, s, ident=10, extra=None
):
    length = cat.shape[0]
    spans = length // SPAN
    return kernel_call(
        partial(mixer_backward_kernel, ranges, half, cuts),
        [
            shape((length, cuts.width), bf16),
            shape((1, cuts.value), f32),
            shape(up.shape, f32),
            shape((1, cuts.key), f32),
        ],
        [
            pltpu.VMEM((spans, cuts.value, cuts.key), f32),
            pltpu.VMEM((length, cuts.value), f32),
            pltpu.VMEM((length, cuts.key), f32),
            pltpu.VMEM((length, cuts.key), f32),
            pltpu.VMEM((length, cuts.value), f32),
            pltpu.VMEM((ranges, cuts.value + PAD, cuts.key), bf16),
            pltpu.SemaphoreType.DMA((4, half)),
        ],
        ident,
        dgated, inner, cat, up, hg, c, logits, s,
        extra=extra,
    )


class Ranges:
    def __init__(self, half):
        self.half = half
        self.s, self.l = lax.axis_index("section"), lax.axis_index("stage")
        self.q = lax.axis_index("q")
        self.stays = self.s == self.l

    def enter(self, cores):
        barrier = pltpu.get_barrier_semaphore()
        for d in range(1, self.half):
            pl.semaphore_signal(barrier, inc=1, device_id={"q": self.after(d)})
        count = self.half - 1
        if cores:
            pl.semaphore_signal(barrier, inc=1, device_id={"section": 1 - self.s})
            count = count + 1

        @pl.when(self.stays)
        def _():
            pl.semaphore_wait(barrier, count)

        @pl.when(jnp.logical_not(self.stays))
        def _():
            pl.semaphore_signal(barrier, inc=1, device_id={"section": self.l, "stage": self.s})
            pl.semaphore_wait(barrier, count + 1)

    def after(self, d):
        return lax.rem(self.q + d, self.half)

    def before(self, d):
        return lax.rem(self.q + self.half - d, self.half)

    def at(self, section, q, rows):
        return pl.ds(pl.multiple_of((section * self.half + q) * rows, rows), rows)


def gather_kernel(half, count, *refs):
    ins, outs, bounce = refs[:count], refs[count : 2 * count], refs[2 * count : 3 * count]
    swap_sems, z_sems, core_sems, keep_sems = refs[3 * count :]
    r = Ranges(half)
    r.enter(True)

    def held(i):
        rows = ins[i].shape[0]
        return outs[i].at[r.at(r.s, r.q, rows)]

    def swap(i):
        rows = ins[i].shape[0]
        return pltpu.make_async_remote_copy(
            src_ref=ins[i],
            dst_ref=outs[i].at[r.at(r.l, r.q, rows)],
            send_sem=swap_sems.at[0, i],
            recv_sem=swap_sems.at[1, i],
            device_id={"section": r.l, "stage": r.s},
        )

    def along(i, d, src):
        return pltpu.make_async_remote_copy(
            src_ref=src,
            dst_ref=held(i),
            send_sem=z_sems.at[0, i, d - 1],
            recv_sem=z_sems.at[1, i, d - 1],
            device_id={"q": r.after(d)},
        )

    def across(i, d, src):
        rows = ins[i].shape[0]
        return pltpu.make_async_remote_copy(
            src_ref=src,
            dst_ref=outs[i].at[r.at(r.s, r.before(d), rows)],
            send_sem=core_sems.at[0, i, d],
            recv_sem=core_sems.at[1, i, d],
            device_id={"section": 1 - r.s},
        )

    def load(i):
        return pltpu.make_async_copy(ins[i], bounce[i], keep_sems.at[0, i])

    def keep(i):
        return pltpu.make_async_copy(bounce[i], held(i), keep_sems.at[1, i])

    @pl.when(r.stays)
    def _():
        for i in range(count):
            for d in range(1, half):
                along(i, d, ins[i]).start()
            across(i, 0, ins[i]).start()
            load(i).start()
        for i in range(count):
            load(i).wait()
            keep(i).start()

    @pl.when(jnp.logical_not(r.stays))
    def _():
        for i in range(count):
            swap(i).start()

    for i in range(count):
        rows = ins[i].shape[0]

        @pl.when(jnp.logical_not(r.stays))
        def _():
            swap(i).wait_recv()
            for d in range(1, half):
                along(i, d, held(i)).start()
            across(i, 0, held(i)).start()

        for d in range(1, half):
            along(i, d, ins[i]).wait_recv()
            across(i, d, outs[i].at[r.at(r.s, r.before(d), rows)]).start()

    for i in range(count):

        @pl.when(r.stays)
        def _():
            keep(i).wait()

        @pl.when(jnp.logical_not(r.stays))
        def _():
            swap(i).wait_send()

        for d in range(1, half):
            along(i, d, ins[i]).wait_send()
        for d in range(half):
            across(i, d, ins[i]).wait()


def gather_weights(half, ident, *shards_in):
    count = len(shards_in)
    anywhere = pl.BlockSpec(memory_space=pl.ANY)
    return pl.pallas_call(
        partial(gather_kernel, half, count),
        out_shape=[shape((2 * half * a.shape[0], a.shape[1]), a.dtype) for a in shards_in],
        in_specs=[anywhere] * count,
        out_specs=[anywhere] * count,
        scratch_shapes=[pltpu.VMEM(a.shape, a.dtype) for a in shards_in]
        + [
            pltpu.SemaphoreType.DMA((2, count)),
            pltpu.SemaphoreType.DMA((2, count, half - 1)),
            pltpu.SemaphoreType.DMA((2, count, half)),
            pltpu.SemaphoreType.DMA((2, count)),
        ],
        compiler_params=pltpu.CompilerParams(
            collective_id=ident, has_side_effects=True, vmem_limit_bytes=40 * 1024 * 1024
        ),
    )(*shards_in)


class GatherStart:
    def __init__(self, half, home, whole, bounce, swap_sems, z_sems, core_sems, keep_sems):
        r = self.r = Ranges(half)
        rows = home.shape[0]
        self.half = half
        moves = jnp.logical_not(r.stays)
        self.signals = {("q", d): (None, {"q": r.after(d)}) for d in range(1, half)}
        self.signals["core"] = (None, {"section": 1 - r.s})
        self.signals["swap"] = (moves, {"section": r.l, "stage": r.s})
        self.waits = {name: condition for name, (condition, _) in self.signals.items()}
        held = whole.at[r.at(r.s, r.q, rows)]
        self.swap = pltpu.make_async_remote_copy(
            src_ref=home,
            dst_ref=whole.at[r.at(r.l, r.q, rows)],
            send_sem=swap_sems.at[0],
            recv_sem=swap_sems.at[1],
            device_id={"section": r.l, "stage": r.s},
        )
        self.along = [
            pltpu.make_async_remote_copy(
                src_ref=home,
                dst_ref=held,
                send_sem=z_sems.at[0, d - 1],
                recv_sem=z_sems.at[1, d - 1],
                device_id={"q": r.after(d)},
            )
            for d in range(1, half)
        ]
        self.across = pltpu.make_async_remote_copy(
            src_ref=home,
            dst_ref=held,
            send_sem=core_sems.at[0],
            recv_sem=core_sems.at[1],
            device_id={"section": 1 - r.s},
        )
        self.load = pltpu.make_async_copy(home, bounce, keep_sems.at[0])
        self.keep = pltpu.make_async_copy(bounce, held, keep_sems.at[1])

    def start(self):
        @pl.when(self.r.stays)
        def _():
            for copy in self.along:
                copy.start()
            self.across.start()
            self.load.start()

        @pl.when(jnp.logical_not(self.r.stays))
        def _():
            self.swap.start()

    def finish(self):
        @pl.when(self.r.stays)
        def _():
            self.load.wait()
            self.keep.start()
            for copy in self.along:
                copy.wait()
            self.across.wait_send()
            self.keep.wait()

        @pl.when(jnp.logical_not(self.r.stays))
        def _():
            self.swap.wait()
            self.across.wait_recv()


def gather_start(half, home):
    return (
        partial(GatherStart, half),
        [home],
        [shape((2 * half * home.shape[0], home.shape[1]), home.dtype)],
        [
            pltpu.VMEM(home.shape, home.dtype),
            pltpu.SemaphoreType.DMA((2,)),
            pltpu.SemaphoreType.DMA((2, half - 1)),
            pltpu.SemaphoreType.DMA((2,)),
            pltpu.SemaphoreType.DMA((2,)),
        ],
    )


def gather_end_kernel(half, count, rows, *refs):
    outs = refs[count : 2 * count]
    z_sems, core_sems = refs[2 * count :]
    r = Ranges(half)
    r.enter(True)

    def piece(i, q):
        return outs[i].at[r.at(r.s, q, rows)]

    def along(i, d):
        return pltpu.make_async_remote_copy(
            src_ref=piece(i, r.q),
            dst_ref=piece(i, r.q),
            send_sem=z_sems.at[0, i, d - 1],
            recv_sem=z_sems.at[1, i, d - 1],
            device_id={"q": r.after(d)},
        )

    def across(i, d):
        return pltpu.make_async_remote_copy(
            src_ref=piece(i, r.before(d)),
            dst_ref=piece(i, r.before(d)),
            send_sem=core_sems.at[0, i, d],
            recv_sem=core_sems.at[1, i, d],
            device_id={"section": 1 - r.s},
        )

    @pl.when(r.stays)
    def _():
        for i in range(count):
            for d in range(1, half):
                across(i, d).start()
        for i in range(count):
            for d in range(1, half):
                across(i, d).wait()
            across(i, 0).wait_recv()

    @pl.when(jnp.logical_not(r.stays))
    def _():
        for i in range(count):
            for d in range(1, half):
                along(i, d).start()
        for i in range(count):
            across(i, 0).start()
        for i in range(count):
            for d in range(1, half):
                along(i, d).wait_recv()
                across(i, d).start()
        for i in range(count):
            for d in range(1, half):
                along(i, d).wait_send()
                across(i, d).wait()
            across(i, 0).wait_send()


def gather_end(half, ident, *begun):
    count = len(begun)
    rows = begun[0].shape[0] // (2 * half)
    anywhere = pl.BlockSpec(memory_space=pl.ANY)
    return pl.pallas_call(
        partial(gather_end_kernel, half, count, rows),
        out_shape=[shape(a.shape, a.dtype) for a in begun],
        in_specs=[anywhere] * count,
        out_specs=[anywhere] * count,
        scratch_shapes=[
            pltpu.SemaphoreType.DMA((2, count, half - 1)),
            pltpu.SemaphoreType.DMA((2, count, half)),
        ],
        input_output_aliases={i: i for i in range(count)},
        compiler_params=pltpu.CompilerParams(collective_id=ident, has_side_effects=True),
    )(*begun)


class AlongStart:
    def __init__(self, half, rows, *refs):
        r = self.r = Ranges(half)
        self.signals = {("q", d): (None, {"q": r.after(d)}) for d in range(1, half)}
        self.swap = None
        if len(refs) == 3:
            total, away, sems = refs
        else:
            total, summed, away, landed, sems, swap_sems = refs
            self.moves = jnp.logical_not(r.stays)
            self.signals["swap"] = (self.moves, {"section": r.l, "stage": r.s})
            self.swap = pltpu.make_async_remote_copy(
                src_ref=summed,
                dst_ref=landed,
                send_sem=swap_sems.at[0],
                recv_sem=swap_sems.at[1],
                device_id={"section": r.l, "stage": r.s},
            )
        self.waits = {name: condition for name, (condition, _) in self.signals.items()}
        self.copies = [
            pltpu.make_async_remote_copy(
                src_ref=total.at[r.at(0, r.after(d), rows)],
                dst_ref=away.at[d - 1],
                send_sem=sems.at[0, d - 1],
                recv_sem=sems.at[1, d - 1],
                device_id={"q": r.after(d)},
            )
            for d in range(1, half)
        ]

    def start(self):
        for copy in self.copies:
            copy.start()
        if self.swap is not None:

            @pl.when(self.moves)
            def _():
                self.swap.start()

    def finish(self):
        for copy in self.copies:
            copy.wait()
        if self.swap is not None:

            @pl.when(self.moves)
            def _():
                self.swap.wait()


def along_start(half, total, summed=None):
    rows = total.shape[0] // half
    away = shape((half - 1, rows, total.shape[1]), total.dtype)
    sems = pltpu.SemaphoreType.DMA((2, half - 1))
    kind = partial(AlongStart, half, rows)
    if summed is None:
        return kind, [total], [away], [sems]
    landed = shape(summed.shape, summed.dtype)
    return kind, [total, summed], [away, landed], [sems, pltpu.SemaphoreType.DMA((2,))]


class HomeStart:
    def __init__(self, half, src, landed, sems):
        r = Ranges(half)
        self.moves = jnp.logical_not(r.stays)
        self.signals = {"swap": (self.moves, {"section": r.l, "stage": r.s})}
        self.waits = {"swap": self.moves}
        self.copy = pltpu.make_async_remote_copy(
            src_ref=src,
            dst_ref=landed,
            send_sem=sems.at[0],
            recv_sem=sems.at[1],
            device_id={"section": r.l, "stage": r.s},
        )

    def start(self):
        @pl.when(self.moves)
        def _():
            self.copy.start()

    def finish(self):
        @pl.when(self.moves)
        def _():
            self.copy.wait()


def home_start(half, array):
    sems = [pltpu.SemaphoreType.DMA((2,))]
    return partial(HomeStart, half), [array], [shape(array.shape, array.dtype)], sems


def finish_kernel(half, count, come, places, lanes, *refs):
    totals, aways = refs[:count], refs[count : count + come]
    refs = refs[count + come :]
    rows_in, small = refs[:places], refs[places]
    refs = refs[places + 1 :]
    outs, full, down, small_own, small_sum = (
        refs[:count],
        refs[count : count + places],
        refs[count + places],
        refs[count + places + 1],
        refs[count + places + 2],
    )
    refs = refs[count + places + 3 :]
    mine, got = refs[:count], refs[count : 2 * count]
    small_mine, small_got, small_land, down_send, down_land, held = refs[
        2 * count : 2 * count + 6
    ]
    (
        swap_sems, z_sems, load_sems, away_sems, place_sems, keep_sems, share_sems, small_sems,
        pool_sems,
    ) = refs[2 * count + 6 :]
    peers_n = full[0].shape[1]
    r = Ranges(half)
    peers = Peers(peers_n)
    barrier = pltpu.get_barrier_semaphore()
    for d in range(1, peers_n):
        pl.semaphore_signal(barrier, inc=1, device_id={"tensor": peers.at(d)})
    for d in range(1, half):
        pl.semaphore_signal(barrier, inc=1, device_id={"q": r.after(d)})
    signals = peers_n + half - 2

    @pl.when(r.stays)
    def _():
        pl.semaphore_wait(barrier, signals)

    @pl.when(jnp.logical_not(r.stays))
    def _():
        pl.semaphore_signal(barrier, inc=1, device_id={"section": r.l, "stage": r.s})
        pl.semaphore_wait(barrier, signals + 1)

    def whole(i):
        return i < count - come

    def part(i, q):
        return totals[i].at[r.at(0, q, outs[i].shape[0])]

    def load_away(i):
        return pltpu.make_async_copy(aways[i - count + come], got[i], away_sems.at[i - count + come])

    def along(i, d):
        return pltpu.make_async_remote_copy(
            src_ref=part(i, r.after(d)),
            dst_ref=got[i].at[d - 1],
            send_sem=z_sems.at[0, i, d - 1],
            recv_sem=z_sems.at[1, i, d - 1],
            device_id={"q": r.after(d)},
        )

    def load(i):
        return pltpu.make_async_copy(part(i, r.q), mine[i], load_sems.at[i])

    def home(src, dst, sems):
        return pltpu.make_async_remote_copy(
            src_ref=src,
            dst_ref=dst,
            send_sem=sems.at[0],
            recv_sem=sems.at[1],
            device_id={"section": r.l, "stage": r.s},
        )

    def swap(i):
        return home(mine[i], outs[i], swap_sems.at[i])

    def place(j):
        return home(rows_in[j], held.at[j], place_sems.at[j])

    def shared(j, d, src):
        return pltpu.make_async_remote_copy(
            src_ref=src,
            dst_ref=full[j].at[:, peers.me],
            send_sem=share_sems.at[0, j, d - 1],
            recv_sem=share_sems.at[1, j, d - 1],
            device_id={"tensor": peers.at(d)},
        )

    def keep(j, src):
        return pltpu.make_async_copy(src, full[j].at[:, peers.me], keep_sems.at[j])

    def small_along(d):
        return pltpu.make_async_remote_copy(
            src_ref=small.at[r.after(d)],
            dst_ref=small_got.at[d - 1],
            send_sem=small_sems.at[0, d],
            recv_sem=small_sems.at[1, d],
            device_id={"q": r.after(d)},
        )

    def pool(n, d, src, dst):
        return pltpu.make_async_remote_copy(
            src_ref=src,
            dst_ref=dst,
            send_sem=pool_sems.at[0, n, d - 1],
            recv_sem=pool_sems.at[1, n, d - 1],
            device_id={"tensor": peers.at(d)},
        )

    for d in range(1, half):
        small_along(d).start()
    order = sorted(range(count), key=whole)
    ahead = [i for i in order if whole(i)]

    def begin(n):
        if n < len(ahead):
            for d in range(1, half):
                along(ahead[n], d).start()

    for n in range(WINDOW):
        begin(n)
    for i in order:
        load(i).start()
        if not whole(i):
            load_away(i).start()

    def show(j, src):
        keep(j, src).start()
        for d in range(1, peers_n):
            shared(j, d, src).start()

    @pl.when(r.stays)
    def _():
        for j in range(places):
            show(j, rows_in[j])

    @pl.when(jnp.logical_not(r.stays))
    def _():
        show(0, rows_in[0])
        for j in range(1, places):
            place(j).start()

    for i in order:
        load(i).wait()
        if whole(i):
            for d in range(1, half):
                along(i, d).wait_recv()
            begin(ahead.index(i) + WINDOW)
        else:
            load_away(i).wait()

        @pl.loop(0, outs[i].shape[0] // STRIP)
        def _(n):
            strip = pl.ds(pl.multiple_of(n * STRIP, STRIP), STRIP)
            total = mine[i][strip, :].astype(f32)
            for d in range(1, half):
                total = total + got[i][d - 1, strip, :].astype(f32)
            mine[i][strip, :] = total.astype(bf16)

        @pl.when(r.stays)
        def _():
            @pl.loop(0, outs[i].shape[0] // STRIP)
            def _(n):
                strip = pl.ds(pl.multiple_of(n * STRIP, STRIP), STRIP)
                outs[i][strip, :] = mine[i][strip, :]

        @pl.when(jnp.logical_not(r.stays))
        def _():
            swap(i).start()

    total = small[r.q]
    for d in range(1, half):
        small_along(d).wait()
        total = total + small_got[d - 1]
    small_mine[...] = total

    @pl.when(r.stays)
    def _():
        small_own[...] = total

    @pl.when(jnp.logical_not(r.stays))
    def _():
        home(small_mine, small_own, small_sems.at[:, 0]).start()
        for j in range(1, places):
            place(j).wait_recv()
            show(j, held.at[j])
        home(small_mine, small_own, small_sems.at[:, 0]).wait()
        for i in range(count):
            swap(i).wait()
        for j in range(1, places):
            place(j).wait_send()

    down_send[...] = outs[0][:, lanes]
    for d in range(1, peers_n):
        pool(0, d, small_own, small_land.at[d - 1]).start()
        pool(1, d, down_send, down_land.at[d - 1]).start()
    total = small_own[...]
    pooled = down_send[...].astype(f32)
    for d in range(1, peers_n):
        pool(0, d, small_own, small_land.at[d - 1]).wait()
        pool(1, d, down_send, down_land.at[d - 1]).wait()
        total = total + small_land[d - 1]
        pooled = pooled + down_land[d - 1].astype(f32)
    small_sum[...] = total
    down[...] = pooled
    for i in range(count):
        if whole(i):
            for d in range(1, half):
                along(i, d).wait_send()
    for j in range(places):
        keep(j, rows_in[j]).wait()
        for d in range(1, peers_n):
            shared(j, d, rows_in[j]).wait()


def finish(half, peers, ident, totals, aways, rows_in, small, lanes):
    count, come, places = len(totals), len(aways), len(rows_in)
    high = totals[0].shape[0] // half
    micro, rows, width = rows_in[0].shape
    wide = lanes.stop - lanes.start
    anywhere = pl.BlockSpec(memory_space=pl.ANY)
    vmem = pl.BlockSpec(memory_space=pltpu.VMEM)
    tile = small.shape[1:]
    return pl.pallas_call(
        partial(finish_kernel, half, count, come, places, lanes),
        out_shape=[shape((high, a.shape[1]), bf16) for a in totals]
        + [shape((micro, peers, rows, width), bf16)] * places
        + [shape((high, wide), f32), shape(tile, f32), shape(tile, f32)],
        in_specs=[anywhere] * (count + come) + [vmem] * (places + 1),
        out_specs=[vmem] * count + [anywhere] * places + [vmem] * 3,
        scratch_shapes=[pltpu.VMEM((high, a.shape[1]), bf16) for a in totals]
        + [pltpu.VMEM((half - 1, high, a.shape[1]), bf16) for a in totals]
        + [
            pltpu.VMEM(tile, f32),
            pltpu.VMEM((half - 1,) + tile, f32),
            pltpu.VMEM((peers - 1,) + tile, f32),
            pltpu.VMEM((high, wide), bf16),
            pltpu.VMEM((peers - 1, high, wide), bf16),
            pltpu.VMEM((places, micro, rows, width), bf16),
            pltpu.SemaphoreType.DMA((count, 2)),
            pltpu.SemaphoreType.DMA((2, count, half - 1)),
            pltpu.SemaphoreType.DMA((count,)),
            pltpu.SemaphoreType.DMA((max(come, 1),)),
            pltpu.SemaphoreType.DMA((places, 2)),
            pltpu.SemaphoreType.DMA((places,)),
            pltpu.SemaphoreType.DMA((2, places, peers - 1)),
            pltpu.SemaphoreType.DMA((2, half)),
            pltpu.SemaphoreType.DMA((2, 2, peers - 1)),
        ],
        compiler_params=pltpu.CompilerParams(
            collective_id=ident, has_side_effects=True, vmem_limit_bytes=48 * 1024 * 1024
        ),
    )(*totals, *aways, *rows_in, small)


def swapped(array):
    moved = swap_moved(array)
    stays = lax.axis_index("section") == lax.axis_index("stage")
    return jnp.where(stays, array, moved)


def swap_moved(array):
    return lax.ppermute(array, ("section", "stage"), [(1, 2), (2, 1)])


def exchanged(array, axis):
    return lax.ppermute(array, axis, [(0, 1), (1, 0)])


def core_sum(left, right):
    high = left.shape[1] // 2
    section = lax.axis_index("section")

    def rows_for(who):
        return dot_left(lax.dynamic_slice_in_dim(left, who * high, high, 1), right)

    theirs = exchanged(rows_for(1 - section).astype(bf16), "section")
    return (rows_for(section) + theirs.astype(f32)).astype(bf16)


def tiles_of(array, lead, low):
    width = -(-array.shape[1] // (low * LANES)) * LANES
    array = jnp.pad(array, ((0, 0), (0, low * width - array.shape[1])))
    return array.reshape(lead, low, width)


def shards(
    inputs,
    cotangent,
    query_proj,
    key_proj,
    value_proj,
    outgate_proj,
    output_proj,
    decay_down,
    decay_up,
    decay_bias,
    head_gain,
    mixer_gain,
    feed_gain,
    feed_gate,
    feed_up,
    feed_down,
):
    micro, length, width = inputs.shape
    peers = lax.axis_size("tensor")
    half = lax.axis_size("q")
    ranges = 2 * half
    stage = lax.axis_index("stage")
    me = lax.axis_index("tensor")
    rows = length // peers
    rank = decay_down.shape[2]
    cuts = Cuts(query_proj.shape[2], value_proj.shape[2], rank)
    sizes = (ranges, half, cuts)

    def own_rows(array):
        return swapped(lax.dynamic_slice_in_dim(array, me * rows, rows, 1))

    own_in = own_rows(inputs)
    small = [decay_up[0], decay_bias[0], head_gain[0], mixer_gain[0], feed_gain[0]]
    counts = [a.size for a in small]
    ends = [sum(counts[:n]) for n in range(len(counts) + 1)]
    small = tiles_of(jnp.concatenate([a.reshape(1, -1) for a in small], axis=1), 1, 16)[0]
    lanes = cuts.width - cuts.begin
    cat = jnp.concatenate(
        [query_proj[0], key_proj[0], value_proj[0], outgate_proj[0], decay_down[0]], axis=1
    )
    cat = jnp.pad(cat, ((0, 0), (0, cuts.width - cat.shape[1])))
    packed, cat, output = gather_weights(half, 11, small, cat, output_proj[0])
    packed = packed.reshape(ranges, -1).astype(f32)
    up_w, bias_w, head_w, mixer_w, feed_w = (
        packed[:, ends[n] : ends[n + 1]] for n in range(len(counts))
    )
    w = dict(
        up=jnp.pad(up_w.reshape(-1, rank).T, ((0, lanes - rank), (0, 0))),
        bias=bias_w.reshape(1, -1),
        head_gain=head_w.reshape(1, -1),
        mixer_gain=mixer_w.reshape(1, -1),
        feed_gain=feed_w.reshape(1, -1),
    )
    w["cat"], w["output"] = cat, output
    homes = [feed_gate[0], feed_up[0], feed_down[0]]
    own_cot = own_rows(cotangent)

    calls = Rows(rows, width, peers)
    kept, ys = [], []
    h = jnp.where(stage == 0, own_in[0], jnp.zeros_like(own_in[0]))
    normed, gate = calls.first(h, w["mixer_gain"], gather_start(half, homes[0]))
    for step in range(micro + 1):
        cat_v = dot_plain(normed, w["cat"])
        inner, cumul, logits, states, *upper = mixer_forward(
            ranges, half, cuts, cat_v, w["up"], w["bias"],
            **(dict(ident=14, extra=gather_start(half, homes[1])) if step == 0 else {}),
        )
        gated = head_output(inner, cat_v[:, cuts.og], w["head_gain"]).astype(bf16)
        middle, feed_in, *lower = calls.forward_mid(
            dot_right(gated, w["output"]), h, w["feed_gain"],
            **(dict(ident=15, extra=gather_start(half, homes[2])) if step == 0 else {}),
        )
        if step == 0:
            w["gate"], w["upper"], w["lower"] = gather_end(half, 12, gate, *upper, *lower)
        gate_v = dot_plain(feed_in, w["gate"])
        upper_v = dot_plain(feed_in, w["upper"])
        hidden = (jax.nn.silu(gate_v) * upper_v).astype(bf16)
        kept.append(
            dict(
                h=h, normed=normed, cat=cat_v, inner=inner, gated=gated, cumul=cumul,
                logits=logits, states=states, middle=middle, feed_in=feed_in, gate_v=gate_v,
                upper_v=upper_v, hidden=hidden,
            )
        )
        part = dot_right(hidden, w["lower"])
        if step < micro:
            y, h, normed = calls.forward_end(
                part, middle, w["mixer_gain"], own_in[min(step + 1, micro - 1)]
            )
        else:
            gy = jnp.where(stage == 1, own_cot[micro - 1], jnp.zeros_like(own_cot[0]))
            y, d_feed = calls.forward_last(part, middle, gy)
        ys.append(y)

    grads, saved = [], []

    def picked(zero, one):
        return jnp.where(stage == 0, zero, one)

    def rows_of(name):
        items = [item[name] for item in (kept if name in kept[0] else saved[::-1])]
        return jnp.concatenate([picked(items[m], items[m + 1]) for m in range(micro)])

    def with_away(total, away):
        place, high = lax.axis_index("q"), total.shape[0] // half
        own = lax.dynamic_slice_in_dim(total, place * high, high, 0)
        return (own.astype(f32) + jnp.sum(away.astype(f32), axis=0)).astype(bf16)

    worked = picked(jnp.stack(ys[:micro]), jnp.stack(ys[1:]))

    for step in range(micro + 1):
        now = kept[micro - step]
        d_hidden = dot_plain(d_feed, w["lower"])
        sig = jax.nn.sigmoid(now["gate_v"])
        d_gate = (
            d_hidden * now["upper_v"] * (sig * (1.0 + now["gate_v"] * (1.0 - sig)))
        ).astype(bf16)
        d_upper = (d_hidden * (now["gate_v"] * sig)).astype(bf16)
        part = dot_right(d_gate, w["gate"]) + dot_right(d_upper, w["upper"])
        saved.append(dict(d_feed=d_feed, d_gate=d_gate, d_upper=d_upper))
        if step == micro:
            feed_in = rows_of("feed_in")
            feed_totals = [
                core_sum(feed_in, rows_of("d_gate")),
                core_sum(feed_in, rows_of("d_upper")),
                core_sum(rows_of("d_feed"), rows_of("hidden")),
            ]
            feed_totals, part = lax.optimization_barrier((feed_totals, part))
        last = step == micro
        d_middle, feed_part, d_mixed, *away_0 = calls.backward_mid(
            part, gy, now["middle"], w["feed_gain"],
            **(dict(ident=16, extra=along_start(half, feed_totals[0])) if last else {}),
        )
        if last:
            gate_sum = with_away(feed_totals[0], away_0[0])
        d_gated = dot_plain(d_mixed, w["output"])
        d_cat, head_part, up_part, bias_part, *away_1 = mixer_backward(
            ranges, half, cuts, d_gated, now["inner"], now["cat"], w["up"], w["head_gain"],
            now["cumul"], now["logits"], now["states"],
            **(dict(ident=17, extra=along_start(half, feed_totals[1], gate_sum)) if last else {}),
        )
        part = dot_right(d_cat, w["cat"])
        saved[-1].update(d_mixed=d_mixed, d_cat=d_cat)
        if step < micro:
            later = micro - 2 - step
            own = own_cot[later] if later >= 0 else jnp.zeros_like(own_cot[0])
            grad, mixer_part, gy, d_feed, *more = calls.backward_end(
                part, d_middle, now["h"], w["mixer_gain"], own,
                **(dict(ident=18, extra=home_start(half, worked)) if step == 0 else {}),
            )
            if step == 0:
                outputs_in = jnp.where(lax.axis_index("section") == stage, worked, more[0])
        else:
            upper_sum = with_away(feed_totals[1], away_1[0])
            grad, mixer_part, *away_2 = calls.backward_last(
                part, d_middle, now["h"], w["mixer_gain"],
                along_start(half, feed_totals[2], upper_sum),
            )
        grads.append(grad)
        saved[-1].update(
            head=head_part, mixer=mixer_part, feed=feed_part, up=up_part, bias=bias_part
        )

    def sum_of(name):
        return sum(item[name] for item in saved)

    totals = [
        core_sum(rows_of("normed"), rows_of("d_cat")),
        core_sum(rows_of("d_mixed"), rows_of("gated")),
    ] + feed_totals[2:]
    small_grads = [
        sum_of("up")[:rank].T,
        sum_of("bias"),
        sum_of("head"),
        sum_of("mixer"),
        sum_of("feed"),
    ]
    small_grads = tiles_of(
        jnp.concatenate([g.reshape(ranges, -1) for g in small_grads], axis=1), ranges, 8
    )
    section = lax.axis_index("section")
    theirs = exchanged(
        lax.dynamic_slice_in_dim(small_grads, (1 - section) * half, half, 0), "section"
    )
    small_grads = lax.dynamic_slice_in_dim(small_grads, section * half, half, 0) + theirs

    places = [outputs_in, picked(jnp.stack(grads[:0:-1]), jnp.stack(grads[micro - 1 :: -1]))]
    cat_grad, output_grad, lower_grad, outputs, input_grads, down, own, pooled = finish(
        half, peers, 13, totals, away_2[:1], places, small_grads, cuts.rank
    )
    stays = section == stage
    gate_grad = jnp.where(stays, gate_sum, away_1[1]).astype(f32)
    upper_grad = jnp.where(stays, upper_sum, away_2[1]).astype(f32)
    cat_grad, output_grad, lower_grad, input_grads = (
        g.astype(f32) for g in (cat_grad, output_grad, lower_grad, input_grads)
    )
    own, pooled = own.reshape(-1), pooled.reshape(-1)

    def piece(n, like):
        return (own if n < 2 else pooled)[ends[n] : ends[n + 1]].reshape(like.shape)

    return (
        outputs.reshape(1, micro, length, width),
        input_grads.reshape(1, micro, length, width),
        cat_grad[None, :, cuts.q],
        cat_grad[None, :, cuts.k],
        cat_grad[None, :, cuts.v],
        cat_grad[None, :, cuts.og],
        output_grad[None],
        down[None, :, :rank],
        piece(0, decay_up),
        piece(1, decay_bias),
        piece(2, head_gain),
        piece(3, mixer_gain),
        piece(4, feed_gain),
        gate_grad[None],
        upper_grad[None],
        lower_grad[None],
    )


def solution(mesh):
    sections, ranges, peers = (mesh.shape[a] for a in ("section", "seq", "tensor"))
    staged = Mesh(
        mesh.devices.reshape(sections, 2, ranges // 2, peers), ("section", "stage", "q", "tensor")
    )
    seq = ("stage", "q")
    whole = P("section", seq, "tensor")
    row = P("section", seq)
    rows = P("section", None, seq, None)
    tokens = P(None, seq, None)
    narrow = P("section", seq, None)
    return jax.shard_map(
        shards,
        mesh=staged,
        in_specs=(tokens, tokens)
        + (whole,) * 5
        + (narrow, whole, whole, row, row, row)
        + (whole,) * 3,
        out_specs=(rows, rows) + (whole,) * 5 + (narrow, whole, whole, row, row, row) + (whole,) * 3,
        check_vma=False,
    )
```

```python
from functools import partial

import jax
import jax.numpy as jnp
from jax import lax
from jax.experimental import pallas as pl
from jax.experimental.pallas import tpu as pltpu
from jax.sharding import Mesh
from jax.sharding import PartitionSpec as P

SPAN = 64
LANES = 128
STRIP = 64
CHUNKS = 2
ORDER = (1, 0)
DIRECT, SUMMED, PASSED = 0, 1, 2
WINDOW = 2

HIGH = lax.Precision.HIGHEST
MODEL_EPS = 1e-06
HEAD_EPS = 1e-05
GATE_SCALE = 16.0

f32 = jnp.float32
bf16 = jnp.bfloat16
GROUP = ("section", "q")


def dot_plain(left, right):
    return jnp.dot(left, right, preferred_element_type=f32)


def dot_left(left, right):
    return lax.dot_general(left, right, (((0,), (0,)), ((), ())), preferred_element_type=f32)


def dot_right(left, right):
    return lax.dot_general(left, right, (((1,), (1,)), ((), ())), preferred_element_type=f32)


def head_output(inner, out_gate, gain):
    r = lax.rsqrt(jnp.mean(inner * inner, axis=-1, keepdims=True) + HEAD_EPS)
    return gain * inner * r * jax.nn.silu(out_gate)


def normed_rows(u, gain):
    return gain * u * lax.rsqrt(jnp.mean(u * u, axis=-1, keepdims=True) + MODEL_EPS)


def norm_back(d, u, gain):
    s = lax.rsqrt(jnp.mean(u * u, axis=-1, keepdims=True) + MODEL_EPS)
    w = gain * d
    d_u = s * w - u * (s * s * s) * jnp.mean(w * u, axis=-1, keepdims=True)
    return d_u, jnp.sum(d * u * s, axis=0, keepdims=True)


def greet(signals, waits, extra=None):
    if extra is not None:
        signals, waits = {**extra.signals, **signals}, {**extra.waits, **waits}
    barrier = pltpu.get_barrier_semaphore()
    for condition, device in signals.values():
        if condition is None:
            pl.semaphore_signal(barrier, inc=1, device_id=device)
        else:

            @pl.when(condition)
            def _():
                pl.semaphore_signal(barrier, inc=1, device_id=device)

    due = sum(1 for condition in waits.values() if condition is None)
    for condition in waits.values():
        if condition is not None:
            due = due + condition.astype(jnp.int32)
    pl.semaphore_wait(barrier, due)


class Peers:
    def __init__(self, peers):
        assert peers == 4, peers
        self.peers = peers
        self.me = lax.axis_index("tensor")
        low, high = lax.rem(self.me, 2), self.me // 2
        self.beside = (high * 2 + 1 - low, (1 - high) * 2 + low)
        self.opposite = 3 - self.me

    def at(self, d):
        return lax.rem(self.me + d, self.peers)

    def enter(self, relay_to=None, extra=None):
        signals = {("tensor", d): (None, {"tensor": self.at(d)}) for d in range(1, self.peers)}
        waits = dict.fromkeys(signals)
        if relay_to is not None:
            stage = lax.axis_index("stage")
            signals["stage"] = (stage == relay_to, {"stage": 1 - relay_to})
            waits["stage"] = stage != relay_to
        greet(signals, waits, extra)


class Sum:
    def __init__(self, peers, part, send, land, sems, fine=None, fine_sems=None):
        self.peers, self.part, self.send, self.land, self.sems = peers, part, send, land, sems
        self.fine, self.fine_sems = fine, fine_sems
        self.pieces = part.shape[2] // LANES
        self.step = part.shape[1] // CHUNKS

    def rows(self, c):
        return slice(c * self.step, (c + 1) * self.step)

    def copy(self, kind, c):
        target = self.peers.beside[1 - c if kind == SUMMED else c]
        return pltpu.make_async_remote_copy(
            src_ref=self.send.at[kind, c],
            dst_ref=self.land.at[kind, c],
            send_sem=self.sems.at[0, kind, c],
            recv_sem=self.sems.at[1, kind, c],
            device_id={"tensor": target},
        )

    def fine_copy(self, d):
        return pltpu.make_async_remote_copy(
            src_ref=self.fine.at[0],
            dst_ref=self.fine.at[d],
            send_sem=self.fine_sems.at[0, d - 1],
            recv_sem=self.fine_sems.at[1, d - 1],
            device_id={"tensor": 0},
        )

    def lanes(self, n):
        return slice(n * LANES, (n + 1) * LANES)

    def start(self):
        peers = self.peers
        for c in ORDER:
            self.send[PASSED, c] = self.part[peers.opposite, self.rows(c), :].astype(bf16)
            self.copy(PASSED, c).start()
        for c in ORDER:
            self.send[DIRECT, c] = self.part[peers.beside[c], self.rows(c), :].astype(bf16)
            self.copy(DIRECT, c).start()
        if self.fine is not None:
            for n in range(self.pieces):
                self.fine[0, n : n + 1, :] = self.part[0, 0:1, self.lanes(n)]
            for d in range(1, peers.peers):

                @pl.when(peers.at(d) == 0)
                def _():
                    self.fine_copy(d).start()

        for c in ORDER:
            self.copy(PASSED, c).wait_recv()
            own = self.part[peers.beside[1 - c], self.rows(c), :].astype(f32)
            self.send[SUMMED, c] = (own + self.land[PASSED, c].astype(f32)).astype(bf16)
            self.copy(SUMMED, c).start()

    def finish(self, c, total):
        self.copy(DIRECT, c).wait_recv()
        acc = self.part[self.peers.me, self.rows(c), :].astype(f32)
        acc = acc + self.land[DIRECT, c].astype(f32)
        self.copy(SUMMED, c).wait_recv()
        total[self.rows(c), :] = acc + self.land[SUMMED, c].astype(f32)
        if c == 0 and self.fine is not None:

            @pl.when(self.peers.me == 0)
            def _():
                top = self.fine[0]
                for d in range(1, self.peers.peers):
                    self.fine_copy(d).wait_recv()
                    top = top + self.fine[d]
                for n in range(self.pieces):
                    total[0:1, self.lanes(n)] = top[n : n + 1, :]

        return total[self.rows(c), :]

    def drain(self):
        for c in ORDER:
            for kind in (PASSED, DIRECT, SUMMED):
                self.copy(kind, c).wait_send()
        if self.fine is not None:
            for d in range(1, self.peers.peers):

                @pl.when(self.peers.at(d) == 0)
                def _():
                    self.fine_copy(d).wait_send()


class Share:
    def __init__(self, peers, full, sems):
        self.peers, self.full, self.sems = peers, full, sems
        self.step = full.shape[1] // CHUNKS

    def copy(self, kind, c):
        peers = self.peers
        if kind == PASSED:
            source, target = peers.beside[c], peers.beside[1 - c]
        else:
            source, target = peers.me, peers.beside[kind]
        block = self.full.at[source, pl.ds(c * self.step, self.step)]
        return pltpu.make_async_remote_copy(
            src_ref=block,
            dst_ref=block,
            send_sem=self.sems.at[0, kind, c],
            recv_sem=self.sems.at[1, kind, c],
            device_id={"tensor": target},
        )

    def start(self, c, value):
        self.full[self.peers.me, c * self.step : (c + 1) * self.step, :] = value
        for kind in range(2):
            self.copy(kind, c).start()

    def finish(self):
        for c in ORDER:
            self.copy(c, c).wait_recv()
            self.copy(PASSED, c).start()
        for c in ORDER:
            self.copy(1 - c, c).wait_recv()
            self.copy(PASSED, c).wait_recv()
            for kind in range(3):
                self.copy(kind, c).wait_send()


def relay_rows(src, land, sems, c, relay_to):
    step = src.shape[0] // CHUNKS
    rows = pl.ds(c * step, step)
    return pltpu.make_async_remote_copy(
        src_ref=src.at[rows],
        dst_ref=land.at[rows],
        send_sem=sems.at[0, c],
        recv_sem=sems.at[1, c],
        device_id={"stage": relay_to},
    )


def first_kernel(peers_n, h, gain, full, share_sems, extra=None):
    peers = Peers(peers_n)
    peers.enter(extra=extra)
    if extra is not None:
        extra.start()
    share = Share(peers, full, share_sems)
    for c in ORDER:
        rows = slice(c * share.step, (c + 1) * share.step)
        share.start(c, normed_rows(h[rows, :].astype(f32), gain[...]).astype(bf16))
    share.finish()
    if extra is not None:
        extra.finish()


def forward_mid_kernel(
    peers_n, part, h, gain, middle, full, send, land, fine, total, sems, fine_sems, share_sems, extra=None):
    peers = Peers(peers_n)
    peers.enter(extra=extra)
    if extra is not None:
        extra.start()
    reduced = Sum(peers, part, send, land, sems, fine, fine_sems)
    share = Share(peers, full, share_sems)
    reduced.start()
    for c in ORDER:
        rows = reduced.rows(c)
        value = h[rows, :].astype(f32) + reduced.finish(c, total)
        middle[rows, :] = value
        share.start(c, normed_rows(value, gain[...]).astype(bf16))
    share.finish()
    reduced.drain()
    if extra is not None:
        extra.finish()


def forward_end_kernel(
    peers_n,
    part,
    middle,
    gain,
    own,
    y,
    h,
    full,
    send,
    land,
    fine,
    total,
    relayed,
    sems,
    fine_sems,
    share_sems,
    relay_sems,
):
    peers = Peers(peers_n)
    stage = lax.axis_index("stage")
    peers.enter(1)
    reduced = Sum(peers, part, send, land, sems, fine, fine_sems)
    share = Share(peers, full, share_sems)
    reduced.start()
    for c in ORDER:
        rows = reduced.rows(c)
        relay = relay_rows(y, relayed, relay_sems, c, 1)

        @pl.when(stage == 0)
        def _():
            y[rows, :] = (middle[rows, :] + reduced.finish(c, total)).astype(bf16)
            relay.start()
            h[rows, :] = own[rows, :]

        @pl.when(stage == 1)
        def _():
            y[rows, :] = (middle[rows, :] + reduced.finish(c, total)).astype(bf16)
            relay.wait_recv()
            h[rows, :] = relayed[rows, :]

        share.start(c, normed_rows(h[rows, :].astype(f32), gain[...]).astype(bf16))

    share.finish()

    @pl.when(stage == 0)
    def _():
        for c in ORDER:
            relay_rows(y, relayed, relay_sems, c, 1).wait_send()
    reduced.drain()


def forward_last_kernel(
    peers_n, part, middle, gy, y, full, send, land, fine, total, sems, fine_sems, share_sems
):
    peers = Peers(peers_n)
    peers.enter()
    reduced = Sum(peers, part, send, land, sems, fine, fine_sems)
    share = Share(peers, full, share_sems)
    reduced.start()
    for c in ORDER:
        share.start(c, gy[reduced.rows(c), :])
    for c in ORDER:
        rows = reduced.rows(c)
        y[rows, :] = (middle[rows, :] + reduced.finish(c, total)).astype(bf16)
    share.finish()
    reduced.drain()


def backward_mid_kernel(
    peers_n, part, gy, middle, gain, d_middle, gain_part, full, send, land, total, sems, share_sems, extra=None):
    peers = Peers(peers_n)
    peers.enter(extra=extra)
    if extra is not None:
        extra.start()
    reduced = Sum(peers, part, send, land, sems)
    share = Share(peers, full, share_sems)
    reduced.start()
    gains = jnp.zeros(gain_part.shape, f32)
    for c in ORDER:
        rows = reduced.rows(c)
        d_u, g = norm_back(reduced.finish(c, total), middle[rows, :], gain[...])
        value = gy[rows, :].astype(f32) + d_u
        d_middle[rows, :] = value
        gains = gains + g
        share.start(c, value.astype(bf16))
    gain_part[...] = gains
    share.finish()
    reduced.drain()
    if extra is not None:
        extra.finish()


def backward_end_kernel(
    peers_n,
    part,
    d_middle,
    h,
    gain,
    own,
    grad,
    gain_part,
    gy,
    full,
    send,
    land,
    total,
    relayed,
    sems,
    share_sems,
    relay_sems,
):
    peers = Peers(peers_n)
    stage = lax.axis_index("stage")
    peers.enter(0)
    reduced = Sum(peers, part, send, land, sems)
    share = Share(peers, full, share_sems)
    reduced.start()
    gain_part[...] = jnp.zeros(gain_part.shape, f32)

    def finish(c):
        rows = reduced.rows(c)
        d_u, g = norm_back(reduced.finish(c, total), h[rows, :].astype(f32), gain[...])
        grad[rows, :] = (d_middle[rows, :] + d_u).astype(bf16)
        gain_part[...] += g

    for c in ORDER:
        rows = reduced.rows(c)
        relay = relay_rows(grad, relayed, relay_sems, c, 0)

        @pl.when(stage == 1)
        def _():
            finish(c)
            relay.start()
            gy[rows, :] = own[rows, :]

        @pl.when(stage == 0)
        def _():
            finish(c)
            relay.wait_recv()
            gy[rows, :] = relayed[rows, :]

        share.start(c, gy[rows, :])

    share.finish()

    @pl.when(stage == 1)
    def _():
        for c in ORDER:
            relay_rows(grad, relayed, relay_sems, c, 0).wait_send()
    reduced.drain()


def backward_last_kernel(
    peers_n, part, d_middle, h, gain, grad, gain_part, send, land, total, sems, extra=None):
    peers = Peers(peers_n)
    peers.enter(extra=extra)
    if extra is not None:
        extra.start()
    reduced = Sum(peers, part, send, land, sems)
    reduced.start()
    gains = jnp.zeros(gain_part.shape, f32)
    for c in ORDER:
        rows = reduced.rows(c)
        d_u, g = norm_back(reduced.finish(c, total), h[rows, :].astype(f32), gain[...])
        grad[rows, :] = (d_middle[rows, :] + d_u).astype(bf16)
        gains = gains + g
    gain_part[...] = gains
    reduced.drain()
    if extra is not None:
        extra.finish()


def in_vmem(count):
    return [pl.BlockSpec(memory_space=pltpu.VMEM)] * count


def kernel_call(body, outs, scratch, ident, *args, extra=None):
    outs = outs if isinstance(outs, list) else [outs]
    in_specs, out_specs = in_vmem(len(args)), in_vmem(len(outs))
    if extra is not None:
        kind, more_args, more_outs, more_scratch = extra
        sizes = [len(args), len(more_args), len(outs), len(more_outs), len(scratch)]
        own_body = body

        def body(*refs):
            cuts = [sum(sizes[:n]) for n in range(len(sizes) + 1)]
            parts = [refs[cuts[n] : cuts[n + 1]] for n in range(len(sizes))] + [refs[cuts[-1] :]]
            own_body(
                *parts[0], *parts[2], *parts[4], extra=kind(*parts[1], *parts[3], *parts[5])
            )

        anywhere = pl.BlockSpec(memory_space=pl.ANY)
        args, outs = args + tuple(more_args), outs + more_outs
        scratch = scratch + more_scratch
        in_specs = in_specs + [anywhere] * len(more_args)
        out_specs = out_specs + [anywhere] * len(more_outs)
    results = pl.pallas_call(
        body,
        out_shape=outs,
        in_specs=in_specs,
        out_specs=out_specs,
        scratch_shapes=scratch,
        compiler_params=pltpu.CompilerParams(
            collective_id=ident, has_side_effects=True, vmem_limit_bytes=40 * 1024 * 1024
        ),
    )(*args)
    return results[0] if len(results) == 1 else list(results)


def shape(dims, kind):
    return jax.ShapeDtypeStruct(dims, kind)


class Rows:
    def __init__(self, rows, width, peers):
        self.rows, self.width, self.peers = rows, width, peers
        self.slice_b = shape((rows, width), bf16)
        self.slice_f = shape((rows, width), f32)
        self.gain_f = shape((1, width), f32)
        self.full = shape((peers, rows, width), bf16)
        self.pair = pltpu.SemaphoreType.DMA((2, peers - 1))
        self.many = pltpu.SemaphoreType.DMA((2, 3, CHUNKS))
        self.reduce = [
            pltpu.VMEM((3, CHUNKS, rows // CHUNKS, width), bf16),
            pltpu.VMEM((3, CHUNKS, rows // CHUNKS, width), bf16),
        ]
        self.fine = [pltpu.VMEM((peers, width // LANES, LANES), f32)]
        self.total = [pltpu.VMEM((rows, width), f32)]
        self.relayed = [pltpu.VMEM((rows, width), bf16)]
        self.relay = pltpu.SemaphoreType.DMA((2, CHUNKS))

    def parts(self, part):
        return part.reshape(self.peers, self.rows, self.width)

    def flat(self, full):
        return full.reshape(self.peers * self.rows, self.width)

    def first(self, h, gain, extra):
        body = partial(first_kernel, self.peers)
        full, *more = kernel_call(body, self.full, [self.many], 1, h, gain, extra=extra)
        return self.flat(full), *more

    def forward_mid(self, part, h, gain, ident=3, extra=None):
        middle, full, *more = kernel_call(
            partial(forward_mid_kernel, self.peers),
            [self.slice_f, self.full],
            self.reduce + self.fine + self.total + [self.many, self.pair, self.many],
            ident,
            self.parts(part),
            h,
            gain,
            extra=extra,
        )
        return middle, self.flat(full), *more

    def forward_end(self, part, middle, gain, own):
        y, h, full = kernel_call(
            partial(forward_end_kernel, self.peers),
            [self.slice_b, self.slice_b, self.full],
            self.reduce
            + self.fine
            + self.total
            + self.relayed
            + [self.many, self.pair, self.many, self.relay],
            4,
            self.parts(part),
            middle,
            gain,
            own,
        )
        return y, h, self.flat(full)

    def forward_last(self, part, middle, gy):
        y, full = kernel_call(
            partial(forward_last_kernel, self.peers),
            [self.slice_b, self.full],
            self.reduce + self.fine + self.total + [self.many, self.pair, self.many],
            5,
            self.parts(part),
            middle,
            gy,
        )
        return y, self.flat(full)

    def backward_mid(self, part, gy, middle, gain, ident=6, extra=None):
        d_middle, gain_part, full, *more = kernel_call(
            partial(backward_mid_kernel, self.peers),
            [self.slice_f, self.gain_f, self.full],
            self.reduce + self.total + [self.many] * 2,
            ident,
            self.parts(part),
            gy,
            middle,
            gain,
            extra=extra,
        )
        return d_middle, gain_part, self.flat(full), *more

    def backward_end(self, part, d_middle, h, gain, own):
        grad, gain_part, gy, full = kernel_call(
            partial(backward_end_kernel, self.peers),
            [self.slice_b, self.gain_f, self.slice_b, self.full],
            self.reduce + self.total + self.relayed + [self.many] * 2 + [self.relay],
            7,
            self.parts(part),
            d_middle,
            h,
            gain,
            own,
        )
        return grad, gain_part, gy, self.flat(full)

    def backward_last(self, part, d_middle, h, gain, extra=None):
        return kernel_call(
            partial(backward_last_kernel, self.peers),
            [self.slice_b, self.gain_f],
            self.reduce + self.total + [self.many],
            8,
            self.parts(part),
            d_middle,
            h,
            gain,
            extra=extra,
        )


PAD = 16


class Chain:
    def __init__(self, ranges, half):
        self.ranges, self.half = ranges, half
        self.s, self.q = lax.axis_index("section"), lax.axis_index("q")
        self.me = self.s * half + self.q

    def after(self, d):
        return lax.rem(self.q + d, self.half)

    def before(self, d):
        return self.s * self.half + lax.rem(self.q + self.half - d, self.half)

    def enter(self, extra=None):
        signals = {("q", d): (None, {"q": self.after(d)}) for d in range(1, self.half)}
        signals["core"] = (None, {"section": 1 - self.s})
        greet(signals, dict.fromkeys(signals), extra)

    def along(self, land, sems, d):
        return pltpu.make_async_remote_copy(
            src_ref=land.at[self.me],
            dst_ref=land.at[self.me],
            send_sem=sems.at[0, d],
            recv_sem=sems.at[1, d],
            device_id={"q": self.after(d)},
        )

    def across(self, land, sems, d):
        return pltpu.make_async_remote_copy(
            src_ref=land.at[self.before(d)],
            dst_ref=land.at[self.before(d)],
            send_sem=sems.at[2, d],
            recv_sem=sems.at[3, d],
            device_id={"section": 1 - self.s},
        )

    def start(self, land, sems, state, through):
        high = state.shape[0]
        land[self.me, 0:high, :] = state.astype(bf16)
        land[self.me, high : high + PAD, :] = jnp.broadcast_to(
            through, (PAD, through.shape[1])
        ).astype(bf16)
        for d in range(1, self.half):
            self.along(land, sems, d).start()
        self.across(land, sems, 0).start()

    def forward(self, land, sems):
        for d in range(1, self.half):
            self.along(land, sems, d).wait_recv()
            self.across(land, sems, d).start()

    def finish(self, land, sems, high, later):
        for d in range(1, self.half):
            self.along(land, sems, d).wait_send()
        for d in range(self.half):
            self.across(land, sems, d).wait()

        def step(n, state):
            place = self.ranges - 1 - n if later else n
            taken = (place > self.me) if later else (place < self.me)
            through = land[place, high : high + PAD, :].astype(f32)[0:1, :]
            joined = through * state + land[place, 0:high, :].astype(f32)
            return jnp.where(taken, joined, state)

        zero = jnp.zeros((high, land.shape[2]), f32)
        state = zero
        for n in range(self.ranges):
            state = step(n, state)
        return state


def triangle(size):
    row = lax.broadcasted_iota(jnp.int32, (size, size), 0)
    col = lax.broadcasted_iota(jnp.int32, (size, size), 1)
    return row, col


def scores_of(q, k, c, fine):
    row, col = triangle(SPAN)
    middle = c[SPAN // 2 : SPAN // 2 + 1, :]
    up, down = jnp.exp(c - middle), jnp.exp(middle - c)
    a, b = q * up, k * down
    own = jnp.sum(q * k, axis=1, keepdims=True)
    if fine:
        scores = lax.dot_general(
            a, b, (((1,), (1,)), ((), ())), precision=HIGH, preferred_element_type=f32
        )
    a, b = a.astype(bf16), b.astype(bf16)
    if not fine:
        scores = dot_right(a, b)
    return jnp.where(row > col, scores, 0.0).astype(bf16), own, a, b, up, down


class Cuts:
    def __init__(self, key_dim, value_dim, rank):
        self.key, self.value = key_dim, value_dim
        self.q = slice(0, key_dim)
        self.k = slice(key_dim, 2 * key_dim)
        self.v = slice(2 * key_dim, 2 * key_dim + value_dim)
        self.og = slice(2 * key_dim + value_dim, 2 * key_dim + 2 * value_dim)
        self.begin = 2 * key_dim + 2 * value_dim
        self.width = self.begin + LANES * (-(-rank // LANES))
        self.rank = slice(self.begin, self.width)


def rounded(array):
    return array.astype(bf16).astype(f32)


def log_sigmoid(u):
    return jnp.minimum(u, 0.0) - jnp.log1p(jnp.exp(-jnp.abs(u)))


def mixer_forward_kernel(
    ranges, half, cuts, cat, up, bias, inner_ref, c_ref, l_ref, s_ref,
    moved, out, land, sems, extra=None,
):
    chain = Chain(ranges, half)
    chain.enter(extra)
    length = cat.shape[0]
    spans = length // SPAN
    scale = cuts.key ** (-0.5)
    row, col = triangle(SPAN)
    lower = (row >= col).astype(f32)
    state = jnp.zeros((cuts.value, cuts.key), f32)
    reach = jnp.zeros((1, cuts.key), f32)
    for i in range(spans):
        rows = slice(i * SPAN, (i + 1) * SPAN)
        logits = (
            jnp.dot(cat[rows, cuts.rank], up[...], precision=HIGH, preferred_element_type=f32)
            + bias[...]
        )
        l_ref[rows, :] = logits
        decay = log_sigmoid(logits) * (1.0 / GATE_SCALE)
        c = jnp.dot(lower, decay, precision=HIGH, preferred_element_type=f32)
        c_ref[rows, :] = c
        last = c[SPAN - 1 : SPAN, :]
        fading = (rounded(cat[rows, cuts.k]) * jnp.exp(last - c)).astype(bf16)
        step = dot_left(cat[rows, cuts.v].astype(bf16), fading)
        moved[i] = step
        state = jnp.exp(last) * state + step
        reach = reach + last
    chain.start(land, sems, state, jnp.exp(reach))
    if extra is not None:
        extra.start()
    for i in range(spans):
        rows = slice(i * SPAN, (i + 1) * SPAN)
        q = rounded(cat[rows, cuts.q]) * scale
        k = rounded(cat[rows, cuts.k])
        scores, own, *_ = scores_of(q, k, c_ref[rows, :], True)
        v = cat[rows, cuts.v].astype(bf16)
        out[rows, :] = dot_plain(scores, v) + own * v.astype(f32)
    chain.forward(land, sems)
    state = chain.finish(land, sems, cuts.value, False)
    for i in range(spans):
        rows = slice(i * SPAN, (i + 1) * SPAN)
        c = c_ref[rows, :]
        held = state.astype(bf16)
        s_ref[i] = held
        q = (rounded(cat[rows, cuts.q]) * scale * jnp.exp(c)).astype(bf16)
        inner_ref[rows, :] = out[rows, :] + dot_right(q, held)
        state = jnp.exp(c[SPAN - 1 : SPAN, :]) * state + moved[i]
    s_ref[spans] = state.astype(bf16)
    if extra is not None:
        extra.finish()


def mixer_backward_kernel(
    ranges, half, cuts, dgated_ref, inner_ref, cat, up, hg_ref, c_ref, l_ref, s_ref,
    dcat, hgp_ref, dup_ref, dbias_ref, pulled, o_ref, dqs, dks, dvs, land, sems, extra=None,
):
    chain = Chain(ranges, half)
    chain.enter(extra)
    length = cat.shape[0]
    spans = length // SPAN
    scale = cuts.key ** (-0.5)
    row, col = triangle(SPAN)
    upper = (row <= col).astype(f32)
    state = jnp.zeros((cuts.value, cuts.key), f32)
    reach = jnp.zeros((1, cuts.key), f32)
    hg = hg_ref[...]
    head_part = jnp.zeros((1, cuts.value), f32)
    for i in reversed(range(spans)):
        rows = slice(i * SPAN, (i + 1) * SPAN)
        inner, og, dgated = inner_ref[rows, :], cat[rows, cuts.og], dgated_ref[rows, :]
        r = lax.rsqrt(jnp.mean(inner * inner, axis=-1, keepdims=True) + HEAD_EPS)
        sg = 1.0 / (1.0 + jnp.exp(-og))
        d_norm = dgated * (og * sg)
        unit = inner * r
        head_part = head_part + jnp.sum(d_norm * unit, axis=0, keepdims=True)
        w = d_norm * hg
        d_inner = r * w - inner * (r * r * r) * jnp.mean(w * inner, axis=-1, keepdims=True)
        dog = dgated * unit * hg * (sg * (1.0 + og * (1.0 - sg)))
        dcat[rows, cuts.og] = dog.astype(bf16)
        o_ref[rows, :] = d_inner
        o = d_inner.astype(bf16)
        c = c_ref[rows, :]
        q = (rounded(cat[rows, cuts.q]) * scale * jnp.exp(c)).astype(bf16)
        step = dot_left(o, q)
        pulled[i] = step
        last = c[SPAN - 1 : SPAN, :]
        state = jnp.exp(last) * state + step
        reach = reach + last
    hgp_ref[...] = head_part
    chain.start(land, sems, state, jnp.exp(reach))
    if extra is not None:
        extra.start()
    for i in range(spans):
        rows = slice(i * SPAN, (i + 1) * SPAN)
        q = rounded(cat[rows, cuts.q]) * scale
        k = rounded(cat[rows, cuts.k])
        scores, own, a, b, gain_up, gain_down = scores_of(q, k, c_ref[rows, :], False)
        d_inner, v = o_ref[rows, :], cat[rows, cuts.v].astype(bf16)
        o = d_inner.astype(bf16)
        d_own = jnp.sum(d_inner * v.astype(f32), axis=1, keepdims=True)
        d_scores = jnp.where(row > col, dot_right(o, v), 0.0).astype(bf16)
        dvs[rows, :] = dot_left(scores, o) + own * d_inner
        dqs[rows, :] = (
            d_own * k
            + gain_up * dot_plain(d_scores, b)
            + jnp.exp(c_ref[rows, :]) * dot_plain(o, s_ref[i])
        )
        dks[rows, :] = d_own * q + gain_down * dot_left(d_scores, a)
    chain.forward(land, sems)
    state = chain.finish(land, sems, cuts.value, True)
    d_up = jnp.zeros(dup_ref.shape, f32)
    d_bias = jnp.zeros(dbias_ref.shape, f32)
    for i in reversed(range(spans)):
        rows = slice(i * SPAN, (i + 1) * SPAN)
        c = c_ref[rows, :]
        last = c[SPAN - 1 : SPAN, :]
        fade = jnp.exp(last - c)
        held = state.astype(bf16)
        k = rounded(cat[rows, cuts.k])
        dk = dks[rows, :] + fade * dot_plain(cat[rows, cuts.v].astype(bf16), held)
        dv = dvs[rows, :] + dot_right((k * fade).astype(bf16), held)
        dq = dqs[rows, :]
        dcat[rows, cuts.q] = (dq * scale).astype(bf16)
        dcat[rows, cuts.k] = dk.astype(bf16)
        dcat[rows, cuts.v] = dv.astype(bf16)
        ended = jnp.sum(state * s_ref[i + 1].astype(f32), axis=0, keepdims=True)
        terms = rounded(cat[rows, cuts.q]) * scale * dq - k * dk
        d_decay = jnp.dot(upper, terms, precision=HIGH, preferred_element_type=f32) + ended
        d_logits = d_decay * (1.0 / (1.0 + jnp.exp(l_ref[rows, :]))) * (1.0 / GATE_SCALE)
        d_bias = d_bias + jnp.sum(d_logits, axis=0, keepdims=True)
        d_up = d_up + lax.dot_general(
            cat[rows, cuts.rank], d_logits, (((0,), (0,)), ((), ())),
            precision=HIGH, preferred_element_type=f32,
        )
        d_rank = lax.dot_general(
            d_logits, up[...], (((1,), (1,)), ((), ())),
            precision=HIGH, preferred_element_type=f32,
        )
        dcat[rows, cuts.rank] = d_rank.astype(bf16)
        state = jnp.exp(last) * state + pulled[i]
    dup_ref[...] = d_up
    dbias_ref[...] = d_bias
    if extra is not None:
        extra.finish()


def mixer_forward(ranges, half, cuts, cat, up, bias, ident=9, extra=None):
    length = cat.shape[0]
    spans = length // SPAN
    return kernel_call(
        partial(mixer_forward_kernel, ranges, half, cuts),
        [
            shape((length, cuts.value), f32),
            shape((length, cuts.key), f32),
            shape((length, cuts.key), f32),
            shape((spans + 1, cuts.value, cuts.key), bf16),
        ],
        [
            pltpu.VMEM((spans, cuts.value, cuts.key), f32),
            pltpu.VMEM((length, cuts.value), f32),
            pltpu.VMEM((ranges, cuts.value + PAD, cuts.key), bf16),
            pltpu.SemaphoreType.DMA((4, half)),
        ],
        ident,
        cat, up, bias,
        extra=extra,
    )


def mixer_backward(
    ranges, half, cuts, dgated, inner, cat, up, hg, c, logits, s, ident=10, extra=None
):
    length = cat.shape[0]
    spans = length // SPAN
    return kernel_call(
        partial(mixer_backward_kernel, ranges, half, cuts),
        [
            shape((length, cuts.width), bf16),
            shape((1, cuts.value), f32),
            shape(up.shape, f32),
            shape((1, cuts.key), f32),
        ],
        [
            pltpu.VMEM((spans, cuts.value, cuts.key), f32),
            pltpu.VMEM((length, cuts.value), f32),
            pltpu.VMEM((length, cuts.key), f32),
            pltpu.VMEM((length, cuts.key), f32),
            pltpu.VMEM((length, cuts.value), f32),
            pltpu.VMEM((ranges, cuts.value + PAD, cuts.key), bf16),
            pltpu.SemaphoreType.DMA((4, half)),
        ],
        ident,
        dgated, inner, cat, up, hg, c, logits, s,
        extra=extra,
    )


class Ranges:
    def __init__(self, half):
        self.half = half
        self.s, self.l = lax.axis_index("section"), lax.axis_index("stage")
        self.q = lax.axis_index("q")
        self.stays = self.s == self.l

    def enter(self, cores):
        barrier = pltpu.get_barrier_semaphore()
        for d in range(1, self.half):
            pl.semaphore_signal(barrier, inc=1, device_id={"q": self.after(d)})
        count = self.half - 1
        if cores:
            pl.semaphore_signal(barrier, inc=1, device_id={"section": 1 - self.s})
            count = count + 1

        @pl.when(self.stays)
        def _():
            pl.semaphore_wait(barrier, count)

        @pl.when(jnp.logical_not(self.stays))
        def _():
            pl.semaphore_signal(barrier, inc=1, device_id={"section": self.l, "stage": self.s})
            pl.semaphore_wait(barrier, count + 1)

    def after(self, d):
        return lax.rem(self.q + d, self.half)

    def before(self, d):
        return lax.rem(self.q + self.half - d, self.half)

    def at(self, section, q, rows):
        return pl.ds(pl.multiple_of((section * self.half + q) * rows, rows), rows)


def gather_kernel(half, count, *refs):
    ins, outs, bounce = refs[:count], refs[count : 2 * count], refs[2 * count : 3 * count]
    swap_sems, z_sems, core_sems, keep_sems = refs[3 * count :]
    r = Ranges(half)
    r.enter(True)

    def held(i):
        rows = ins[i].shape[0]
        return outs[i].at[r.at(r.s, r.q, rows)]

    def swap(i):
        rows = ins[i].shape[0]
        return pltpu.make_async_remote_copy(
            src_ref=ins[i],
            dst_ref=outs[i].at[r.at(r.l, r.q, rows)],
            send_sem=swap_sems.at[0, i],
            recv_sem=swap_sems.at[1, i],
            device_id={"section": r.l, "stage": r.s},
        )

    def along(i, d, src):
        return pltpu.make_async_remote_copy(
            src_ref=src,
            dst_ref=held(i),
            send_sem=z_sems.at[0, i, d - 1],
            recv_sem=z_sems.at[1, i, d - 1],
            device_id={"q": r.after(d)},
        )

    def across(i, d, src):
        rows = ins[i].shape[0]
        return pltpu.make_async_remote_copy(
            src_ref=src,
            dst_ref=outs[i].at[r.at(r.s, r.before(d), rows)],
            send_sem=core_sems.at[0, i, d],
            recv_sem=core_sems.at[1, i, d],
            device_id={"section": 1 - r.s},
        )

    def load(i):
        return pltpu.make_async_copy(ins[i], bounce[i], keep_sems.at[0, i])

    def keep(i):
        return pltpu.make_async_copy(bounce[i], held(i), keep_sems.at[1, i])

    @pl.when(r.stays)
    def _():
        for i in range(count):
            for d in range(1, half):
                along(i, d, ins[i]).start()
            across(i, 0, ins[i]).start()
            load(i).start()
        for i in range(count):
            load(i).wait()
            keep(i).start()

    @pl.when(jnp.logical_not(r.stays))
    def _():
        for i in range(count):
            swap(i).start()

    for i in range(count):
        rows = ins[i].shape[0]

        @pl.when(jnp.logical_not(r.stays))
        def _():
            swap(i).wait_recv()
            for d in range(1, half):
                along(i, d, held(i)).start()
            across(i, 0, held(i)).start()

        for d in range(1, half):
            along(i, d, ins[i]).wait_recv()
            across(i, d, outs[i].at[r.at(r.s, r.before(d), rows)]).start()

    for i in range(count):

        @pl.when(r.stays)
        def _():
            keep(i).wait()

        @pl.when(jnp.logical_not(r.stays))
        def _():
            swap(i).wait_send()

        for d in range(1, half):
            along(i, d, ins[i]).wait_send()
        for d in range(half):
            across(i, d, ins[i]).wait()


def gather_weights(half, ident, *shards_in):
    count = len(shards_in)
    anywhere = pl.BlockSpec(memory_space=pl.ANY)
    return pl.pallas_call(
        partial(gather_kernel, half, count),
        out_shape=[shape((2 * half * a.shape[0], a.shape[1]), a.dtype) for a in shards_in],
        in_specs=[anywhere] * count,
        out_specs=[anywhere] * count,
        scratch_shapes=[pltpu.VMEM(a.shape, a.dtype) for a in shards_in]
        + [
            pltpu.SemaphoreType.DMA((2, count)),
            pltpu.SemaphoreType.DMA((2, count, half - 1)),
            pltpu.SemaphoreType.DMA((2, count, half)),
            pltpu.SemaphoreType.DMA((2, count)),
        ],
        compiler_params=pltpu.CompilerParams(
            collective_id=ident, has_side_effects=True, vmem_limit_bytes=40 * 1024 * 1024
        ),
    )(*shards_in)


class GatherStart:
    def __init__(self, half, home, whole, bounce, swap_sems, z_sems, core_sems, keep_sems):
        r = self.r = Ranges(half)
        rows = home.shape[0]
        self.half = half
        moves = jnp.logical_not(r.stays)
        self.signals = {("q", d): (None, {"q": r.after(d)}) for d in range(1, half)}
        self.signals["core"] = (None, {"section": 1 - r.s})
        self.signals["swap"] = (moves, {"section": r.l, "stage": r.s})
        self.waits = {name: condition for name, (condition, _) in self.signals.items()}
        held = whole.at[r.at(r.s, r.q, rows)]
        self.swap = pltpu.make_async_remote_copy(
            src_ref=home,
            dst_ref=whole.at[r.at(r.l, r.q, rows)],
            send_sem=swap_sems.at[0],
            recv_sem=swap_sems.at[1],
            device_id={"section": r.l, "stage": r.s},
        )
        self.along = [
            pltpu.make_async_remote_copy(
                src_ref=home,
                dst_ref=held,
                send_sem=z_sems.at[0, d - 1],
                recv_sem=z_sems.at[1, d - 1],
                device_id={"q": r.after(d)},
            )
            for d in range(1, half)
        ]
        self.across = pltpu.make_async_remote_copy(
            src_ref=home,
            dst_ref=held,
            send_sem=core_sems.at[0],
            recv_sem=core_sems.at[1],
            device_id={"section": 1 - r.s},
        )
        self.load = pltpu.make_async_copy(home, bounce, keep_sems.at[0])
        self.keep = pltpu.make_async_copy(bounce, held, keep_sems.at[1])

    def start(self):
        @pl.when(self.r.stays)
        def _():
            for copy in self.along:
                copy.start()
            self.across.start()
            self.load.start()

        @pl.when(jnp.logical_not(self.r.stays))
        def _():
            self.swap.start()

    def finish(self):
        @pl.when(self.r.stays)
        def _():
            self.load.wait()
            self.keep.start()
            for copy in self.along:
                copy.wait()
            self.across.wait_send()
            self.keep.wait()

        @pl.when(jnp.logical_not(self.r.stays))
        def _():
            self.swap.wait()
            self.across.wait_recv()


def gather_start(half, home):
    return (
        partial(GatherStart, half),
        [home],
        [shape((2 * half * home.shape[0], home.shape[1]), home.dtype)],
        [
            pltpu.VMEM(home.shape, home.dtype),
            pltpu.SemaphoreType.DMA((2,)),
            pltpu.SemaphoreType.DMA((2, half - 1)),
            pltpu.SemaphoreType.DMA((2,)),
            pltpu.SemaphoreType.DMA((2,)),
        ],
    )


def gather_end_kernel(half, count, rows, *refs):
    outs = refs[count : 2 * count]
    z_sems, core_sems = refs[2 * count :]
    r = Ranges(half)
    r.enter(True)

    def piece(i, q):
        return outs[i].at[r.at(r.s, q, rows)]

    def along(i, d):
        return pltpu.make_async_remote_copy(
            src_ref=piece(i, r.q),
            dst_ref=piece(i, r.q),
            send_sem=z_sems.at[0, i, d - 1],
            recv_sem=z_sems.at[1, i, d - 1],
            device_id={"q": r.after(d)},
        )

    def across(i, d):
        return pltpu.make_async_remote_copy(
            src_ref=piece(i, r.before(d)),
            dst_ref=piece(i, r.before(d)),
            send_sem=core_sems.at[0, i, d],
            recv_sem=core_sems.at[1, i, d],
            device_id={"section": 1 - r.s},
        )

    @pl.when(r.stays)
    def _():
        for i in range(count):
            for d in range(1, half):
                across(i, d).start()
        for i in range(count):
            for d in range(1, half):
                across(i, d).wait()
            across(i, 0).wait_recv()

    @pl.when(jnp.logical_not(r.stays))
    def _():
        for i in range(count):
            for d in range(1, half):
                along(i, d).start()
        for i in range(count):
            across(i, 0).start()
        for i in range(count):
            for d in range(1, half):
                along(i, d).wait_recv()
                across(i, d).start()
        for i in range(count):
            for d in range(1, half):
                along(i, d).wait_send()
                across(i, d).wait()
            across(i, 0).wait_send()


def gather_end(half, ident, *begun):
    count = len(begun)
    rows = begun[0].shape[0] // (2 * half)
    anywhere = pl.BlockSpec(memory_space=pl.ANY)
    return pl.pallas_call(
        partial(gather_end_kernel, half, count, rows),
        out_shape=[shape(a.shape, a.dtype) for a in begun],
        in_specs=[anywhere] * count,
        out_specs=[anywhere] * count,
        scratch_shapes=[
            pltpu.SemaphoreType.DMA((2, count, half - 1)),
            pltpu.SemaphoreType.DMA((2, count, half)),
        ],
        input_output_aliases={i: i for i in range(count)},
        compiler_params=pltpu.CompilerParams(collective_id=ident, has_side_effects=True),
    )(*begun)


class AlongStart:
    def __init__(self, half, rows, *refs):
        r = self.r = Ranges(half)
        self.signals = {("q", d): (None, {"q": r.after(d)}) for d in range(1, half)}
        self.swap = None
        if len(refs) == 3:
            total, away, sems = refs
        else:
            total, summed, away, landed, sems, swap_sems = refs
            self.moves = jnp.logical_not(r.stays)
            self.signals["swap"] = (self.moves, {"section": r.l, "stage": r.s})
            self.swap = pltpu.make_async_remote_copy(
                src_ref=summed,
                dst_ref=landed,
                send_sem=swap_sems.at[0],
                recv_sem=swap_sems.at[1],
                device_id={"section": r.l, "stage": r.s},
            )
        self.waits = {name: condition for name, (condition, _) in self.signals.items()}
        self.copies = [
            pltpu.make_async_remote_copy(
                src_ref=total.at[r.at(0, r.after(d), rows)],
                dst_ref=away.at[d - 1],
                send_sem=sems.at[0, d - 1],
                recv_sem=sems.at[1, d - 1],
                device_id={"q": r.after(d)},
            )
            for d in range(1, half)
        ]

    def start(self):
        for copy in self.copies:
            copy.start()
        if self.swap is not None:

            @pl.when(self.moves)
            def _():
                self.swap.start()

    def finish(self):
        for copy in self.copies:
            copy.wait()
        if self.swap is not None:

            @pl.when(self.moves)
            def _():
                self.swap.wait()


def along_start(half, total, summed=None):
    rows = total.shape[0] // half
    away = shape((half - 1, rows, total.shape[1]), total.dtype)
    sems = pltpu.SemaphoreType.DMA((2, half - 1))
    kind = partial(AlongStart, half, rows)
    if summed is None:
        return kind, [total], [away], [sems]
    landed = shape(summed.shape, summed.dtype)
    return kind, [total, summed], [away, landed], [sems, pltpu.SemaphoreType.DMA((2,))]


class HomeStart:
    def __init__(self, half, src, landed, sems):
        r = Ranges(half)
        self.moves = jnp.logical_not(r.stays)
        self.signals = {"swap": (self.moves, {"section": r.l, "stage": r.s})}
        self.waits = {"swap": self.moves}
        self.copy = pltpu.make_async_remote_copy(
            src_ref=src,
            dst_ref=landed,
            send_sem=sems.at[0],
            recv_sem=sems.at[1],
            device_id={"section": r.l, "stage": r.s},
        )

    def start(self):
        @pl.when(self.moves)
        def _():
            self.copy.start()

    def finish(self):
        @pl.when(self.moves)
        def _():
            self.copy.wait()


def home_start(half, array):
    sems = [pltpu.SemaphoreType.DMA((2,))]
    return partial(HomeStart, half), [array], [shape(array.shape, array.dtype)], sems


def finish_kernel(half, count, come, places, lanes, *refs):
    totals, aways = refs[:count], refs[count : count + come]
    refs = refs[count + come :]
    rows_in, small = refs[:places], refs[places]
    refs = refs[places + 1 :]
    outs, full, down, small_own, small_sum = (
        refs[:count],
        refs[count : count + places],
        refs[count + places],
        refs[count + places + 1],
        refs[count + places + 2],
    )
    refs = refs[count + places + 3 :]
    mine, got = refs[:count], refs[count : 2 * count]
    small_mine, small_got, small_land, down_send, down_land, held = refs[
        2 * count : 2 * count + 6
    ]
    (
        swap_sems, z_sems, load_sems, away_sems, place_sems, keep_sems, share_sems, small_sems,
        pool_sems,
    ) = refs[2 * count + 6 :]
    peers_n = full[0].shape[1]
    r = Ranges(half)
    peers = Peers(peers_n)
    barrier = pltpu.get_barrier_semaphore()
    for d in range(1, peers_n):
        pl.semaphore_signal(barrier, inc=1, device_id={"tensor": peers.at(d)})
    for d in range(1, half):
        pl.semaphore_signal(barrier, inc=1, device_id={"q": r.after(d)})
    signals = peers_n + half - 2

    @pl.when(r.stays)
    def _():
        pl.semaphore_wait(barrier, signals)

    @pl.when(jnp.logical_not(r.stays))
    def _():
        pl.semaphore_signal(barrier, inc=1, device_id={"section": r.l, "stage": r.s})
        pl.semaphore_wait(barrier, signals + 1)

    def whole(i):
        return i < count - come

    def part(i, q):
        return totals[i].at[r.at(0, q, outs[i].shape[0])]

    def load_away(i):
        return pltpu.make_async_copy(aways[i - count + come], got[i], away_sems.at[i - count + come])

    def along(i, d):
        return pltpu.make_async_remote_copy(
            src_ref=part(i, r.after(d)),
            dst_ref=got[i].at[d - 1],
            send_sem=z_sems.at[0, i, d - 1],
            recv_sem=z_sems.at[1, i, d - 1],
            device_id={"q": r.after(d)},
        )

    def load(i):
        return pltpu.make_async_copy(part(i, r.q), mine[i], load_sems.at[i])

    def home(src, dst, sems):
        return pltpu.make_async_remote_copy(
            src_ref=src,
            dst_ref=dst,
            send_sem=sems.at[0],
            recv_sem=sems.at[1],
            device_id={"section": r.l, "stage": r.s},
        )

    def swap(i):
        return home(mine[i], outs[i], swap_sems.at[i])

    def place(j):
        return home(rows_in[j], held.at[j], place_sems.at[j])

    def shared(j, d, src):
        return pltpu.make_async_remote_copy(
            src_ref=src,
            dst_ref=full[j].at[:, peers.me],
            send_sem=share_sems.at[0, j, d - 1],
            recv_sem=share_sems.at[1, j, d - 1],
            device_id={"tensor": peers.at(d)},
        )

    def keep(j, src):
        return pltpu.make_async_copy(src, full[j].at[:, peers.me], keep_sems.at[j])

    def small_along(d):
        return pltpu.make_async_remote_copy(
            src_ref=small.at[r.after(d)],
            dst_ref=small_got.at[d - 1],
            send_sem=small_sems.at[0, d],
            recv_sem=small_sems.at[1, d],
            device_id={"q": r.after(d)},
        )

    def pool(n, d, src, dst):
        return pltpu.make_async_remote_copy(
            src_ref=src,
            dst_ref=dst,
            send_sem=pool_sems.at[0, n, d - 1],
            recv_sem=pool_sems.at[1, n, d - 1],
            device_id={"tensor": peers.at(d)},
        )

    for d in range(1, half):
        small_along(d).start()
    order = sorted(range(count), key=whole)
    ahead = [i for i in order if whole(i)]

    def begin(n):
        if n < len(ahead):
            for d in range(1, half):
                along(ahead[n], d).start()

    for n in range(WINDOW):
        begin(n)
    for i in order:
        load(i).start()
        if not whole(i):
            load_away(i).start()

    def show(j, src):
        keep(j, src).start()
        for d in range(1, peers_n):
            shared(j, d, src).start()

    @pl.when(r.stays)
    def _():
        for j in range(places):
            show(j, rows_in[j])

    @pl.when(jnp.logical_not(r.stays))
    def _():
        show(0, rows_in[0])
        for j in range(1, places):
            place(j).start()

    for i in order:
        load(i).wait()
        if whole(i):
            for d in range(1, half):
                along(i, d).wait_recv()
            begin(ahead.index(i) + WINDOW)
        else:
            load_away(i).wait()

        @pl.loop(0, outs[i].shape[0] // STRIP)
        def _(n):
            strip = pl.ds(pl.multiple_of(n * STRIP, STRIP), STRIP)
            total = mine[i][strip, :].astype(f32)
            for d in range(1, half):
                total = total + got[i][d - 1, strip, :].astype(f32)
            mine[i][strip, :] = total.astype(bf16)

        @pl.when(r.stays)
        def _():
            @pl.loop(0, outs[i].shape[0] // STRIP)
            def _(n):
                strip = pl.ds(pl.multiple_of(n * STRIP, STRIP), STRIP)
                outs[i][strip, :] = mine[i][strip, :]

        @pl.when(jnp.logical_not(r.stays))
        def _():
            swap(i).start()

    total = small[r.q]
    for d in range(1, half):
        small_along(d).wait()
        total = total + small_got[d - 1]
    small_mine[...] = total

    @pl.when(r.stays)
    def _():
        small_own[...] = total

    @pl.when(jnp.logical_not(r.stays))
    def _():
        home(small_mine, small_own, small_sems.at[:, 0]).start()
        for j in range(1, places):
            place(j).wait_recv()
            show(j, held.at[j])
        home(small_mine, small_own, small_sems.at[:, 0]).wait()
        for i in range(count):
            swap(i).wait()
        for j in range(1, places):
            place(j).wait_send()

    down_send[...] = outs[0][:, lanes]
    for d in range(1, peers_n):
        pool(0, d, small_own, small_land.at[d - 1]).start()
        pool(1, d, down_send, down_land.at[d - 1]).start()
    total = small_own[...]
    pooled = down_send[...].astype(f32)
    for d in range(1, peers_n):
        pool(0, d, small_own, small_land.at[d - 1]).wait()
        pool(1, d, down_send, down_land.at[d - 1]).wait()
        total = total + small_land[d - 1]
        pooled = pooled + down_land[d - 1].astype(f32)
    small_sum[...] = total
    down[...] = pooled
    for i in range(count):
        if whole(i):
            for d in range(1, half):
                along(i, d).wait_send()
    for j in range(places):
        keep(j, rows_in[j]).wait()
        for d in range(1, peers_n):
            shared(j, d, rows_in[j]).wait()


def finish(half, peers, ident, totals, aways, rows_in, small, lanes):
    count, come, places = len(totals), len(aways), len(rows_in)
    high = totals[0].shape[0] // half
    micro, rows, width = rows_in[0].shape
    wide = lanes.stop - lanes.start
    anywhere = pl.BlockSpec(memory_space=pl.ANY)
    vmem = pl.BlockSpec(memory_space=pltpu.VMEM)
    tile = small.shape[1:]
    return pl.pallas_call(
        partial(finish_kernel, half, count, come, places, lanes),
        out_shape=[shape((high, a.shape[1]), bf16) for a in totals]
        + [shape((micro, peers, rows, width), bf16)] * places
        + [shape((high, wide), f32), shape(tile, f32), shape(tile, f32)],
        in_specs=[anywhere] * (count + come) + [vmem] * (places + 1),
        out_specs=[vmem] * count + [anywhere] * places + [vmem] * 3,
        scratch_shapes=[pltpu.VMEM((high, a.shape[1]), bf16) for a in totals]
        + [pltpu.VMEM((half - 1, high, a.shape[1]), bf16) for a in totals]
        + [
            pltpu.VMEM(tile, f32),
            pltpu.VMEM((half - 1,) + tile, f32),
            pltpu.VMEM((peers - 1,) + tile, f32),
            pltpu.VMEM((high, wide), bf16),
            pltpu.VMEM((peers - 1, high, wide), bf16),
            pltpu.VMEM((places, micro, rows, width), bf16),
            pltpu.SemaphoreType.DMA((count, 2)),
            pltpu.SemaphoreType.DMA((2, count, half - 1)),
            pltpu.SemaphoreType.DMA((count,)),
            pltpu.SemaphoreType.DMA((max(come, 1),)),
            pltpu.SemaphoreType.DMA((places, 2)),
            pltpu.SemaphoreType.DMA((places,)),
            pltpu.SemaphoreType.DMA((2, places, peers - 1)),
            pltpu.SemaphoreType.DMA((2, half)),
            pltpu.SemaphoreType.DMA((2, 2, peers - 1)),
        ],
        compiler_params=pltpu.CompilerParams(
            collective_id=ident, has_side_effects=True, vmem_limit_bytes=48 * 1024 * 1024
        ),
    )(*totals, *aways, *rows_in, small)


def swapped(array):
    moved = swap_moved(array)
    stays = lax.axis_index("section") == lax.axis_index("stage")
    return jnp.where(stays, array, moved)


def swap_moved(array):
    return lax.ppermute(array, ("section", "stage"), [(1, 2), (2, 1)])


def exchanged(array, axis):
    return lax.ppermute(array, axis, [(0, 1), (1, 0)])


def core_sum(left, right):
    high = left.shape[1] // 2
    section = lax.axis_index("section")

    def rows_for(who):
        return dot_left(lax.dynamic_slice_in_dim(left, who * high, high, 1), right)

    theirs = exchanged(rows_for(1 - section).astype(bf16), "section")
    return (rows_for(section) + theirs.astype(f32)).astype(bf16)


def range_sum(total):
    if lax.axis_size("q") != 2:
        return lax.psum_scatter(total, "q", scatter_dimension=0, tiled=True)
    place, high = lax.axis_index("q"), total.shape[0] // 2
    away = exchanged(lax.dynamic_slice_in_dim(total, (1 - place) * high, high, 0), "q")
    own = lax.dynamic_slice_in_dim(total, place * high, high, 0)
    return (own.astype(f32) + away.astype(f32)).astype(bf16)


def tiles_of(array, lead, low):
    width = -(-array.shape[1] // (low * LANES)) * LANES
    array = jnp.pad(array, ((0, 0), (0, low * width - array.shape[1])))
    return array.reshape(lead, low, width)


def shards(
    inputs,
    cotangent,
    query_proj,
    key_proj,
    value_proj,
    outgate_proj,
    output_proj,
    decay_down,
    decay_up,
    decay_bias,
    head_gain,
    mixer_gain,
    feed_gain,
    feed_gate,
    feed_up,
    feed_down,
):
    micro, length, width = inputs.shape
    peers = lax.axis_size("tensor")
    half = lax.axis_size("q")
    ranges = 2 * half
    stage = lax.axis_index("stage")
    me = lax.axis_index("tensor")
    rows = length // peers
    rank = decay_down.shape[2]
    cuts = Cuts(query_proj.shape[2], value_proj.shape[2], rank)
    sizes = (ranges, half, cuts)

    def own_rows(array):
        return swapped(lax.dynamic_slice_in_dim(array, me * rows, rows, 1))

    own_in = own_rows(inputs)
    small = [decay_up[0], decay_bias[0], head_gain[0], mixer_gain[0], feed_gain[0]]
    counts = [a.size for a in small]
    ends = [sum(counts[:n]) for n in range(len(counts) + 1)]
    small = tiles_of(jnp.concatenate([a.reshape(1, -1) for a in small], axis=1), 1, 16)[0]
    lanes = cuts.width - cuts.begin
    cat = jnp.concatenate(
        [query_proj[0], key_proj[0], value_proj[0], outgate_proj[0], decay_down[0]], axis=1
    )
    cat = jnp.pad(cat, ((0, 0), (0, cuts.width - cat.shape[1])))
    packed, cat, output = gather_weights(half, 11, small, cat, output_proj[0])
    packed = packed.reshape(ranges, -1).astype(f32)
    up_w, bias_w, head_w, mixer_w, feed_w = (
        packed[:, ends[n] : ends[n + 1]] for n in range(len(counts))
    )
    w = dict(
        up=jnp.pad(up_w.reshape(-1, rank).T, ((0, lanes - rank), (0, 0))),
        bias=bias_w.reshape(1, -1),
        head_gain=head_w.reshape(1, -1),
        mixer_gain=mixer_w.reshape(1, -1),
        feed_gain=feed_w.reshape(1, -1),
    )
    w["cat"], w["output"] = cat, output
    homes = [feed_gate[0], feed_up[0], feed_down[0]]
    own_cot = own_rows(cotangent)

    calls = Rows(rows, width, peers)
    kept, ys = [], []
    h = jnp.where(stage == 0, own_in[0], jnp.zeros_like(own_in[0]))
    normed, gate = calls.first(h, w["mixer_gain"], gather_start(half, homes[0]))
    for step in range(micro + 1):
        cat_v = dot_plain(normed, w["cat"])
        inner, cumul, logits, states, *upper = mixer_forward(
            ranges, half, cuts, cat_v, w["up"], w["bias"],
            **(dict(ident=14, extra=gather_start(half, homes[1])) if step == 0 else {}),
        )
        gated = head_output(inner, cat_v[:, cuts.og], w["head_gain"]).astype(bf16)
        middle, feed_in, *lower = calls.forward_mid(
            dot_right(gated, w["output"]), h, w["feed_gain"],
            **(dict(ident=15, extra=gather_start(half, homes[2])) if step == 0 else {}),
        )
        if step == 0:
            w["gate"], w["upper"], w["lower"] = gather_end(half, 12, gate, *upper, *lower)
        gate_v = dot_plain(feed_in, w["gate"])
        upper_v = dot_plain(feed_in, w["upper"])
        hidden = (jax.nn.silu(gate_v) * upper_v).astype(bf16)
        kept.append(
            dict(
                h=h, normed=normed, cat=cat_v, inner=inner, gated=gated, cumul=cumul,
                logits=logits, states=states, middle=middle, feed_in=feed_in, gate_v=gate_v,
                upper_v=upper_v, hidden=hidden,
            )
        )
        part = dot_right(hidden, w["lower"])
        if step < micro:
            y, h, normed = calls.forward_end(
                part, middle, w["mixer_gain"], own_in[min(step + 1, micro - 1)]
            )
        else:
            gy = jnp.where(stage == 1, own_cot[micro - 1], jnp.zeros_like(own_cot[0]))
            y, d_feed = calls.forward_last(part, middle, gy)
        ys.append(y)

    grads, saved = [], []

    def picked(zero, one):
        return jnp.where(stage == 0, zero, one)

    def rows_of(name):
        items = [item[name] for item in (kept if name in kept[0] else saved[::-1])]
        return jnp.concatenate([picked(items[m], items[m + 1]) for m in range(micro)])

    def with_away(total, away):
        place, high = lax.axis_index("q"), total.shape[0] // half
        own = lax.dynamic_slice_in_dim(total, place * high, high, 0)
        return (own.astype(f32) + jnp.sum(away.astype(f32), axis=0)).astype(bf16)

    worked = picked(jnp.stack(ys[:micro]), jnp.stack(ys[1:]))

    for step in range(micro + 1):
        now = kept[micro - step]
        d_hidden = dot_plain(d_feed, w["lower"])
        sig = jax.nn.sigmoid(now["gate_v"])
        d_gate = (
            d_hidden * now["upper_v"] * (sig * (1.0 + now["gate_v"] * (1.0 - sig)))
        ).astype(bf16)
        d_upper = (d_hidden * (now["gate_v"] * sig)).astype(bf16)
        part = dot_right(d_gate, w["gate"]) + dot_right(d_upper, w["upper"])
        saved.append(dict(d_feed=d_feed, d_gate=d_gate, d_upper=d_upper))
        if step == micro:
            feed_in = rows_of("feed_in")
            gate_total = core_sum(feed_in, rows_of("d_gate"))
            gate_total, feed_in, d_feed_rows = lax.optimization_barrier(
                (gate_total, feed_in, rows_of("d_feed"))
            )
            feed_totals = [
                gate_total,
                core_sum(feed_in, rows_of("d_upper")),
                core_sum(d_feed_rows, rows_of("hidden")),
            ]
            gate_sum = range_sum(feed_totals[0])
            feed_totals, gate_sum, part = lax.optimization_barrier((feed_totals, gate_sum, part))
        last = step == micro
        d_middle, feed_part, d_mixed, *away_0 = calls.backward_mid(
            part, gy, now["middle"], w["feed_gain"],
            **(dict(ident=16, extra=along_start(half, feed_totals[1], gate_sum)) if last else {}),
            **(dict(ident=18, extra=home_start(half, worked)) if step == 1 else {}),
        )
        if step == 1:
            outputs_in = jnp.where(lax.axis_index("section") == stage, worked, away_0[0])
        if last:
            upper_sum = with_away(feed_totals[1], away_0[0])
        d_gated = dot_plain(d_mixed, w["output"])
        d_cat, head_part, up_part, bias_part, *away_1 = mixer_backward(
            ranges, half, cuts, d_gated, now["inner"], now["cat"], w["up"], w["head_gain"],
            now["cumul"], now["logits"], now["states"],
            **(dict(ident=17, extra=along_start(half, feed_totals[2], upper_sum)) if last else {}),
        )
        part = dot_right(d_cat, w["cat"])
        saved[-1].update(d_mixed=d_mixed, d_cat=d_cat)
        if step < micro:
            later = micro - 2 - step
            own = own_cot[later] if later >= 0 else jnp.zeros_like(own_cot[0])
            grad, mixer_part, gy, d_feed = calls.backward_end(
                part, d_middle, now["h"], w["mixer_gain"], own,
            )
        else:
            lower_sum = with_away(feed_totals[2], away_1[0])
            output_total = core_sum(rows_of("d_mixed"), rows_of("gated"))
            grad, mixer_part, *away_2 = calls.backward_last(
                part, d_middle, now["h"], w["mixer_gain"],
                along_start(half, output_total, lower_sum),
            )
        grads.append(grad)
        saved[-1].update(
            head=head_part, mixer=mixer_part, feed=feed_part, up=up_part, bias=bias_part
        )

    def sum_of(name):
        return sum(item[name] for item in saved)

    totals = [
        core_sum(rows_of("normed"), rows_of("d_cat")),
        output_total,
    ]
    small_grads = [
        sum_of("up")[:rank].T,
        sum_of("bias"),
        sum_of("head"),
        sum_of("mixer"),
        sum_of("feed"),
    ]
    small_grads = tiles_of(
        jnp.concatenate([g.reshape(ranges, -1) for g in small_grads], axis=1), ranges, 8
    )
    section = lax.axis_index("section")
    theirs = exchanged(
        lax.dynamic_slice_in_dim(small_grads, (1 - section) * half, half, 0), "section"
    )
    small_grads = lax.dynamic_slice_in_dim(small_grads, section * half, half, 0) + theirs

    places = [outputs_in, picked(jnp.stack(grads[:0:-1]), jnp.stack(grads[micro - 1 :: -1]))]
    cat_grad, output_grad, outputs, input_grads, down, own, pooled = finish(
        half, peers, 13, totals, away_2[:1], places, small_grads, cuts.rank
    )
    stays = section == stage
    gate_grad = jnp.where(stays, gate_sum, away_0[1]).astype(f32)
    upper_grad = jnp.where(stays, upper_sum, away_1[1]).astype(f32)
    lower_grad = jnp.where(stays, lower_sum, away_2[1]).astype(f32)
    cat_grad, output_grad, input_grads = (
        g.astype(f32) for g in (cat_grad, output_grad, input_grads)
    )
    own, pooled = own.reshape(-1), pooled.reshape(-1)

    def piece(n, like):
        return (own if n < 2 else pooled)[ends[n] : ends[n + 1]].reshape(like.shape)

    return (
        outputs.reshape(1, micro, length, width),
        input_grads.reshape(1, micro, length, width),
        cat_grad[None, :, cuts.q],
        cat_grad[None, :, cuts.k],
        cat_grad[None, :, cuts.v],
        cat_grad[None, :, cuts.og],
        output_grad[None],
        down[None, :, :rank],
        piece(0, decay_up),
        piece(1, decay_bias),
        piece(2, head_gain),
        piece(3, mixer_gain),
        piece(4, feed_gain),
        gate_grad[None],
        upper_grad[None],
        lower_grad[None],
    )


def solution(mesh):
    sections, ranges, peers = (mesh.shape[a] for a in ("section", "seq", "tensor"))
    staged = Mesh(
        mesh.devices.reshape(sections, 2, ranges // 2, peers), ("section", "stage", "q", "tensor")
    )
    seq = ("stage", "q")
    whole = P("section", seq, "tensor")
    row = P("section", seq)
    rows = P("section", None, seq, None)
    tokens = P(None, seq, None)
    narrow = P("section", seq, None)
    return jax.shard_map(
        shards,
        mesh=staged,
        in_specs=(tokens, tokens)
        + (whole,) * 5
        + (narrow, whole, whole, row, row, row)
        + (whole,) * 3,
        out_specs=(rows, rows) + (whole,) * 5 + (narrow, whole, whole, row, row, row) + (whole,) * 3,
        check_vma=False,
    )
```

```python
from functools import partial

import jax
import jax.numpy as jnp
from jax import lax
from jax.experimental import pallas as pl
from jax.experimental.pallas import tpu as pltpu
from jax.sharding import Mesh
from jax.sharding import PartitionSpec as P

SPAN = 64
LANES = 128
STRIP = 64
CHUNKS = 2
ORDER = (1, 0)
DIRECT, SUMMED, PASSED = 0, 1, 2
WINDOW = 2

HIGH = lax.Precision.HIGHEST
MODEL_EPS = 1e-06
HEAD_EPS = 1e-05
GATE_SCALE = 16.0

f32 = jnp.float32
bf16 = jnp.bfloat16
GROUP = ("section", "q")


def dot_plain(left, right):
    return jnp.dot(left, right, preferred_element_type=f32)


def dot_left(left, right):
    return lax.dot_general(left, right, (((0,), (0,)), ((), ())), preferred_element_type=f32)


def dot_right(left, right):
    return lax.dot_general(left, right, (((1,), (1,)), ((), ())), preferred_element_type=f32)


def head_output(inner, out_gate, gain):
    r = lax.rsqrt(jnp.mean(inner * inner, axis=-1, keepdims=True) + HEAD_EPS)
    return gain * inner * r * jax.nn.silu(out_gate)


def normed_rows(u, gain):
    return gain * u * lax.rsqrt(jnp.mean(u * u, axis=-1, keepdims=True) + MODEL_EPS)


def norm_back(d, u, gain):
    s = lax.rsqrt(jnp.mean(u * u, axis=-1, keepdims=True) + MODEL_EPS)
    w = gain * d
    d_u = s * w - u * (s * s * s) * jnp.mean(w * u, axis=-1, keepdims=True)
    return d_u, jnp.sum(d * u * s, axis=0, keepdims=True)


def greet(signals, waits, extra=None):
    if extra is not None:
        signals, waits = {**extra.signals, **signals}, {**extra.waits, **waits}
    barrier = pltpu.get_barrier_semaphore()
    for condition, device in signals.values():
        if condition is None:
            pl.semaphore_signal(barrier, inc=1, device_id=device)
        else:

            @pl.when(condition)
            def _():
                pl.semaphore_signal(barrier, inc=1, device_id=device)

    due = sum(1 for condition in waits.values() if condition is None)
    for condition in waits.values():
        if condition is not None:
            due = due + condition.astype(jnp.int32)
    pl.semaphore_wait(barrier, due)


class Peers:
    def __init__(self, peers):
        assert peers == 4, peers
        self.peers = peers
        self.me = lax.axis_index("tensor")
        low, high = lax.rem(self.me, 2), self.me // 2
        self.beside = (high * 2 + 1 - low, (1 - high) * 2 + low)
        self.opposite = 3 - self.me

    def at(self, d):
        return lax.rem(self.me + d, self.peers)

    def enter(self, relay_to=None, extra=None):
        signals = {("tensor", d): (None, {"tensor": self.at(d)}) for d in range(1, self.peers)}
        waits = dict.fromkeys(signals)
        if relay_to is not None:
            stage = lax.axis_index("stage")
            signals["stage"] = (stage == relay_to, {"stage": 1 - relay_to})
            waits["stage"] = stage != relay_to
        greet(signals, waits, extra)


class Sum:
    def __init__(self, peers, part, send, land, sems, fine=None, fine_sems=None):
        self.peers, self.part, self.send, self.land, self.sems = peers, part, send, land, sems
        self.fine, self.fine_sems = fine, fine_sems
        self.pieces = part.shape[2] // LANES
        self.step = part.shape[1] // CHUNKS

    def rows(self, c):
        return slice(c * self.step, (c + 1) * self.step)

    def copy(self, kind, c):
        target = self.peers.beside[1 - c if kind == SUMMED else c]
        return pltpu.make_async_remote_copy(
            src_ref=self.send.at[kind, c],
            dst_ref=self.land.at[kind, c],
            send_sem=self.sems.at[0, kind, c],
            recv_sem=self.sems.at[1, kind, c],
            device_id={"tensor": target},
        )

    def fine_copy(self, d):
        return pltpu.make_async_remote_copy(
            src_ref=self.fine.at[0],
            dst_ref=self.fine.at[d],
            send_sem=self.fine_sems.at[0, d - 1],
            recv_sem=self.fine_sems.at[1, d - 1],
            device_id={"tensor": 0},
        )

    def lanes(self, n):
        return slice(n * LANES, (n + 1) * LANES)

    def start(self):
        peers = self.peers
        for c in ORDER:
            self.send[PASSED, c] = self.part[peers.opposite, self.rows(c), :].astype(bf16)
            self.copy(PASSED, c).start()
        for c in ORDER:
            self.send[DIRECT, c] = self.part[peers.beside[c], self.rows(c), :].astype(bf16)
            self.copy(DIRECT, c).start()
        if self.fine is not None:
            for n in range(self.pieces):
                self.fine[0, n : n + 1, :] = self.part[0, 0:1, self.lanes(n)]
            for d in range(1, peers.peers):

                @pl.when(peers.at(d) == 0)
                def _():
                    self.fine_copy(d).start()

        for c in ORDER:
            self.copy(PASSED, c).wait_recv()
            own = self.part[peers.beside[1 - c], self.rows(c), :].astype(f32)
            self.send[SUMMED, c] = (own + self.land[PASSED, c].astype(f32)).astype(bf16)
            self.copy(SUMMED, c).start()

    def finish(self, c, total):
        self.copy(DIRECT, c).wait_recv()
        acc = self.part[self.peers.me, self.rows(c), :].astype(f32)
        acc = acc + self.land[DIRECT, c].astype(f32)
        self.copy(SUMMED, c).wait_recv()
        total[self.rows(c), :] = acc + self.land[SUMMED, c].astype(f32)
        if c == 0 and self.fine is not None:

            @pl.when(self.peers.me == 0)
            def _():
                top = self.fine[0]
                for d in range(1, self.peers.peers):
                    self.fine_copy(d).wait_recv()
                    top = top + self.fine[d]
                for n in range(self.pieces):
                    total[0:1, self.lanes(n)] = top[n : n + 1, :]

        return total[self.rows(c), :]

    def drain(self):
        for c in ORDER:
            for kind in (PASSED, DIRECT, SUMMED):
                self.copy(kind, c).wait_send()
        if self.fine is not None:
            for d in range(1, self.peers.peers):

                @pl.when(self.peers.at(d) == 0)
                def _():
                    self.fine_copy(d).wait_send()


class Share:
    def __init__(self, peers, full, sems):
        self.peers, self.full, self.sems = peers, full, sems
        self.step = full.shape[1] // CHUNKS

    def copy(self, kind, c):
        peers = self.peers
        if kind == PASSED:
            source, target = peers.beside[c], peers.beside[1 - c]
        else:
            source, target = peers.me, peers.beside[kind]
        block = self.full.at[source, pl.ds(c * self.step, self.step)]
        return pltpu.make_async_remote_copy(
            src_ref=block,
            dst_ref=block,
            send_sem=self.sems.at[0, kind, c],
            recv_sem=self.sems.at[1, kind, c],
            device_id={"tensor": target},
        )

    def start(self, c, value):
        self.full[self.peers.me, c * self.step : (c + 1) * self.step, :] = value
        for kind in range(2):
            self.copy(kind, c).start()

    def finish(self):
        for c in ORDER:
            self.copy(c, c).wait_recv()
            self.copy(PASSED, c).start()
        for c in ORDER:
            self.copy(1 - c, c).wait_recv()
            self.copy(PASSED, c).wait_recv()
            for kind in range(3):
                self.copy(kind, c).wait_send()


def relay_rows(src, land, sems, c, relay_to):
    step = src.shape[0] // CHUNKS
    rows = pl.ds(c * step, step)
    return pltpu.make_async_remote_copy(
        src_ref=src.at[rows],
        dst_ref=land.at[rows],
        send_sem=sems.at[0, c],
        recv_sem=sems.at[1, c],
        device_id={"stage": relay_to},
    )


def first_kernel(peers_n, h, gain, full, share_sems, extra=None):
    peers = Peers(peers_n)
    peers.enter(extra=extra)
    if extra is not None:
        extra.start()
    share = Share(peers, full, share_sems)
    for c in ORDER:
        rows = slice(c * share.step, (c + 1) * share.step)
        share.start(c, normed_rows(h[rows, :].astype(f32), gain[...]).astype(bf16))
    share.finish()
    if extra is not None:
        extra.finish()


def forward_mid_kernel(
    peers_n, part, h, gain, middle, full, send, land, fine, total, sems, fine_sems, share_sems, extra=None):
    peers = Peers(peers_n)
    peers.enter(extra=extra)
    if extra is not None:
        extra.start()
    reduced = Sum(peers, part, send, land, sems, fine, fine_sems)
    share = Share(peers, full, share_sems)
    reduced.start()
    for c in ORDER:
        rows = reduced.rows(c)
        value = h[rows, :].astype(f32) + reduced.finish(c, total)
        middle[rows, :] = value
        share.start(c, normed_rows(value, gain[...]).astype(bf16))
    share.finish()
    reduced.drain()
    if extra is not None:
        extra.finish()


def forward_end_kernel(
    peers_n,
    part,
    middle,
    gain,
    own,
    y,
    h,
    full,
    send,
    land,
    fine,
    total,
    relayed,
    sems,
    fine_sems,
    share_sems,
    relay_sems,
):
    peers = Peers(peers_n)
    stage = lax.axis_index("stage")
    peers.enter(1)
    reduced = Sum(peers, part, send, land, sems, fine, fine_sems)
    share = Share(peers, full, share_sems)
    reduced.start()
    for c in ORDER:
        rows = reduced.rows(c)
        relay = relay_rows(y, relayed, relay_sems, c, 1)

        @pl.when(stage == 0)
        def _():
            y[rows, :] = (middle[rows, :] + reduced.finish(c, total)).astype(bf16)
            relay.start()
            h[rows, :] = own[rows, :]

        @pl.when(stage == 1)
        def _():
            y[rows, :] = (middle[rows, :] + reduced.finish(c, total)).astype(bf16)
            relay.wait_recv()
            h[rows, :] = relayed[rows, :]

        share.start(c, normed_rows(h[rows, :].astype(f32), gain[...]).astype(bf16))

    share.finish()

    @pl.when(stage == 0)
    def _():
        for c in ORDER:
            relay_rows(y, relayed, relay_sems, c, 1).wait_send()
    reduced.drain()


def forward_last_kernel(
    peers_n, part, middle, gy, y, full, send, land, fine, total, sems, fine_sems, share_sems
):
    peers = Peers(peers_n)
    peers.enter()
    reduced = Sum(peers, part, send, land, sems, fine, fine_sems)
    share = Share(peers, full, share_sems)
    reduced.start()
    for c in ORDER:
        share.start(c, gy[reduced.rows(c), :])
    for c in ORDER:
        rows = reduced.rows(c)
        y[rows, :] = (middle[rows, :] + reduced.finish(c, total)).astype(bf16)
    share.finish()
    reduced.drain()


def backward_mid_kernel(
    peers_n, part, gy, middle, gain, d_middle, gain_part, full, send, land, total, sems, share_sems, extra=None):
    peers = Peers(peers_n)
    peers.enter(extra=extra)
    if extra is not None:
        extra.start()
    reduced = Sum(peers, part, send, land, sems)
    share = Share(peers, full, share_sems)
    reduced.start()
    gains = jnp.zeros(gain_part.shape, f32)
    for c in ORDER:
        rows = reduced.rows(c)
        d_u, g = norm_back(reduced.finish(c, total), middle[rows, :], gain[...])
        value = gy[rows, :].astype(f32) + d_u
        d_middle[rows, :] = value
        gains = gains + g
        share.start(c, value.astype(bf16))
    gain_part[...] = gains
    share.finish()
    reduced.drain()
    if extra is not None:
        extra.finish()


def backward_end_kernel(
    peers_n,
    part,
    d_middle,
    h,
    gain,
    own,
    grad,
    gain_part,
    gy,
    full,
    send,
    land,
    total,
    relayed,
    sems,
    share_sems,
    relay_sems,
):
    peers = Peers(peers_n)
    stage = lax.axis_index("stage")
    peers.enter(0)
    reduced = Sum(peers, part, send, land, sems)
    share = Share(peers, full, share_sems)
    reduced.start()
    gain_part[...] = jnp.zeros(gain_part.shape, f32)

    def finish(c):
        rows = reduced.rows(c)
        d_u, g = norm_back(reduced.finish(c, total), h[rows, :].astype(f32), gain[...])
        grad[rows, :] = (d_middle[rows, :] + d_u).astype(bf16)
        gain_part[...] += g

    for c in ORDER:
        rows = reduced.rows(c)
        relay = relay_rows(grad, relayed, relay_sems, c, 0)

        @pl.when(stage == 1)
        def _():
            finish(c)
            relay.start()
            gy[rows, :] = own[rows, :]

        @pl.when(stage == 0)
        def _():
            finish(c)
            relay.wait_recv()
            gy[rows, :] = relayed[rows, :]

        share.start(c, gy[rows, :])

    share.finish()

    @pl.when(stage == 1)
    def _():
        for c in ORDER:
            relay_rows(grad, relayed, relay_sems, c, 0).wait_send()
    reduced.drain()


def backward_last_kernel(
    peers_n, part, d_middle, h, gain, grad, gain_part, send, land, total, sems, extra=None):
    peers = Peers(peers_n)
    peers.enter(extra=extra)
    if extra is not None:
        extra.start()
    reduced = Sum(peers, part, send, land, sems)
    reduced.start()
    gains = jnp.zeros(gain_part.shape, f32)
    for c in ORDER:
        rows = reduced.rows(c)
        d_u, g = norm_back(reduced.finish(c, total), h[rows, :].astype(f32), gain[...])
        grad[rows, :] = (d_middle[rows, :] + d_u).astype(bf16)
        gains = gains + g
    gain_part[...] = gains
    reduced.drain()
    if extra is not None:
        extra.finish()


def in_vmem(count):
    return [pl.BlockSpec(memory_space=pltpu.VMEM)] * count


def kernel_call(body, outs, scratch, ident, *args, extra=None):
    outs = outs if isinstance(outs, list) else [outs]
    in_specs, out_specs = in_vmem(len(args)), in_vmem(len(outs))
    if extra is not None:
        kind, more_args, more_outs, more_scratch = extra
        sizes = [len(args), len(more_args), len(outs), len(more_outs), len(scratch)]
        own_body = body

        def body(*refs):
            cuts = [sum(sizes[:n]) for n in range(len(sizes) + 1)]
            parts = [refs[cuts[n] : cuts[n + 1]] for n in range(len(sizes))] + [refs[cuts[-1] :]]
            own_body(
                *parts[0], *parts[2], *parts[4], extra=kind(*parts[1], *parts[3], *parts[5])
            )

        anywhere = pl.BlockSpec(memory_space=pl.ANY)
        args, outs = args + tuple(more_args), outs + more_outs
        scratch = scratch + more_scratch
        in_specs = in_specs + [anywhere] * len(more_args)
        out_specs = out_specs + [anywhere] * len(more_outs)
    results = pl.pallas_call(
        body,
        out_shape=outs,
        in_specs=in_specs,
        out_specs=out_specs,
        scratch_shapes=scratch,
        compiler_params=pltpu.CompilerParams(
            collective_id=ident, has_side_effects=True, vmem_limit_bytes=40 * 1024 * 1024
        ),
    )(*args)
    return results[0] if len(results) == 1 else list(results)


def shape(dims, kind):
    return jax.ShapeDtypeStruct(dims, kind)


class Rows:
    def __init__(self, rows, width, peers):
        self.rows, self.width, self.peers = rows, width, peers
        self.slice_b = shape((rows, width), bf16)
        self.slice_f = shape((rows, width), f32)
        self.gain_f = shape((1, width), f32)
        self.full = shape((peers, rows, width), bf16)
        self.pair = pltpu.SemaphoreType.DMA((2, peers - 1))
        self.many = pltpu.SemaphoreType.DMA((2, 3, CHUNKS))
        self.reduce = [
            pltpu.VMEM((3, CHUNKS, rows // CHUNKS, width), bf16),
            pltpu.VMEM((3, CHUNKS, rows // CHUNKS, width), bf16),
        ]
        self.fine = [pltpu.VMEM((peers, width // LANES, LANES), f32)]
        self.total = [pltpu.VMEM((rows, width), f32)]
        self.relayed = [pltpu.VMEM((rows, width), bf16)]
        self.relay = pltpu.SemaphoreType.DMA((2, CHUNKS))

    def parts(self, part):
        return part.reshape(self.peers, self.rows, self.width)

    def flat(self, full):
        return full.reshape(self.peers * self.rows, self.width)

    def first(self, h, gain, extra):
        body = partial(first_kernel, self.peers)
        full, *more = kernel_call(body, self.full, [self.many], 1, h, gain, extra=extra)
        return self.flat(full), *more

    def forward_mid(self, part, h, gain, ident=3, extra=None):
        middle, full, *more = kernel_call(
            partial(forward_mid_kernel, self.peers),
            [self.slice_f, self.full],
            self.reduce + self.fine + self.total + [self.many, self.pair, self.many],
            ident,
            self.parts(part),
            h,
            gain,
            extra=extra,
        )
        return middle, self.flat(full), *more

    def forward_end(self, part, middle, gain, own):
        y, h, full = kernel_call(
            partial(forward_end_kernel, self.peers),
            [self.slice_b, self.slice_b, self.full],
            self.reduce
            + self.fine
            + self.total
            + self.relayed
            + [self.many, self.pair, self.many, self.relay],
            4,
            self.parts(part),
            middle,
            gain,
            own,
        )
        return y, h, self.flat(full)

    def forward_last(self, part, middle, gy):
        y, full = kernel_call(
            partial(forward_last_kernel, self.peers),
            [self.slice_b, self.full],
            self.reduce + self.fine + self.total + [self.many, self.pair, self.many],
            5,
            self.parts(part),
            middle,
            gy,
        )
        return y, self.flat(full)

    def backward_mid(self, part, gy, middle, gain, ident=6, extra=None):
        d_middle, gain_part, full, *more = kernel_call(
            partial(backward_mid_kernel, self.peers),
            [self.slice_f, self.gain_f, self.full],
            self.reduce + self.total + [self.many] * 2,
            ident,
            self.parts(part),
            gy,
            middle,
            gain,
            extra=extra,
        )
        return d_middle, gain_part, self.flat(full), *more

    def backward_end(self, part, d_middle, h, gain, own):
        grad, gain_part, gy, full = kernel_call(
            partial(backward_end_kernel, self.peers),
            [self.slice_b, self.gain_f, self.slice_b, self.full],
            self.reduce + self.total + self.relayed + [self.many] * 2 + [self.relay],
            7,
            self.parts(part),
            d_middle,
            h,
            gain,
            own,
        )
        return grad, gain_part, gy, self.flat(full)

    def backward_last(self, part, d_middle, h, gain, extra=None):
        return kernel_call(
            partial(backward_last_kernel, self.peers),
            [self.slice_b, self.gain_f],
            self.reduce + self.total + [self.many],
            8,
            self.parts(part),
            d_middle,
            h,
            gain,
            extra=extra,
        )


PAD = 16


class Chain:
    def __init__(self, ranges, half):
        self.ranges, self.half = ranges, half
        self.s, self.q = lax.axis_index("section"), lax.axis_index("q")
        self.me = self.s * half + self.q

    def after(self, d):
        return lax.rem(self.q + d, self.half)

    def before(self, d):
        return self.s * self.half + lax.rem(self.q + self.half - d, self.half)

    def enter(self, extra=None):
        signals = {("q", d): (None, {"q": self.after(d)}) for d in range(1, self.half)}
        signals["core"] = (None, {"section": 1 - self.s})
        greet(signals, dict.fromkeys(signals), extra)

    def along(self, land, sems, d):
        return pltpu.make_async_remote_copy(
            src_ref=land.at[self.me],
            dst_ref=land.at[self.me],
            send_sem=sems.at[0, d],
            recv_sem=sems.at[1, d],
            device_id={"q": self.after(d)},
        )

    def across(self, land, sems, d):
        return pltpu.make_async_remote_copy(
            src_ref=land.at[self.before(d)],
            dst_ref=land.at[self.before(d)],
            send_sem=sems.at[2, d],
            recv_sem=sems.at[3, d],
            device_id={"section": 1 - self.s},
        )

    def start(self, land, sems, state, through):
        high = state.shape[0]
        land[self.me, 0:high, :] = state.astype(bf16)
        land[self.me, high : high + PAD, :] = jnp.broadcast_to(
            through, (PAD, through.shape[1])
        ).astype(bf16)
        for d in range(1, self.half):
            self.along(land, sems, d).start()
        self.across(land, sems, 0).start()

    def forward(self, land, sems):
        for d in range(1, self.half):
            self.along(land, sems, d).wait_recv()
            self.across(land, sems, d).start()

    def finish(self, land, sems, high, later):
        for d in range(1, self.half):
            self.along(land, sems, d).wait_send()
        for d in range(self.half):
            self.across(land, sems, d).wait()

        def step(n, state):
            place = self.ranges - 1 - n if later else n
            taken = (place > self.me) if later else (place < self.me)
            through = land[place, high : high + PAD, :].astype(f32)[0:1, :]
            joined = through * state + land[place, 0:high, :].astype(f32)
            return jnp.where(taken, joined, state)

        zero = jnp.zeros((high, land.shape[2]), f32)
        state = zero
        for n in range(self.ranges):
            state = step(n, state)
        return state


def triangle(size):
    row = lax.broadcasted_iota(jnp.int32, (size, size), 0)
    col = lax.broadcasted_iota(jnp.int32, (size, size), 1)
    return row, col


def scores_of(q, k, c, fine):
    row, col = triangle(SPAN)
    middle = c[SPAN // 2 : SPAN // 2 + 1, :]
    up, down = jnp.exp(c - middle), jnp.exp(middle - c)
    a, b = q * up, k * down
    own = jnp.sum(q * k, axis=1, keepdims=True)
    if fine:
        scores = lax.dot_general(
            a, b, (((1,), (1,)), ((), ())), precision=HIGH, preferred_element_type=f32
        )
    a, b = a.astype(bf16), b.astype(bf16)
    if not fine:
        scores = dot_right(a, b)
    return jnp.where(row > col, scores, 0.0).astype(bf16), own, a, b, up, down


class Cuts:
    def __init__(self, key_dim, value_dim, rank):
        self.key, self.value = key_dim, value_dim
        self.q = slice(0, key_dim)
        self.k = slice(key_dim, 2 * key_dim)
        self.v = slice(2 * key_dim, 2 * key_dim + value_dim)
        self.og = slice(2 * key_dim + value_dim, 2 * key_dim + 2 * value_dim)
        self.begin = 2 * key_dim + 2 * value_dim
        self.width = self.begin + LANES * (-(-rank // LANES))
        self.rank = slice(self.begin, self.width)


def rounded(array):
    return array.astype(bf16).astype(f32)


def log_sigmoid(u):
    return jnp.minimum(u, 0.0) - jnp.log1p(jnp.exp(-jnp.abs(u)))


def mixer_forward_kernel(
    ranges, half, cuts, cat, up, bias, inner_ref, c_ref, l_ref, s_ref,
    moved, out, land, sems, extra=None,
):
    chain = Chain(ranges, half)
    chain.enter(extra)
    length = cat.shape[0]
    spans = length // SPAN
    scale = cuts.key ** (-0.5)
    row, col = triangle(SPAN)
    lower = (row >= col).astype(f32)
    state = jnp.zeros((cuts.value, cuts.key), f32)
    reach = jnp.zeros((1, cuts.key), f32)
    for i in range(spans):
        rows = slice(i * SPAN, (i + 1) * SPAN)
        logits = (
            jnp.dot(cat[rows, cuts.rank], up[...], precision=HIGH, preferred_element_type=f32)
            + bias[...]
        )
        l_ref[rows, :] = logits
        decay = log_sigmoid(logits) * (1.0 / GATE_SCALE)
        c = jnp.dot(lower, decay, precision=HIGH, preferred_element_type=f32)
        c_ref[rows, :] = c
        last = c[SPAN - 1 : SPAN, :]
        fading = (rounded(cat[rows, cuts.k]) * jnp.exp(last - c)).astype(bf16)
        step = dot_left(cat[rows, cuts.v].astype(bf16), fading)
        moved[i] = step
        state = jnp.exp(last) * state + step
        reach = reach + last
    chain.start(land, sems, state, jnp.exp(reach))
    if extra is not None:
        extra.start()
    for i in range(spans):
        rows = slice(i * SPAN, (i + 1) * SPAN)
        q = rounded(cat[rows, cuts.q]) * scale
        k = rounded(cat[rows, cuts.k])
        scores, own, *_ = scores_of(q, k, c_ref[rows, :], True)
        v = cat[rows, cuts.v].astype(bf16)
        out[rows, :] = dot_plain(scores, v) + own * v.astype(f32)
    chain.forward(land, sems)
    state = chain.finish(land, sems, cuts.value, False)
    for i in range(spans):
        rows = slice(i * SPAN, (i + 1) * SPAN)
        c = c_ref[rows, :]
        held = state.astype(bf16)
        s_ref[i] = held
        q = (rounded(cat[rows, cuts.q]) * scale * jnp.exp(c)).astype(bf16)
        inner_ref[rows, :] = out[rows, :] + dot_right(q, held)
        state = jnp.exp(c[SPAN - 1 : SPAN, :]) * state + moved[i]
    s_ref[spans] = state.astype(bf16)
    if extra is not None:
        extra.finish()


def mixer_backward_kernel(
    ranges, half, cuts, dgated_ref, inner_ref, cat, up, hg_ref, c_ref, l_ref, s_ref,
    dcat, hgp_ref, dup_ref, dbias_ref, pulled, o_ref, dqs, dks, dvs, land, sems, extra=None,
):
    chain = Chain(ranges, half)
    chain.enter(extra)
    length = cat.shape[0]
    spans = length // SPAN
    scale = cuts.key ** (-0.5)
    row, col = triangle(SPAN)
    upper = (row <= col).astype(f32)
    state = jnp.zeros((cuts.value, cuts.key), f32)
    reach = jnp.zeros((1, cuts.key), f32)
    hg = hg_ref[...]
    head_part = jnp.zeros((1, cuts.value), f32)
    for i in reversed(range(spans)):
        rows = slice(i * SPAN, (i + 1) * SPAN)
        inner, og, dgated = inner_ref[rows, :], cat[rows, cuts.og], dgated_ref[rows, :]
        r = lax.rsqrt(jnp.mean(inner * inner, axis=-1, keepdims=True) + HEAD_EPS)
        sg = 1.0 / (1.0 + jnp.exp(-og))
        d_norm = dgated * (og * sg)
        unit = inner * r
        head_part = head_part + jnp.sum(d_norm * unit, axis=0, keepdims=True)
        w = d_norm * hg
        d_inner = r * w - inner * (r * r * r) * jnp.mean(w * inner, axis=-1, keepdims=True)
        dog = dgated * unit * hg * (sg * (1.0 + og * (1.0 - sg)))
        dcat[rows, cuts.og] = dog.astype(bf16)
        o_ref[rows, :] = d_inner
        o = d_inner.astype(bf16)
        c = c_ref[rows, :]
        q = (rounded(cat[rows, cuts.q]) * scale * jnp.exp(c)).astype(bf16)
        step = dot_left(o, q)
        pulled[i] = step
        last = c[SPAN - 1 : SPAN, :]
        state = jnp.exp(last) * state + step
        reach = reach + last
    hgp_ref[...] = head_part
    chain.start(land, sems, state, jnp.exp(reach))
    if extra is not None:
        extra.start()
    for i in range(spans):
        rows = slice(i * SPAN, (i + 1) * SPAN)
        q = rounded(cat[rows, cuts.q]) * scale
        k = rounded(cat[rows, cuts.k])
        scores, own, a, b, gain_up, gain_down = scores_of(q, k, c_ref[rows, :], False)
        d_inner, v = o_ref[rows, :], cat[rows, cuts.v].astype(bf16)
        o = d_inner.astype(bf16)
        d_own = jnp.sum(d_inner * v.astype(f32), axis=1, keepdims=True)
        d_scores = jnp.where(row > col, dot_right(o, v), 0.0).astype(bf16)
        dvs[rows, :] = dot_left(scores, o) + own * d_inner
        dqs[rows, :] = (
            d_own * k
            + gain_up * dot_plain(d_scores, b)
            + jnp.exp(c_ref[rows, :]) * dot_plain(o, s_ref[i])
        )
        dks[rows, :] = d_own * q + gain_down * dot_left(d_scores, a)
    chain.forward(land, sems)
    state = chain.finish(land, sems, cuts.value, True)
    d_up = jnp.zeros(dup_ref.shape, f32)
    d_bias = jnp.zeros(dbias_ref.shape, f32)
    for i in reversed(range(spans)):
        rows = slice(i * SPAN, (i + 1) * SPAN)
        c = c_ref[rows, :]
        last = c[SPAN - 1 : SPAN, :]
        fade = jnp.exp(last - c)
        held = state.astype(bf16)
        k = rounded(cat[rows, cuts.k])
        dk = dks[rows, :] + fade * dot_plain(cat[rows, cuts.v].astype(bf16), held)
        dv = dvs[rows, :] + dot_right((k * fade).astype(bf16), held)
        dq = dqs[rows, :]
        dcat[rows, cuts.q] = (dq * scale).astype(bf16)
        dcat[rows, cuts.k] = dk.astype(bf16)
        dcat[rows, cuts.v] = dv.astype(bf16)
        ended = jnp.sum(state * s_ref[i + 1].astype(f32), axis=0, keepdims=True)
        terms = rounded(cat[rows, cuts.q]) * scale * dq - k * dk
        d_decay = jnp.dot(upper, terms, precision=HIGH, preferred_element_type=f32) + ended
        d_logits = d_decay * (1.0 / (1.0 + jnp.exp(l_ref[rows, :]))) * (1.0 / GATE_SCALE)
        d_bias = d_bias + jnp.sum(d_logits, axis=0, keepdims=True)
        d_up = d_up + lax.dot_general(
            cat[rows, cuts.rank], d_logits, (((0,), (0,)), ((), ())),
            precision=HIGH, preferred_element_type=f32,
        )
        d_rank = lax.dot_general(
            d_logits, up[...], (((1,), (1,)), ((), ())),
            precision=HIGH, preferred_element_type=f32,
        )
        dcat[rows, cuts.rank] = d_rank.astype(bf16)
        state = jnp.exp(last) * state + pulled[i]
    dup_ref[...] = d_up
    dbias_ref[...] = d_bias
    if extra is not None:
        extra.finish()


def mixer_forward(ranges, half, cuts, cat, up, bias, ident=9, extra=None):
    length = cat.shape[0]
    spans = length // SPAN
    return kernel_call(
        partial(mixer_forward_kernel, ranges, half, cuts),
        [
            shape((length, cuts.value), f32),
            shape((length, cuts.key), f32),
            shape((length, cuts.key), f32),
            shape((spans + 1, cuts.value, cuts.key), bf16),
        ],
        [
            pltpu.VMEM((spans, cuts.value, cuts.key), f32),
            pltpu.VMEM((length, cuts.value), f32),
            pltpu.VMEM((ranges, cuts.value + PAD, cuts.key), bf16),
            pltpu.SemaphoreType.DMA((4, half)),
        ],
        ident,
        cat, up, bias,
        extra=extra,
    )


def mixer_backward(
    ranges, half, cuts, dgated, inner, cat, up, hg, c, logits, s, ident=10, extra=None
):
    length = cat.shape[0]
    spans = length // SPAN
    return kernel_call(
        partial(mixer_backward_kernel, ranges, half, cuts),
        [
            shape((length, cuts.width), bf16),
            shape((1, cuts.value), f32),
            shape(up.shape, f32),
            shape((1, cuts.key), f32),
        ],
        [
            pltpu.VMEM((spans, cuts.value, cuts.key), f32),
            pltpu.VMEM((length, cuts.value), f32),
            pltpu.VMEM((length, cuts.key), f32),
            pltpu.VMEM((length, cuts.key), f32),
            pltpu.VMEM((length, cuts.value), f32),
            pltpu.VMEM((ranges, cuts.value + PAD, cuts.key), bf16),
            pltpu.SemaphoreType.DMA((4, half)),
        ],
        ident,
        dgated, inner, cat, up, hg, c, logits, s,
        extra=extra,
    )


class Ranges:
    def __init__(self, half):
        self.half = half
        self.s, self.l = lax.axis_index("section"), lax.axis_index("stage")
        self.q = lax.axis_index("q")
        self.stays = self.s == self.l

    def enter(self, cores):
        barrier = pltpu.get_barrier_semaphore()
        for d in range(1, self.half):
            pl.semaphore_signal(barrier, inc=1, device_id={"q": self.after(d)})
        count = self.half - 1
        if cores:
            pl.semaphore_signal(barrier, inc=1, device_id={"section": 1 - self.s})
            count = count + 1

        @pl.when(self.stays)
        def _():
            pl.semaphore_wait(barrier, count)

        @pl.when(jnp.logical_not(self.stays))
        def _():
            pl.semaphore_signal(barrier, inc=1, device_id={"section": self.l, "stage": self.s})
            pl.semaphore_wait(barrier, count + 1)

    def after(self, d):
        return lax.rem(self.q + d, self.half)

    def before(self, d):
        return lax.rem(self.q + self.half - d, self.half)

    def at(self, section, q, rows):
        return pl.ds(pl.multiple_of((section * self.half + q) * rows, rows), rows)


def gather_kernel(half, count, *refs):
    ins, outs, bounce = refs[:count], refs[count : 2 * count], refs[2 * count : 3 * count]
    swap_sems, z_sems, core_sems, keep_sems = refs[3 * count :]
    r = Ranges(half)
    r.enter(True)

    def held(i):
        rows = ins[i].shape[0]
        return outs[i].at[r.at(r.s, r.q, rows)]

    def swap(i):
        rows = ins[i].shape[0]
        return pltpu.make_async_remote_copy(
            src_ref=ins[i],
            dst_ref=outs[i].at[r.at(r.l, r.q, rows)],
            send_sem=swap_sems.at[0, i],
            recv_sem=swap_sems.at[1, i],
            device_id={"section": r.l, "stage": r.s},
        )

    def along(i, d, src):
        return pltpu.make_async_remote_copy(
            src_ref=src,
            dst_ref=held(i),
            send_sem=z_sems.at[0, i, d - 1],
            recv_sem=z_sems.at[1, i, d - 1],
            device_id={"q": r.after(d)},
        )

    def across(i, d, src):
        rows = ins[i].shape[0]
        return pltpu.make_async_remote_copy(
            src_ref=src,
            dst_ref=outs[i].at[r.at(r.s, r.before(d), rows)],
            send_sem=core_sems.at[0, i, d],
            recv_sem=core_sems.at[1, i, d],
            device_id={"section": 1 - r.s},
        )

    def load(i):
        return pltpu.make_async_copy(ins[i], bounce[i], keep_sems.at[0, i])

    def keep(i):
        return pltpu.make_async_copy(bounce[i], held(i), keep_sems.at[1, i])

    @pl.when(r.stays)
    def _():
        for i in range(count):
            for d in range(1, half):
                along(i, d, ins[i]).start()
            across(i, 0, ins[i]).start()
            load(i).start()
        for i in range(count):
            load(i).wait()
            keep(i).start()

    @pl.when(jnp.logical_not(r.stays))
    def _():
        for i in range(count):
            swap(i).start()

    for i in range(count):
        rows = ins[i].shape[0]

        @pl.when(jnp.logical_not(r.stays))
        def _():
            swap(i).wait_recv()
            for d in range(1, half):
                along(i, d, held(i)).start()
            across(i, 0, held(i)).start()

        for d in range(1, half):
            along(i, d, ins[i]).wait_recv()
            across(i, d, outs[i].at[r.at(r.s, r.before(d), rows)]).start()

    for i in range(count):

        @pl.when(r.stays)
        def _():
            keep(i).wait()

        @pl.when(jnp.logical_not(r.stays))
        def _():
            swap(i).wait_send()

        for d in range(1, half):
            along(i, d, ins[i]).wait_send()
        for d in range(half):
            across(i, d, ins[i]).wait()


def gather_weights(half, ident, *shards_in):
    count = len(shards_in)
    anywhere = pl.BlockSpec(memory_space=pl.ANY)
    return pl.pallas_call(
        partial(gather_kernel, half, count),
        out_shape=[shape((2 * half * a.shape[0], a.shape[1]), a.dtype) for a in shards_in],
        in_specs=[anywhere] * count,
        out_specs=[anywhere] * count,
        scratch_shapes=[pltpu.VMEM(a.shape, a.dtype) for a in shards_in]
        + [
            pltpu.SemaphoreType.DMA((2, count)),
            pltpu.SemaphoreType.DMA((2, count, half - 1)),
            pltpu.SemaphoreType.DMA((2, count, half)),
            pltpu.SemaphoreType.DMA((2, count)),
        ],
        compiler_params=pltpu.CompilerParams(
            collective_id=ident, has_side_effects=True, vmem_limit_bytes=40 * 1024 * 1024
        ),
    )(*shards_in)


class GatherStart:
    def __init__(self, half, home, whole, bounce, swap_sems, z_sems, core_sems, keep_sems):
        r = self.r = Ranges(half)
        rows = home.shape[0]
        self.half = half
        moves = jnp.logical_not(r.stays)
        self.signals = {("q", d): (None, {"q": r.after(d)}) for d in range(1, half)}
        self.signals["core"] = (None, {"section": 1 - r.s})
        self.signals["swap"] = (moves, {"section": r.l, "stage": r.s})
        self.waits = {name: condition for name, (condition, _) in self.signals.items()}
        held = whole.at[r.at(r.s, r.q, rows)]
        self.swap = pltpu.make_async_remote_copy(
            src_ref=home,
            dst_ref=whole.at[r.at(r.l, r.q, rows)],
            send_sem=swap_sems.at[0],
            recv_sem=swap_sems.at[1],
            device_id={"section": r.l, "stage": r.s},
        )
        self.along = [
            pltpu.make_async_remote_copy(
                src_ref=home,
                dst_ref=held,
                send_sem=z_sems.at[0, d - 1],
                recv_sem=z_sems.at[1, d - 1],
                device_id={"q": r.after(d)},
            )
            for d in range(1, half)
        ]
        self.across = pltpu.make_async_remote_copy(
            src_ref=home,
            dst_ref=held,
            send_sem=core_sems.at[0],
            recv_sem=core_sems.at[1],
            device_id={"section": 1 - r.s},
        )
        self.load = pltpu.make_async_copy(home, bounce, keep_sems.at[0])
        self.keep = pltpu.make_async_copy(bounce, held, keep_sems.at[1])

    def start(self):
        @pl.when(self.r.stays)
        def _():
            for copy in self.along:
                copy.start()
            self.across.start()
            self.load.start()

        @pl.when(jnp.logical_not(self.r.stays))
        def _():
            self.swap.start()

    def finish(self):
        @pl.when(self.r.stays)
        def _():
            self.load.wait()
            self.keep.start()
            for copy in self.along:
                copy.wait()
            self.across.wait_send()
            self.keep.wait()

        @pl.when(jnp.logical_not(self.r.stays))
        def _():
            self.swap.wait()
            self.across.wait_recv()


def gather_start(half, home):
    return (
        partial(GatherStart, half),
        [home],
        [shape((2 * half * home.shape[0], home.shape[1]), home.dtype)],
        [
            pltpu.VMEM(home.shape, home.dtype),
            pltpu.SemaphoreType.DMA((2,)),
            pltpu.SemaphoreType.DMA((2, half - 1)),
            pltpu.SemaphoreType.DMA((2,)),
            pltpu.SemaphoreType.DMA((2,)),
        ],
    )


def gather_end_kernel(half, count, rows, *refs):
    outs = refs[count : 2 * count]
    z_sems, core_sems = refs[2 * count :]
    r = Ranges(half)
    r.enter(True)

    def piece(i, q):
        return outs[i].at[r.at(r.s, q, rows)]

    def along(i, d):
        return pltpu.make_async_remote_copy(
            src_ref=piece(i, r.q),
            dst_ref=piece(i, r.q),
            send_sem=z_sems.at[0, i, d - 1],
            recv_sem=z_sems.at[1, i, d - 1],
            device_id={"q": r.after(d)},
        )

    def across(i, d):
        return pltpu.make_async_remote_copy(
            src_ref=piece(i, r.before(d)),
            dst_ref=piece(i, r.before(d)),
            send_sem=core_sems.at[0, i, d],
            recv_sem=core_sems.at[1, i, d],
            device_id={"section": 1 - r.s},
        )

    @pl.when(r.stays)
    def _():
        for i in range(count):
            for d in range(1, half):
                across(i, d).start()
        for i in range(count):
            for d in range(1, half):
                across(i, d).wait()
            across(i, 0).wait_recv()

    @pl.when(jnp.logical_not(r.stays))
    def _():
        for i in range(count):
            for d in range(1, half):
                along(i, d).start()
        for i in range(count):
            across(i, 0).start()
        for i in range(count):
            for d in range(1, half):
                along(i, d).wait_recv()
                across(i, d).start()
        for i in range(count):
            for d in range(1, half):
                along(i, d).wait_send()
                across(i, d).wait()
            across(i, 0).wait_send()


def gather_end(half, ident, *begun):
    count = len(begun)
    rows = begun[0].shape[0] // (2 * half)
    anywhere = pl.BlockSpec(memory_space=pl.ANY)
    return pl.pallas_call(
        partial(gather_end_kernel, half, count, rows),
        out_shape=[shape(a.shape, a.dtype) for a in begun],
        in_specs=[anywhere] * count,
        out_specs=[anywhere] * count,
        scratch_shapes=[
            pltpu.SemaphoreType.DMA((2, count, half - 1)),
            pltpu.SemaphoreType.DMA((2, count, half)),
        ],
        input_output_aliases={i: i for i in range(count)},
        compiler_params=pltpu.CompilerParams(collective_id=ident, has_side_effects=True),
    )(*begun)


class AlongStart:
    def __init__(self, half, rows, *refs):
        r = self.r = Ranges(half)
        self.signals = {("q", d): (None, {"q": r.after(d)}) for d in range(1, half)}
        self.swap = None
        if len(refs) == 3:
            total, away, sems = refs
        else:
            total, summed, away, landed, sems, swap_sems = refs
            self.moves = jnp.logical_not(r.stays)
            self.signals["swap"] = (self.moves, {"section": r.l, "stage": r.s})
            self.swap = pltpu.make_async_remote_copy(
                src_ref=summed,
                dst_ref=landed,
                send_sem=swap_sems.at[0],
                recv_sem=swap_sems.at[1],
                device_id={"section": r.l, "stage": r.s},
            )
        self.waits = {name: condition for name, (condition, _) in self.signals.items()}
        self.copies = [
            pltpu.make_async_remote_copy(
                src_ref=total.at[r.at(0, r.after(d), rows)],
                dst_ref=away.at[d - 1],
                send_sem=sems.at[0, d - 1],
                recv_sem=sems.at[1, d - 1],
                device_id={"q": r.after(d)},
            )
            for d in range(1, half)
        ]

    def start(self):
        for copy in self.copies:
            copy.start()
        if self.swap is not None:

            @pl.when(self.moves)
            def _():
                self.swap.start()

    def finish(self):
        for copy in self.copies:
            copy.wait()
        if self.swap is not None:

            @pl.when(self.moves)
            def _():
                self.swap.wait()


def along_start(half, total, summed=None):
    rows = total.shape[0] // half
    away = shape((half - 1, rows, total.shape[1]), total.dtype)
    sems = pltpu.SemaphoreType.DMA((2, half - 1))
    kind = partial(AlongStart, half, rows)
    if summed is None:
        return kind, [total], [away], [sems]
    landed = shape(summed.shape, summed.dtype)
    return kind, [total, summed], [away, landed], [sems, pltpu.SemaphoreType.DMA((2,))]


class HomeStart:
    def __init__(self, half, src, landed, sems):
        r = Ranges(half)
        self.moves = jnp.logical_not(r.stays)
        self.signals = {"swap": (self.moves, {"section": r.l, "stage": r.s})}
        self.waits = {"swap": self.moves}
        self.copy = pltpu.make_async_remote_copy(
            src_ref=src,
            dst_ref=landed,
            send_sem=sems.at[0],
            recv_sem=sems.at[1],
            device_id={"section": r.l, "stage": r.s},
        )

    def start(self):
        @pl.when(self.moves)
        def _():
            self.copy.start()

    def finish(self):
        @pl.when(self.moves)
        def _():
            self.copy.wait()


def home_start(half, array):
    sems = [pltpu.SemaphoreType.DMA((2,))]
    return partial(HomeStart, half), [array], [shape(array.shape, array.dtype)], sems


def finish_kernel(half, count, come, places, lanes, *refs):
    totals, aways = refs[:count], refs[count : count + come]
    refs = refs[count + come :]
    rows_in, small = refs[:places], refs[places]
    refs = refs[places + 1 :]
    outs, full, down, small_own, small_sum = (
        refs[:count],
        refs[count : count + places],
        refs[count + places],
        refs[count + places + 1],
        refs[count + places + 2],
    )
    refs = refs[count + places + 3 :]
    mine, got = refs[:count], refs[count : 2 * count]
    small_mine, small_got, small_land, down_send, down_land, held = refs[
        2 * count : 2 * count + 6
    ]
    (
        swap_sems, z_sems, load_sems, away_sems, place_sems, keep_sems, share_sems, small_sems,
        pool_sems,
    ) = refs[2 * count + 6 :]
    peers_n = full[0].shape[1]
    r = Ranges(half)
    peers = Peers(peers_n)
    barrier = pltpu.get_barrier_semaphore()
    for d in range(1, peers_n):
        pl.semaphore_signal(barrier, inc=1, device_id={"tensor": peers.at(d)})
    for d in range(1, half):
        pl.semaphore_signal(barrier, inc=1, device_id={"q": r.after(d)})
    signals = peers_n + half - 2

    @pl.when(r.stays)
    def _():
        pl.semaphore_wait(barrier, signals)

    @pl.when(jnp.logical_not(r.stays))
    def _():
        pl.semaphore_signal(barrier, inc=1, device_id={"section": r.l, "stage": r.s})
        pl.semaphore_wait(barrier, signals + 1)

    def whole(i):
        return i < count - come

    def part(i, q):
        return totals[i].at[r.at(0, q, outs[i].shape[0])]

    def load_away(i):
        return pltpu.make_async_copy(aways[i - count + come], got[i], away_sems.at[i - count + come])

    def along(i, d):
        return pltpu.make_async_remote_copy(
            src_ref=part(i, r.after(d)),
            dst_ref=got[i].at[d - 1],
            send_sem=z_sems.at[0, i, d - 1],
            recv_sem=z_sems.at[1, i, d - 1],
            device_id={"q": r.after(d)},
        )

    def load(i):
        return pltpu.make_async_copy(part(i, r.q), mine[i], load_sems.at[i])

    def home(src, dst, sems):
        return pltpu.make_async_remote_copy(
            src_ref=src,
            dst_ref=dst,
            send_sem=sems.at[0],
            recv_sem=sems.at[1],
            device_id={"section": r.l, "stage": r.s},
        )

    def swap(i):
        return home(mine[i], outs[i], swap_sems.at[i])

    def place(j):
        return home(rows_in[j], held.at[j], place_sems.at[j])

    def shared(j, d, src):
        return pltpu.make_async_remote_copy(
            src_ref=src,
            dst_ref=full[j].at[:, peers.me],
            send_sem=share_sems.at[0, j, d - 1],
            recv_sem=share_sems.at[1, j, d - 1],
            device_id={"tensor": peers.at(d)},
        )

    def keep(j, src):
        return pltpu.make_async_copy(src, full[j].at[:, peers.me], keep_sems.at[j])

    def small_along(d):
        return pltpu.make_async_remote_copy(
            src_ref=small.at[r.after(d)],
            dst_ref=small_got.at[d - 1],
            send_sem=small_sems.at[0, d],
            recv_sem=small_sems.at[1, d],
            device_id={"q": r.after(d)},
        )

    def pool(n, d, src, dst):
        return pltpu.make_async_remote_copy(
            src_ref=src,
            dst_ref=dst,
            send_sem=pool_sems.at[0, n, d - 1],
            recv_sem=pool_sems.at[1, n, d - 1],
            device_id={"tensor": peers.at(d)},
        )

    for d in range(1, half):
        small_along(d).start()
    order = sorted(range(count), key=whole)
    ahead = [i for i in order if whole(i)]

    def begin(n):
        if n < len(ahead):
            for d in range(1, half):
                along(ahead[n], d).start()

    for n in range(WINDOW):
        begin(n)
    for i in order:
        load(i).start()
        if not whole(i):
            load_away(i).start()

    def show(j, src):
        keep(j, src).start()
        for d in range(1, peers_n):
            shared(j, d, src).start()

    @pl.when(r.stays)
    def _():
        for j in range(places):
            show(j, rows_in[j])

    @pl.when(jnp.logical_not(r.stays))
    def _():
        show(0, rows_in[0])
        for j in range(1, places):
            place(j).start()

    for i in order:
        load(i).wait()
        if whole(i):
            for d in range(1, half):
                along(i, d).wait_recv()
            begin(ahead.index(i) + WINDOW)
        else:
            load_away(i).wait()

        @pl.loop(0, outs[i].shape[0] // STRIP)
        def _(n):
            strip = pl.ds(pl.multiple_of(n * STRIP, STRIP), STRIP)
            total = mine[i][strip, :].astype(f32)
            for d in range(1, half):
                total = total + got[i][d - 1, strip, :].astype(f32)
            mine[i][strip, :] = total.astype(bf16)

        @pl.when(r.stays)
        def _():
            @pl.loop(0, outs[i].shape[0] // STRIP)
            def _(n):
                strip = pl.ds(pl.multiple_of(n * STRIP, STRIP), STRIP)
                outs[i][strip, :] = mine[i][strip, :]

        @pl.when(jnp.logical_not(r.stays))
        def _():
            swap(i).start()

    total = small[r.q]
    for d in range(1, half):
        small_along(d).wait()
        total = total + small_got[d - 1]
    small_mine[...] = total

    @pl.when(r.stays)
    def _():
        small_own[...] = total

    @pl.when(jnp.logical_not(r.stays))
    def _():
        home(small_mine, small_own, small_sems.at[:, 0]).start()
        for j in range(1, places):
            place(j).wait_recv()
            show(j, held.at[j])
        home(small_mine, small_own, small_sems.at[:, 0]).wait()
        for i in range(count):
            swap(i).wait()
        for j in range(1, places):
            place(j).wait_send()

    down_send[...] = outs[0][:, lanes]
    for d in range(1, peers_n):
        pool(0, d, small_own, small_land.at[d - 1]).start()
        pool(1, d, down_send, down_land.at[d - 1]).start()
    total = small_own[...]
    pooled = down_send[...].astype(f32)
    for d in range(1, peers_n):
        pool(0, d, small_own, small_land.at[d - 1]).wait()
        pool(1, d, down_send, down_land.at[d - 1]).wait()
        total = total + small_land[d - 1]
        pooled = pooled + down_land[d - 1].astype(f32)
    small_sum[...] = total
    down[...] = pooled
    for i in range(count):
        if whole(i):
            for d in range(1, half):
                along(i, d).wait_send()
    for j in range(places):
        keep(j, rows_in[j]).wait()
        for d in range(1, peers_n):
            shared(j, d, rows_in[j]).wait()


def finish(half, peers, ident, totals, aways, rows_in, small, lanes):
    count, come, places = len(totals), len(aways), len(rows_in)
    high = totals[0].shape[0] // half
    micro, rows, width = rows_in[0].shape
    wide = lanes.stop - lanes.start
    anywhere = pl.BlockSpec(memory_space=pl.ANY)
    vmem = pl.BlockSpec(memory_space=pltpu.VMEM)
    tile = small.shape[1:]
    return pl.pallas_call(
        partial(finish_kernel, half, count, come, places, lanes),
        out_shape=[shape((high, a.shape[1]), bf16) for a in totals]
        + [shape((micro, peers, rows, width), bf16)] * places
        + [shape((high, wide), f32), shape(tile, f32), shape(tile, f32)],
        in_specs=[anywhere] * (count + come) + [vmem] * (places + 1),
        out_specs=[vmem] * count + [anywhere] * places + [vmem] * 3,
        scratch_shapes=[pltpu.VMEM((high, a.shape[1]), bf16) for a in totals]
        + [pltpu.VMEM((half - 1, high, a.shape[1]), bf16) for a in totals]
        + [
            pltpu.VMEM(tile, f32),
            pltpu.VMEM((half - 1,) + tile, f32),
            pltpu.VMEM((peers - 1,) + tile, f32),
            pltpu.VMEM((high, wide), bf16),
            pltpu.VMEM((peers - 1, high, wide), bf16),
            pltpu.VMEM((places, micro, rows, width), bf16),
            pltpu.SemaphoreType.DMA((count, 2)),
            pltpu.SemaphoreType.DMA((2, count, half - 1)),
            pltpu.SemaphoreType.DMA((count,)),
            pltpu.SemaphoreType.DMA((max(come, 1),)),
            pltpu.SemaphoreType.DMA((places, 2)),
            pltpu.SemaphoreType.DMA((places,)),
            pltpu.SemaphoreType.DMA((2, places, peers - 1)),
            pltpu.SemaphoreType.DMA((2, half)),
            pltpu.SemaphoreType.DMA((2, 2, peers - 1)),
        ],
        compiler_params=pltpu.CompilerParams(
            collective_id=ident, has_side_effects=True, vmem_limit_bytes=48 * 1024 * 1024
        ),
    )(*totals, *aways, *rows_in, small)


def swapped(array):
    moved = swap_moved(array)
    stays = lax.axis_index("section") == lax.axis_index("stage")
    return jnp.where(stays, array, moved)


def swap_moved(array):
    return lax.ppermute(array, ("section", "stage"), [(1, 2), (2, 1)])


def exchanged(array, axis):
    return lax.ppermute(array, axis, [(0, 1), (1, 0)])


def core_sum(left, right):
    high = left.shape[1] // 2
    section = lax.axis_index("section")

    def rows_for(who):
        return dot_left(lax.dynamic_slice_in_dim(left, who * high, high, 1), right)

    theirs = exchanged(rows_for(1 - section).astype(bf16), "section")
    return (rows_for(section) + theirs.astype(f32)).astype(bf16)


def range_sum(total):
    if lax.axis_size("q") != 2:
        return lax.psum_scatter(total, "q", scatter_dimension=0, tiled=True)
    place, high = lax.axis_index("q"), total.shape[0] // 2
    away = exchanged(lax.dynamic_slice_in_dim(total, (1 - place) * high, high, 0), "q")
    own = lax.dynamic_slice_in_dim(total, place * high, high, 0)
    return (own.astype(f32) + away.astype(f32)).astype(bf16)


def tiles_of(array, lead, low):
    width = -(-array.shape[1] // (low * LANES)) * LANES
    array = jnp.pad(array, ((0, 0), (0, low * width - array.shape[1])))
    return array.reshape(lead, low, width)


def shards(
    inputs,
    cotangent,
    query_proj,
    key_proj,
    value_proj,
    outgate_proj,
    output_proj,
    decay_down,
    decay_up,
    decay_bias,
    head_gain,
    mixer_gain,
    feed_gain,
    feed_gate,
    feed_up,
    feed_down,
):
    micro, length, width = inputs.shape
    peers = lax.axis_size("tensor")
    half = lax.axis_size("q")
    ranges = 2 * half
    stage = lax.axis_index("stage")
    me = lax.axis_index("tensor")
    rows = length // peers
    rank = decay_down.shape[2]
    cuts = Cuts(query_proj.shape[2], value_proj.shape[2], rank)
    sizes = (ranges, half, cuts)

    def own_rows(array):
        return swapped(lax.dynamic_slice_in_dim(array, me * rows, rows, 1))

    own_in = own_rows(inputs)
    small = [decay_up[0], decay_bias[0], head_gain[0], mixer_gain[0], feed_gain[0]]
    counts = [a.size for a in small]
    ends = [sum(counts[:n]) for n in range(len(counts) + 1)]
    small = tiles_of(jnp.concatenate([a.reshape(1, -1) for a in small], axis=1), 1, 16)[0]
    lanes = cuts.width - cuts.begin
    cat = jnp.concatenate(
        [query_proj[0], key_proj[0], value_proj[0], outgate_proj[0], decay_down[0]], axis=1
    )
    cat = jnp.pad(cat, ((0, 0), (0, cuts.width - cat.shape[1])))
    packed, cat, output = gather_weights(half, 11, small, cat, output_proj[0])
    packed = packed.reshape(ranges, -1).astype(f32)
    up_w, bias_w, head_w, mixer_w, feed_w = (
        packed[:, ends[n] : ends[n + 1]] for n in range(len(counts))
    )
    w = dict(
        up=jnp.pad(up_w.reshape(-1, rank).T, ((0, lanes - rank), (0, 0))),
        bias=bias_w.reshape(1, -1),
        head_gain=head_w.reshape(1, -1),
        mixer_gain=mixer_w.reshape(1, -1),
        feed_gain=feed_w.reshape(1, -1),
    )
    w["cat"], w["output"] = cat, output
    homes = [feed_gate[0], feed_up[0], feed_down[0]]
    calls = Rows(rows, width, peers)
    held_cot = lax.dynamic_slice_in_dim(cotangent, me * rows, rows, 1)
    kept, ys = [], []
    h = jnp.where(stage == 0, own_in[0], jnp.zeros_like(own_in[0]))
    normed, gate = calls.first(h, w["mixer_gain"], gather_start(half, homes[0]))
    for step in range(micro + 1):
        cat_v = dot_plain(normed, w["cat"])
        inner, cumul, logits, states, *upper = mixer_forward(
            ranges, half, cuts, cat_v, w["up"], w["bias"],
            **(dict(ident=14, extra=gather_start(half, homes[1])) if step == 0 else {}),
        )
        gated = head_output(inner, cat_v[:, cuts.og], w["head_gain"]).astype(bf16)
        middle, feed_in, *lower = calls.forward_mid(
            dot_right(gated, w["output"]), h, w["feed_gain"],
            **(dict(ident=15, extra=gather_start(half, homes[2])) if step == 0 else {}),
            **(dict(ident=19, extra=home_start(half, held_cot)) if step == 1 else {}),
        )
        if step == 1:
            own_cot = jnp.where(lax.axis_index("section") == stage, held_cot, lower[0])
        if step == 0:
            w["gate"], w["upper"], w["lower"] = gather_end(half, 12, gate, *upper, *lower)
        gate_v = dot_plain(feed_in, w["gate"])
        upper_v = dot_plain(feed_in, w["upper"])
        hidden = (jax.nn.silu(gate_v) * upper_v).astype(bf16)
        kept.append(
            dict(
                h=h, normed=normed, cat=cat_v, inner=inner, gated=gated, cumul=cumul,
                logits=logits, states=states, middle=middle, feed_in=feed_in, gate_v=gate_v,
                upper_v=upper_v, hidden=hidden,
            )
        )
        part = dot_right(hidden, w["lower"])
        if step < micro:
            y, h, normed = calls.forward_end(
                part, middle, w["mixer_gain"], own_in[min(step + 1, micro - 1)]
            )
        else:
            gy = jnp.where(stage == 1, own_cot[micro - 1], jnp.zeros_like(own_cot[0]))
            y, d_feed = calls.forward_last(part, middle, gy)
        ys.append(y)

    grads, saved = [], []

    def picked(zero, one):
        return jnp.where(stage == 0, zero, one)

    def rows_of(name):
        items = [item[name] for item in (kept if name in kept[0] else saved[::-1])]
        return jnp.concatenate([picked(items[m], items[m + 1]) for m in range(micro)])

    def with_away(total, away):
        place, high = lax.axis_index("q"), total.shape[0] // half
        own = lax.dynamic_slice_in_dim(total, place * high, high, 0)
        return (own.astype(f32) + jnp.sum(away.astype(f32), axis=0)).astype(bf16)

    worked = picked(jnp.stack(ys[:micro]), jnp.stack(ys[1:]))

    for step in range(micro + 1):
        now = kept[micro - step]
        d_hidden = dot_plain(d_feed, w["lower"])
        sig = jax.nn.sigmoid(now["gate_v"])
        d_gate = (
            d_hidden * now["upper_v"] * (sig * (1.0 + now["gate_v"] * (1.0 - sig)))
        ).astype(bf16)
        d_upper = (d_hidden * (now["gate_v"] * sig)).astype(bf16)
        part = dot_right(d_gate, w["gate"]) + dot_right(d_upper, w["upper"])
        saved.append(dict(d_feed=d_feed, d_gate=d_gate, d_upper=d_upper))
        if step == micro:
            feed_in = rows_of("feed_in")
            gate_total = core_sum(feed_in, rows_of("d_gate"))
            gate_total, feed_in, d_feed_rows = lax.optimization_barrier(
                (gate_total, feed_in, rows_of("d_feed"))
            )
            feed_totals = [
                gate_total,
                core_sum(feed_in, rows_of("d_upper")),
                core_sum(d_feed_rows, rows_of("hidden")),
            ]
            gate_sum = range_sum(feed_totals[0])
            feed_totals, gate_sum, part = lax.optimization_barrier((feed_totals, gate_sum, part))
        last = step == micro
        d_middle, feed_part, d_mixed, *away_0 = calls.backward_mid(
            part, gy, now["middle"], w["feed_gain"],
            **(dict(ident=16, extra=along_start(half, feed_totals[1], gate_sum)) if last else {}),
            **(dict(ident=18, extra=home_start(half, worked)) if step == 1 else {}),
        )
        if step == 1:
            outputs_in = jnp.where(lax.axis_index("section") == stage, worked, away_0[0])
        if last:
            upper_sum = with_away(feed_totals[1], away_0[0])
        d_gated = dot_plain(d_mixed, w["output"])
        d_cat, head_part, up_part, bias_part, *away_1 = mixer_backward(
            ranges, half, cuts, d_gated, now["inner"], now["cat"], w["up"], w["head_gain"],
            now["cumul"], now["logits"], now["states"],
            **(dict(ident=17, extra=along_start(half, feed_totals[2], upper_sum)) if last else {}),
        )
        part = dot_right(d_cat, w["cat"])
        saved[-1].update(d_mixed=d_mixed, d_cat=d_cat)
        if step < micro:
            later = micro - 2 - step
            own = own_cot[later] if later >= 0 else jnp.zeros_like(own_cot[0])
            grad, mixer_part, gy, d_feed = calls.backward_end(
                part, d_middle, now["h"], w["mixer_gain"], own,
            )
        else:
            lower_sum = with_away(feed_totals[2], away_1[0])
            output_total = core_sum(rows_of("d_mixed"), rows_of("gated"))
            grad, mixer_part, *away_2 = calls.backward_last(
                part, d_middle, now["h"], w["mixer_gain"],
                along_start(half, output_total, lower_sum),
            )
        grads.append(grad)
        saved[-1].update(
            head=head_part, mixer=mixer_part, feed=feed_part, up=up_part, bias=bias_part
        )

    def sum_of(name):
        return sum(item[name] for item in saved)

    totals = [
        core_sum(rows_of("normed"), rows_of("d_cat")),
        output_total,
    ]
    small_grads = [
        sum_of("up")[:rank].T,
        sum_of("bias"),
        sum_of("head"),
        sum_of("mixer"),
        sum_of("feed"),
    ]
    small_grads = tiles_of(
        jnp.concatenate([g.reshape(ranges, -1) for g in small_grads], axis=1), ranges, 8
    )
    section = lax.axis_index("section")
    theirs = exchanged(
        lax.dynamic_slice_in_dim(small_grads, (1 - section) * half, half, 0), "section"
    )
    small_grads = lax.dynamic_slice_in_dim(small_grads, section * half, half, 0) + theirs

    places = [outputs_in, picked(jnp.stack(grads[:0:-1]), jnp.stack(grads[micro - 1 :: -1]))]
    cat_grad, output_grad, outputs, input_grads, down, own, pooled = finish(
        half, peers, 13, totals, away_2[:1], places, small_grads, cuts.rank
    )
    stays = section == stage
    gate_grad = jnp.where(stays, gate_sum, away_0[1]).astype(f32)
    upper_grad = jnp.where(stays, upper_sum, away_1[1]).astype(f32)
    lower_grad = jnp.where(stays, lower_sum, away_2[1]).astype(f32)
    cat_grad, output_grad, input_grads = (
        g.astype(f32) for g in (cat_grad, output_grad, input_grads)
    )
    own, pooled = own.reshape(-1), pooled.reshape(-1)

    def piece(n, like):
        return (own if n < 2 else pooled)[ends[n] : ends[n + 1]].reshape(like.shape)

    return (
        outputs.reshape(1, micro, length, width),
        input_grads.reshape(1, micro, length, width),
        cat_grad[None, :, cuts.q],
        cat_grad[None, :, cuts.k],
        cat_grad[None, :, cuts.v],
        cat_grad[None, :, cuts.og],
        output_grad[None],
        down[None, :, :rank],
        piece(0, decay_up),
        piece(1, decay_bias),
        piece(2, head_gain),
        piece(3, mixer_gain),
        piece(4, feed_gain),
        gate_grad[None],
        upper_grad[None],
        lower_grad[None],
    )


def solution(mesh):
    sections, ranges, peers = (mesh.shape[a] for a in ("section", "seq", "tensor"))
    staged = Mesh(
        mesh.devices.reshape(sections, 2, ranges // 2, peers), ("section", "stage", "q", "tensor")
    )
    seq = ("stage", "q")
    whole = P("section", seq, "tensor")
    row = P("section", seq)
    rows = P("section", None, seq, None)
    tokens = P(None, seq, None)
    narrow = P("section", seq, None)
    return jax.shard_map(
        shards,
        mesh=staged,
        in_specs=(tokens, tokens)
        + (whole,) * 5
        + (narrow, whole, whole, row, row, row)
        + (whole,) * 3,
        out_specs=(rows, rows) + (whole,) * 5 + (narrow, whole, whole, row, row, row) + (whole,) * 3,
        check_vma=False,
    )
```
